32 devices in a mesh: dp: 8 (over z, y), ctx: 4 (over x, core).
Axes of the slice: x: 2, y: 2, z: 4, core: 2. Of those that a mesh axis runs over, the one named last changes fastest.
Arguments:
- tokens_in: bfloat16 [32, 1024, 768], P('dp', 'ctx'), may hold values from -6 to 6
- segments: int32 [32, 1024], P('dp', 'ctx'), may hold values from 0 to 3, as said below
- cotangent: bfloat16 [32, 1024, 768], P('dp', 'ctx'), may hold values from -6 to 6
- joint_weight: float32 [768, 2304], P(('dp', 'ctx')), may hold values from -0.21875 to 0.21875
- output_weight: float32 [768, 768], P(('dp', 'ctx')), may hold values from -1.75 to 1.75
- expand_weight: float32 [768, 3072], P(('dp', 'ctx')), may hold values from -0.21875 to 0.21875
- shrink_weight: float32 [3072, 768], P(('dp', 'ctx')), may hold values from -0.109375 to 0.109375
- momentum_joint: float32 [768, 2304], P(('dp', 'ctx')), may hold values from -97.75044 to 97.75044
- momentum_output: float32 [768, 768], P(('dp', 'ctx')), may hold values from -23.894552 to 23.894552
- momentum_expand: float32 [768, 3072], P(('dp', 'ctx')), may hold values from -30.41125 to 30.41125
- momentum_shrink: float32 [3072, 768], P(('dp', 'ctx')), may hold values from -72.40774 to 72.40774
- variance_joint: float32 [768, 2304], P(('dp', 'ctx')), may hold values from 19.6608 to 78.6432
- variance_output: float32 [768, 768], P(('dp', 'ctx')), may hold values from 1.31072 to 5.24288
- variance_expand: float32 [768, 3072], P(('dp', 'ctx')), may hold values from 1.96608 to 7.86432
- variance_shrink: float32 [3072, 768], P(('dp', 'ctx')), may hold values from 11.79648 to 47.18592
- small_params: float32 [12, 768], P(None, ('dp', 'ctx')), may hold values from -0.5 to 1.2, as said below
- momentum_small: float32 [12, 768], P(None, ('dp', 'ctx')), may hold values from -85.07909 to 85.07909
- variance_small: float32 [12, 768], P(None, ('dp', 'ctx')), may hold values from 16.384 to 65.536
Outputs:
- block_output: bfloat16 [32, 1024, 768], P('dp', 'ctx')
- input_grad: float32 [32, 1024, 768], P('dp', 'ctx')
- new_joint: float32 [768, 2304], P(('dp', 'ctx'))
- new_output: float32 [768, 768], P(('dp', 'ctx'))
- new_expand: float32 [768, 3072], P(('dp', 'ctx'))
- new_shrink: float32 [3072, 768], P(('dp', 'ctx'))
- first_joint: float32 [768, 2304], P(('dp', 'ctx'))
- first_output: float32 [768, 768], P(('dp', 'ctx'))
- first_expand: float32 [768, 3072], P(('dp', 'ctx'))
- first_shrink: float32 [3072, 768], P(('dp', 'ctx'))
- second_joint: float32 [768, 2304], P(('dp', 'ctx'))
- second_output: float32 [768, 768], P(('dp', 'ctx'))
- second_expand: float32 [768, 3072], P(('dp', 'ctx'))
- second_shrink: float32 [3072, 768], P(('dp', 'ctx'))
- new_small: float32 [12, 768], P(None, ('dp', 'ctx'))
- first_small: float32 [12, 768], P(None, ('dp', 'ctx'))
- second_small: float32 [12, 768], P(None, ('dp', 'ctx'))
The draws below stay inside these ranges and needn't reach their ends.
Inputs may be any that keep to these rules, and one draw needn't show every extreme that they name: `segments`: along each sequence the numbers start at 0, never fall, and step up by one at exactly 3 places, so each sequence holds 4 documents. `small_params`: rows 0 and 5 (the gains) lie in 0.8 to 1.2, the other rows in -0.5 to 0.5.
All inputs are finite; a program needn't handle non-finite values.
Results may differ from the reference program's by a relative error of at most 0.009.
The reference program's roundings to bfloat16 on the way count: a program that leaves them out, or rounds other values in their place, can miss the bound.
Values may be sent and summed in bfloat16 or wider, within the bound.
No kernel may reach another device: no remote copies, remote signals or barrier semaphores. Data moves between devices by JAX's collectives and lax.ppermute only.
A program may use at most 192 MiB of HBM per device.

```python
import math
import jax
import jax.numpy as jnp
from jax import lax

D = 768
HEADS = 12
HDIM = 64
FF = 3072
SEQ_GRP = 4
LEN = 1024
DOCS = 4
STEP = 10
SEQS = 32
STRETCH = 256
TOKENS = 32768
NVEC = 12
N_CTX = 4


def draw_segments(key, part):
    key = jax.random.fold_in(key, 7)
    pick_key, early_key, late_key = jax.random.split(key, 3)
    groups = SEQS // SEQ_GRP
    chosen = jax.random.randint(pick_key, (groups,), 0, SEQ_GRP)
    spanning = jnp.arange(SEQS) % SEQ_GRP == jnp.repeat(chosen, SEQ_GRP)

    def early_bounds(single_key):
        return jax.random.permutation(single_key, LEN - 1)[:DOCS - 1] + 1

    def late_bounds(single_key):
        return jax.random.permutation(single_key, STRETCH - 1)[:DOCS - 1] + (LEN - STRETCH + 1)
    early_sets = jax.vmap(early_bounds)(jax.random.split(early_key, SEQS))
    late_sets = jax.vmap(late_bounds)(jax.random.split(late_key, SEQS))
    bounds = jnp.where(spanning[:, None], late_sets, early_sets)
    places = jnp.arange(LEN)
    return jnp.sum((places[None, :, None] >= bounds[:, None, :]).astype(jnp.int32), axis=2)


def draw_small_params(key, part):
    key = jax.random.fold_in(key, 11)
    gain_key, bias_key = jax.random.split(key)
    spread = jax.random.uniform(gain_key, (NVEC, D), jnp.float32, -1.0, 1.0)
    offset = jax.random.uniform(bias_key, (NVEC, D), jnp.float32, -0.5, 0.5)
    row_ids = jnp.arange(NVEC)[:, None]
    is_gain = (row_ids == 0) | (row_ids == 5)
    return jnp.where(is_gain, 1.0 + 0.2 * spread, offset)


def strengthened(entries, key, source, target, parts, factor):
    owner, partner = [(jnp.arange(entries.shape[dim]) // (entries.shape[dim] // parts)).reshape([-1 if axis == dim else 1 for axis in range(entries.ndim)]) for dim in (source, target)]
    chosen = jax.random.permutation(key, parts)[partner]
    strong = (owner == chosen) | (owner == (partner + parts // 2) % parts)
    return jnp.where(strong, factor * entries, entries)


def block_scale(own_key, dims, cuts, least, top_value):
    loudness = 1.0
    for dim, blocks in cuts:
        heights = jax.random.uniform(jax.random.fold_in(jax.random.fold_in(own_key, 6), dim), (blocks,), jnp.float32, least / len(cuts), top_value / len(cuts))
        loudness = loudness * jnp.repeat(jnp.exp(heights), dims[dim] // blocks).reshape((-1,) + (1,) * (len(dims) - 1 - dim))
    return loudness


def gaussian(own_key, dims, scale, most, shards=(), dtype=jnp.bfloat16):
    factor_of = block_scale(own_key, dims, shards, -0.22, 0.18) if shards else 1.0
    entries = jax.random.normal(own_key, dims, jnp.float32) * scale * factor_of
    return jnp.minimum(jnp.maximum(entries, -most), most).astype(dtype)


def heavy_noise(key, extent, scale, most, shards, heavy, dtype=jnp.bfloat16):
    drawn = scale * jax.random.normal(key, extent, jnp.float32)
    if shards:
        drawn = drawn * block_scale(key, extent, shards, -0.22, 0.18)
    return jnp.clip(strengthened(drawn, jax.random.fold_in(key, 3), *heavy), -most, most).astype(dtype)


def setup_inputs(seed: int = 0) -> dict:
    key_list = jax.random.split(jax.random.key(seed), 19)
    return {
        "tokens_in": gaussian(key_list[0], (SEQS, LEN, D), 1.0, 6.0, ((0, 8), (1, 4))),
        "segments": draw_segments(jax.random.fold_in(key_list[18], 71), 0),
        "cotangent": heavy_noise(key_list[2], (SEQS, LEN, D), 1.0, 6.0, ((0, 8), (1, 4)), (0, 2, 8, 2.0)),
        "joint_weight": gaussian(key_list[3], (D, 3 * D), D ** -0.5, 0.21875, ((0, 32),), jnp.float32),
        "output_weight": gaussian(key_list[4], (D, D), (D // 64) ** -0.5, 1.75, ((0, 32),), jnp.float32),
        "expand_weight": gaussian(key_list[5], (D, FF), D ** -0.5, 0.21875, ((0, 32),), jnp.float32),
        "shrink_weight": gaussian(key_list[6], (FF, D), FF ** -0.5, 0.109375, ((0, 32),), jnp.float32),
        "momentum_joint": gaussian(key_list[7], (D, 3 * D), (0.09 * TOKENS ** 0.5), 97.75044, ((0, 32),), jnp.float32),
        "momentum_output": gaussian(key_list[8], (D, D), (0.022 * TOKENS ** 0.5), 23.894552, ((0, 32),), jnp.float32),
        "momentum_expand": gaussian(key_list[9], (D, FF), (0.028 * TOKENS ** 0.5), 30.41125, ((0, 32),), jnp.float32),
        "momentum_shrink": gaussian(key_list[10], (FF, D), (0.067 * TOKENS ** 0.5), 72.40774, ((0, 32),), jnp.float32),
        "variance_joint": jnp.clip(jnp.exp(math.log(78.6432) - 1.3862944 * jax.random.uniform(key_list[11], (D, 3 * D), jnp.float32) ** block_scale(key_list[11], (D, 3 * D), ((0, 32),), -0.2, 0.2)), 19.6608, 78.6432),
        "variance_output": jnp.clip(jnp.exp(math.log(5.24288) - 1.3862944 * jax.random.uniform(key_list[12], (D, D), jnp.float32) ** block_scale(key_list[12], (D, D), ((0, 32),), -0.2, 0.2)), 1.31072, 5.24288),
        "variance_expand": jnp.clip(jnp.exp(math.log(7.86432) - 1.3862944 * jax.random.uniform(key_list[13], (D, FF), jnp.float32) ** block_scale(key_list[13], (D, FF), ((0, 32),), -0.2, 0.2)), 1.96608, 7.86432),
        "variance_shrink": jnp.clip(jnp.exp(math.log(47.18592) - 1.3862944 * jax.random.uniform(key_list[14], (FF, D), jnp.float32) ** block_scale(key_list[14], (FF, D), ((0, 32),), -0.2, 0.2)), 11.79648, 47.18592),
        "small_params": draw_small_params(jax.random.fold_in(key_list[18], 71), 0),
        "momentum_small": gaussian(key_list[16], (NVEC, D), (0.078 * TOKENS ** 0.5), 85.07909, ((1, 32),), jnp.float32),
        "variance_small": jnp.clip(jnp.exp(math.log(65.536) - 1.3862944 * jax.random.uniform(key_list[17], (NVEC, D), jnp.float32) ** block_scale(key_list[17], (NVEC, D), ((1, 32),), -0.2, 0.2)), 16.384, 65.536),
    }


NORM_EPSILON = 1e-05
MASKED_SCORE = -1000000000.0
BETA_ONE = 0.9
BETA_TWO = 0.999
ADAM_EPSILON = 1e-08
RATE_MATRIX = 0.05
RATE_VECTOR = 0.3
WEIGHT_DECAY = 0.1
HIGHEST = lax.Precision.HIGHEST

@jax.custom_vjp
def low(v):
    return lax.optimization_barrier(v.astype(jnp.bfloat16)).astype(jnp.float32)

@jax.custom_vjp
def low_back(v):
    return v

def low_keep(v):
    return (low(v), None)

def low_pass(kept, grad):
    return (grad,)

def back_keep(v):
    return (v, None)

def back_low(kept, grad):
    return (low(grad),)
low.defvjp(low_keep, low_pass)
low_back.defvjp(back_keep, back_low)

def norm_rows(values, gain, shift):
    centre = values - lax.optimization_barrier(jnp.mean(values, axis=-1, keepdims=True))
    spread = lax.optimization_barrier(jnp.mean(centre * centre, axis=-1, keepdims=True))
    return centre * lax.rsqrt(spread + NORM_EPSILON) * gain + shift

def allowed_pairs(query_seg, key_seg, query_start):
    query_pos = query_start + jnp.arange(query_seg.shape[0])
    key_pos = jnp.arange(key_seg.shape[0])
    return (key_pos[None, :] <= query_pos[:, None]) & (key_seg[None, :] == query_seg[:, None])

def adam_step(weight, gradient, first, second, rate, decay):
    first_new = BETA_ONE * first + (1.0 - BETA_ONE) * gradient
    second_new = BETA_TWO * second + (1.0 - BETA_TWO) * gradient * gradient
    first_hat = first_new / (1.0 - BETA_ONE ** STEP)
    second_hat = second_new / (1.0 - BETA_TWO ** STEP)
    updated = weight - rate * (first_hat / (jnp.sqrt(second_hat) + ADAM_EPSILON) + decay * weight)
    return (updated, first_new, second_new)

def matmul(left, right):
    return jnp.dot(left, right, precision=HIGHEST)

def attend(item):
    queries, keys_set, values_set, seg_row = item
    scale = 1.0 / math.sqrt(HDIM)
    pieces = []
    for blk in range(N_CTX):
        lower = blk * STRETCH
        query_blk = queries[lower:lower + STRETCH]
        key_copy = low_back(keys_set)
        value_copy = low_back(values_set)
        allowed = allowed_pairs(seg_row[lower:lower + STRETCH], seg_row, lower)
        scores = low_back(jnp.einsum('qhd,khd->hqk', query_blk, key_copy, precision=HIGHEST) * scale)
        scores = jnp.where(allowed[None], scores, MASKED_SCORE)
        row_max = lax.optimization_barrier(jnp.max(scores, axis=-1, keepdims=True))
        exponent = jnp.exp(scores - row_max)
        row_sum = lax.optimization_barrier(jnp.sum(exponent, axis=-1, keepdims=True))
        weights = low(exponent / row_sum)
        pieces.append(jnp.einsum('hqk,khd->qhd', weights, value_copy, precision=HIGHEST))
    return jnp.concatenate(pieces, axis=0)

def block(inputs, seg_group, joint, output, expand, shrink, small):
    spans = FF // D
    count = inputs.shape[0]
    flat = inputs.reshape(-1, D)
    normed = low(norm_rows(flat, small[0], small[1]))
    joint_bias = jnp.concatenate([small[2], jnp.zeros((D,), jnp.float32), small[3]])
    joint_out = low(low_back(matmul(normed, joint) + joint_bias))
    queries = joint_out[:, :D].reshape(count, LEN, HEADS, HDIM)
    keys_set = joint_out[:, D:2 * D].reshape(count, LEN, HEADS, HDIM)
    values_set = joint_out[:, 2 * D:].reshape(count, LEN, HEADS, HDIM)
    mixed = lax.map(jax.checkpoint(attend), (queries, keys_set, values_set, seg_group)).reshape(-1, D)
    mixed = low(low_back(mixed))
    branch = low_back(matmul(mixed, output) + small[4])
    residual = flat + branch
    normed_two = low(norm_rows(residual, small[5], small[6]))
    expanded = low_back(matmul(normed_two, expand) + small[7:7 + spans].reshape(FF))
    activated = low(jax.nn.gelu(expanded))
    result = residual + matmul(activated, shrink) + small[7 + spans]
    return result.reshape(inputs.shape)

def reference(tokens_in, segments, cotangent, joint_weight, output_weight, expand_weight, shrink_weight, momentum_joint, momentum_output, momentum_expand, momentum_shrink, variance_joint, variance_output, variance_expand, variance_shrink, small_params, momentum_small, variance_small):
    masters = (joint_weight, output_weight, expand_weight, shrink_weight, small_params)
    rounded = tuple((low(item) for item in masters))
    flat_in = tokens_in.astype(jnp.float32)
    groups = SEQS // SEQ_GRP

    def forward(inputs, joint, output, expand, shrink, small):
        group_in = inputs.reshape(groups, SEQ_GRP, LEN, D)
        group_seg = segments.reshape(groups, SEQ_GRP, LEN)

        def group_step(pair):
            return block(pair[0], pair[1], joint, output, expand, shrink, small)
        return lax.map(jax.checkpoint(group_step), (group_in, group_seg)).reshape(SEQS, LEN, D)
    result, pullback = jax.vjp(forward, flat_in, *rounded)
    grads = pullback(cotangent.astype(jnp.float32))
    input_grad = grads[0]
    new_joint, first_joint, second_joint = adam_step(joint_weight, grads[1], momentum_joint, variance_joint, RATE_MATRIX, WEIGHT_DECAY)
    new_output, first_output, second_output = adam_step(output_weight, grads[2], momentum_output, variance_output, RATE_MATRIX, WEIGHT_DECAY)
    new_expand, first_expand, second_expand = adam_step(expand_weight, grads[3], momentum_expand, variance_expand, RATE_MATRIX, WEIGHT_DECAY)
    new_shrink, first_shrink, second_shrink = adam_step(shrink_weight, grads[4], momentum_shrink, variance_shrink, RATE_MATRIX, WEIGHT_DECAY)
    new_small, first_small, second_small = adam_step(small_params, grads[5], momentum_small, variance_small, RATE_VECTOR, 0.0)
    return (result.astype(jnp.bfloat16), input_grad, new_joint, new_output, new_expand, new_shrink, first_joint, first_output, first_expand, first_shrink, second_joint, second_output, second_expand, second_shrink, new_small, first_small, second_small)
```

```python
import functools

import jax
import jax.numpy as jnp
from jax import lax
from jax.experimental import pallas as pl
from jax.experimental.pallas import tpu as pltpu
from jax.sharding import PartitionSpec as P

HDIM = 64
STEP = 10

NORM_EPSILON = 1e-05
MASKED_SCORE = -1000000000.0
BETA_ONE = 0.9
BETA_TWO = 0.999
ADAM_EPSILON = 1e-08
RATE_MATRIX = 0.05
RATE_VECTOR = 0.3
WEIGHT_DECAY = 0.1

BF16 = jnp.bfloat16
F32 = jnp.float32


def norm_rows(values, gain, shift):
    centre = values - jnp.mean(values, axis=-1, keepdims=True)
    spread = jnp.mean(centre * centre, axis=-1, keepdims=True)
    return centre * lax.rsqrt(spread + NORM_EPSILON) * gain + shift


def norm_plain(values):
    centre = values - jnp.mean(values, axis=-1, keepdims=True)
    spread = jnp.mean(centre * centre, axis=-1, keepdims=True)
    return centre * lax.rsqrt(spread + NORM_EPSILON)


def adam_step(weight, gradient, first, second, rate, decay):
    first_new = BETA_ONE * first + (1.0 - BETA_ONE) * gradient
    second_new = BETA_TWO * second + (1.0 - BETA_TWO) * gradient * gradient
    first_hat = first_new / (1.0 - BETA_ONE**STEP)
    second_hat = second_new / (1.0 - BETA_TWO**STEP)
    updated = weight - rate * (first_hat / (jnp.sqrt(second_hat) + ADAM_EPSILON) + decay * weight)
    return (updated, first_new, second_new)


def dot(left, right, dims):
    return lax.dot_general(left, right, (dims, ((), ())), preferred_element_type=F32)


def fill_bias(bias, start_ref, n_blk, blk, block):
    keys = (block + 1) * blk
    key_pos = lax.broadcasted_iota(jnp.int32, (keys, blk), 0)
    query_pos = lax.broadcasted_iota(jnp.int32, (keys, blk), 1) + block * blk
    first = start_ref[0, :, block * blk : (block + 1) * blk]
    allowed = (key_pos >= first) & (key_pos <= query_pos)
    bias[:keys, :] = jnp.where(allowed, 0.0, MASKED_SCORE)


def forward_kernel(n_blk, blk, heads, me_ref, joint_ref, start_ref, out_ref, log_ref, joint, bias):
    me = me_ref[0]
    group = heads * HDIM
    for block in range(n_blk):
        joint[block * blk : (block + 1) * blk, :] = joint_ref[lax.bitwise_xor(me, block), 0]
    for block in range(n_blk):
        rows = slice(block * blk, (block + 1) * blk)
        keys = (block + 1) * blk
        fill_bias(bias, start_ref, n_blk, blk, block)
        for head in range(heads):
            low = head * HDIM
            query = joint[rows, low : low + HDIM] * 0.125
            key = joint[:keys, group + low : group + low + HDIM]
            value = joint[:keys, 2 * group + low : 2 * group + low + HDIM]
            scores = dot(key, query, ((1,), (1,))) + bias[:keys, :]
            top = jnp.max(scores, axis=0, keepdims=True)
            exponent = jnp.exp(scores - top)
            total = jnp.sum(exponent, axis=0, keepdims=True)
            weights = (exponent * (1.0 / total)).astype(BF16)
            mixed = dot(value, weights, ((0,), (0,)))
            out_ref[lax.bitwise_xor(me, block), 0, :, low : low + HDIM] = mixed.T.astype(BF16)
            log_ref[0, head : head + 1, rows] = top + jnp.log(total)


def backward_kernel(
    n_blk, blk, heads, me_ref, joint_ref, grad_ref, start_ref, log_ref, out_ref, joint, bias, grad_key, grad_value
):
    me = me_ref[0]
    group = heads * HDIM
    for block in range(n_blk):
        joint[block * blk : (block + 1) * blk, :] = joint_ref[lax.bitwise_xor(me, block), 0]
    for block in reversed(range(n_blk)):
        rows = slice(block * blk, (block + 1) * blk)
        keys = (block + 1) * blk
        fill_bias(bias, start_ref, n_blk, blk, block)
        place = lax.bitwise_xor(me, block)
        for head in range(heads):
            low = head * HDIM
            query = joint[rows, low : low + HDIM] * 0.125
            key = joint[:keys, group + low : group + low + HDIM]
            value = joint[:keys, 2 * group + low : 2 * group + low + HDIM]
            grad = grad_ref[place, 0, :, low : low + HDIM]
            scores = dot(key, query, ((1,), (1,))) + bias[:keys, :]
            probs = jnp.exp(scores - log_ref[0, head : head + 1, rows])
            grad_probs = dot(value, grad, ((1,), (1,)))
            inner = jnp.sum(probs * grad_probs, axis=0, keepdims=True)
            grad_scores = (probs * (grad_probs - inner)).astype(BF16)
            key_term = dot(grad_scores, query, ((1,), (0,)))
            value_term = dot(probs.astype(BF16), grad, ((1,), (0,)))
            if block == n_blk - 1:
                grad_key[head, :keys, :] = key_term
                grad_value[head, :keys, :] = value_term
            else:
                grad_key[head, :keys, :] += key_term
                grad_value[head, :keys, :] += value_term
            grad_query = dot(key, grad_scores, ((0,), (0,)))
            out_ref[place, 0, :, low : low + HDIM] = (grad_query.T * 0.125).astype(BF16)
    for block in range(n_blk):
        rows = slice(block * blk, (block + 1) * blk)
        place = lax.bitwise_xor(me, block)
        for head in range(heads):
            low = head * HDIM
            out_ref[place, 0, :, group + low : group + low + HDIM] = grad_key[head, rows, :].astype(BF16)
            out_ref[place, 0, :, 2 * group + low : 2 * group + low + HDIM] = grad_value[head, rows, :].astype(BF16)


def attend_forward(me, joint, start):
    n_blk, seqs, blk, cols = joint.shape
    group = cols // 3
    heads = group // HDIM
    length = n_blk * blk
    return pl.pallas_call(
        functools.partial(forward_kernel, n_blk, blk, heads),
        grid_spec=pltpu.PrefetchScalarGridSpec(
            num_scalar_prefetch=1,
            grid=(seqs,),
            in_specs=[
                pl.BlockSpec((n_blk, 1, blk, cols), lambda s, m: (0, s, 0, 0)),
                pl.BlockSpec((1, 1, length), lambda s, m: (s, 0, 0)),
            ],
            out_specs=[
                pl.BlockSpec((n_blk, 1, blk, group), lambda s, m: (0, s, 0, 0)),
                pl.BlockSpec((1, heads, length), lambda s, m: (s, 0, 0)),
            ],
            scratch_shapes=[pltpu.VMEM((length, cols), BF16), pltpu.VMEM((length, blk), F32)],
        ),
        out_shape=[
            jax.ShapeDtypeStruct((n_blk, seqs, blk, group), BF16),
            jax.ShapeDtypeStruct((seqs, heads, length), F32),
        ],
        compiler_params=pltpu.CompilerParams(vmem_limit_bytes=48 * 1024 * 1024),
        cost_estimate=pl.CostEstimate(
            flops=seqs * heads * length * length * HDIM * 3,
            bytes_accessed=seqs * length * cols * 3,
            transcendentals=seqs * heads * length * length,
        ),
        name="attend_forward",
    )(me, joint, start)


def attend_backward(me, joint, grad, start, logs):
    n_blk, seqs, blk, cols = joint.shape
    group = cols // 3
    heads = group // HDIM
    length = n_blk * blk
    return pl.pallas_call(
        functools.partial(backward_kernel, n_blk, blk, heads),
        grid_spec=pltpu.PrefetchScalarGridSpec(
            num_scalar_prefetch=1,
            grid=(seqs,),
            in_specs=[
                pl.BlockSpec((n_blk, 1, blk, cols), lambda s, m: (0, s, 0, 0)),
                pl.BlockSpec((n_blk, 1, blk, group), lambda s, m: (0, s, 0, 0)),
                pl.BlockSpec((1, 1, length), lambda s, m: (s, 0, 0)),
                pl.BlockSpec((1, heads, length), lambda s, m: (s, 0, 0)),
            ],
            out_specs=pl.BlockSpec((n_blk, 1, blk, cols), lambda s, m: (0, s, 0, 0)),
            scratch_shapes=[
                pltpu.VMEM((length, cols), BF16),
                pltpu.VMEM((length, blk), F32),
                pltpu.VMEM((heads, length, HDIM), F32),
                pltpu.VMEM((heads, length, HDIM), F32),
            ],
        ),
        out_shape=jax.ShapeDtypeStruct((n_blk, seqs, blk, cols), BF16),
        compiler_params=pltpu.CompilerParams(vmem_limit_bytes=48 * 1024 * 1024),
        cost_estimate=pl.CostEstimate(
            flops=seqs * heads * length * length * HDIM * 7,
            bytes_accessed=seqs * length * cols * 6,
            transcendentals=seqs * heads * length * length,
        ),
        name="attend_backward",
    )(me, joint, grad, start, logs)


def build(sizes):
    n_dp, n_ctx = sizes["dp"], sizes["ctx"]
    dp_bits = [bit for bit in range(16) if (1 << bit) < n_dp]
    ctx_bits = [bit for bit in range(16) if (1 << bit) < n_ctx]

    def swap(value, axis, mask):
        return lax.ppermute(value, axis, [(place, place ^ mask) for place in range(sizes[axis])])

    def reorder(items, me):
        stacked = jnp.stack(items)
        return [
            lax.dynamic_index_in_dim(stacked, lax.bitwise_xor(me, j), 0, keepdims=False) for j in range(len(items))
        ]

    def halve(value, labels, order, spots):
        labels = list(labels)
        for axis, bit in order:
            pos = labels.index((axis, bit))
            mine = (spots[axis] >> bit) & 1
            send = lax.dynamic_index_in_dim(value, 1 - mine, pos, keepdims=False).astype(BF16)
            keep = lax.dynamic_index_in_dim(value, mine, pos, keepdims=False)
            value = keep + swap(send, axis, 1 << bit).astype(F32)
            labels.pop(pos)
        return value

    def per_device(
        tokens_in,
        segments,
        cotangent,
        joint_weight,
        output_weight,
        expand_weight,
        shrink_weight,
        momentum_joint,
        momentum_output,
        momentum_expand,
        momentum_shrink,
        variance_joint,
        variance_output,
        variance_expand,
        variance_shrink,
        small_params,
        momentum_small,
        variance_small,
    ):
        seqs, stretch, width = tokens_in.shape
        hidden = expand_weight.shape[1]
        spans = hidden // width
        part = joint_weight.shape[0]
        group = width // n_ctx
        cols = 3 * group
        rows = seqs * stretch
        vectors = small_params.shape[0]
        me_dp, me = lax.axis_index("dp"), lax.axis_index("ctx")
        spots = {"dp": me_dp, "ctx": me}
        me_arr = me.astype(jnp.int32).reshape(1)

        joint_cast, small_cast, output_cast, expand_cast, shrink_cast = lax.optimization_barrier(
            (
                joint_weight.astype(BF16),
                small_params.astype(BF16),
                output_weight.astype(BF16),
                expand_weight.astype(BF16),
                shrink_weight.astype(BF16),
            )
        )
        shrink_wide = shrink_cast.reshape(spans, part, width).transpose(1, 0, 2).reshape(part, hidden)
        rest = lax.all_gather(
            jnp.concatenate([output_cast, expand_cast, shrink_wide], axis=1), ("dp", "ctx"), axis=0, tiled=True
        )

        extra = -(-vectors * part // cols)
        pad = extra * cols - vectors * part
        small_rows = jnp.pad(small_cast.reshape(-1), (0, pad)).reshape(extra, cols)
        joint_cols = joint_cast.reshape(part, 3, n_ctx, group)

        def columns_for(k):
            picked = lax.dynamic_index_in_dim(joint_cols, lax.bitwise_xor(me, k), 2, keepdims=False)
            return jnp.concatenate([picked.reshape(part, cols), small_rows], axis=0)

        pieces = [columns_for(0)] + [swap(columns_for(k), "ctx", k) for k in range(1, n_ctx)]
        gathered = jnp.stack(reorder(pieces, me))
        for bit in reversed(dp_bits):
            other = swap(gathered, "dp", 1 << bit)
            upper = ((me_dp >> bit) & 1) == 1
            gathered = jnp.where(upper, jnp.stack([other, gathered]), jnp.stack([gathered, other]))
        n_bits = len(dp_bits)
        gathered = gathered.transpose(tuple(reversed(range(n_bits))) + tuple(range(n_bits, n_bits + 3)))
        gathered = gathered.reshape(n_dp, n_ctx, part + extra, cols)
        joint_lo = gathered[:, :, :part].reshape(width, cols)
        small_lo = gathered[:, :, part:].reshape(n_dp, n_ctx, extra * cols)[:, :, : vectors * part]
        params = small_lo.reshape(n_dp, n_ctx, vectors, part).transpose(2, 0, 1, 3).reshape(vectors, width).astype(F32)

        blocks = {0: tokens_in}
        for bit in reversed(ctx_bits):
            blocks.update({k ^ (1 << bit): swap(value, "ctx", 1 << bit) for k, value in list(blocks.items())})
        tokens_all = jnp.stack([blocks[k] for k in range(n_ctx)]).reshape(n_ctx * rows, width)

        segs_all = lax.all_gather(segments.astype(BF16), "ctx", axis=1, tiled=True)
        start = jnp.sum(
            (segs_all[:, :, None] > segs_all[:, None, :]).astype(F32), axis=2
        ).astype(jnp.int32)[:, None, :]

        normed_lo = norm_rows(tokens_all.astype(F32), params[0], params[1]).astype(BF16)
        mine_bias = lax.dynamic_slice(params[2:4], (0, me * group), (2, group))
        joint_bias = jnp.concatenate([mine_bias[0], jnp.zeros((group,), F32), mine_bias[1]])
        joint_lo_out = (dot(normed_lo, joint_lo, ((1,), (0,))) + joint_bias).astype(BF16)
        joint_blocks = joint_lo_out.reshape(n_ctx, seqs, stretch, cols)
        attended, logs = attend_forward(me_arr, joint_blocks, start)
        mixed = jnp.concatenate(
            [attended[0]] + [swap(attended[k], "ctx", k) for k in range(1, n_ctx)], axis=-1
        ).reshape(rows, width)

        output_lo = rest[:, :width].reshape(n_ctx, group, width)
        output_lo = jnp.concatenate(reorder([output_lo[j] for j in range(n_ctx)], me), axis=0)
        expand_lo = rest[:, width : width + hidden]
        shrink_lo = (
            rest[:, width + hidden :].reshape(n_dp * n_ctx, part, spans, width).transpose(0, 2, 1, 3)
        ).reshape(hidden, width)

        flat_in = tokens_in.reshape(rows, width).astype(F32)
        residual = flat_in + (dot(mixed, output_lo, ((1,), (0,))) + params[4])
        normed_two, norm_two_back = jax.vjp(norm_rows, residual, params[5], params[6])
        normed_two_lo = normed_two.astype(BF16)
        expanded = dot(normed_two_lo, expand_lo, ((1,), (0,))) + params[7 : 7 + spans].reshape(hidden)
        activated, gelu_back = jax.vjp(jax.nn.gelu, expanded)
        activated_lo = activated.astype(BF16)
        result = residual + dot(activated_lo, shrink_lo, ((1,), (0,))) + params[7 + spans]
        block_output = result.reshape(tokens_in.shape).astype(BF16)

        labels = [("dp", bit) for bit in reversed(dp_bits)] + [("ctx", bit) for bit in reversed(ctx_bits)]
        bit_dims = (2,) * len(labels)
        near_first = [("ctx", bit) for bit in ctx_bits] + [("dp", bit) for bit in dp_bits]
        far_last = [("ctx", ctx_bits[0])] + [("dp", bit) for bit in dp_bits[1:]]
        far_last += [("dp", dp_bits[0])] + [("ctx", bit) for bit in ctx_bits[1:]]

        upstream = cotangent.reshape(rows, width)
        grad_shrink = dot(activated_lo, upstream, ((0,), (0,)))
        sum_shrink = halve(grad_shrink.reshape(bit_dims + (spans * part, width)), labels, near_first, spots)
        grad_bias_shrink = jnp.sum(upstream, axis=0, dtype=F32)
        grad_act = dot(upstream, shrink_lo, ((1,), (1,)))
        (grad_pre,) = gelu_back(grad_act)
        grad_pre_lo = grad_pre.astype(BF16)
        grad_expand = dot(normed_two_lo, grad_pre_lo, ((0,), (0,)))
        sum_expand = halve(grad_expand.reshape(bit_dims + (part, hidden)), labels, far_last, spots)
        grad_bias_expand = jnp.sum(grad_pre_lo, axis=0, dtype=F32)
        grad_normed_two = dot(grad_pre_lo, expand_lo, ((1,), (1,)))
        grad_resid_norm, grad_gain_two, grad_shift_two = norm_two_back(grad_normed_two)
        grad_resid = upstream.astype(F32) + grad_resid_norm
        grad_branch_lo = grad_resid.astype(BF16)
        grad_bias_out = jnp.sum(grad_branch_lo, axis=0, dtype=F32)
        grad_mixed = dot(grad_branch_lo, output_lo, ((1,), (1,))).astype(BF16).reshape(seqs, stretch, n_ctx, group)
        grad_pieces = jnp.stack(
            [grad_mixed[:, :, 0]] + [swap(grad_mixed[:, :, k], "ctx", k) for k in range(1, n_ctx)]
        )
        grad_output = dot(mixed, grad_branch_lo, ((0,), (0,))).reshape(n_ctx, group, width)
        grad_output = jnp.concatenate(reorder([grad_output[k] for k in range(n_ctx)], me), axis=0)
        sum_output = halve(grad_output.reshape(bit_dims + (part, width)), labels, near_first, spots)

        grad_joint_lo = attend_backward(me_arr, joint_blocks, grad_pieces, start, logs).reshape(n_ctx * rows, cols)

        grad_share = dot(grad_joint_lo, joint_lo, ((1,), (1,)))
        plain_all = norm_plain(tokens_all.astype(F32))
        grad_gain_one = jnp.sum(grad_share * plain_all, axis=0)
        grad_shift_one = jnp.sum(grad_share, axis=0)
        shares = {k: value for k, value in enumerate(grad_share.reshape(n_ctx, rows, width))}
        for bit in ctx_bits:
            mask = 1 << bit
            kept = {k: value for k, value in shares.items() if not k & mask}
            shares = {k: value + swap(shares[k | mask].astype(BF16), "ctx", mask).astype(F32) for k, value in kept.items()}
        _, norm_one_back = jax.vjp(norm_rows, flat_in, params[0], params[1])
        input_grad = (grad_resid + norm_one_back(shares[0])[0]).reshape(tokens_in.shape)

        grad_joint = dot(normed_lo, grad_joint_lo, ((0,), (0,)))
        grad_bias_joint = jnp.sum(grad_joint_lo, axis=0, dtype=F32)
        placed = lax.dynamic_update_slice(
            jnp.zeros((2, width), F32),
            jnp.stack([grad_bias_joint[:group], grad_bias_joint[2 * group :]]),
            (0, me * group),
        )
        grad_small = jnp.concatenate(
            [
                grad_gain_one[None],
                grad_shift_one[None],
                placed,
                grad_bias_out[None],
                grad_gain_two[None],
                grad_shift_two[None],
                grad_bias_expand.reshape(spans, width),
                grad_bias_shrink[None],
            ],
            axis=0,
        )
        small_terms = grad_small.reshape(vectors, n_dp, n_ctx, part).transpose(1, 2, 0, 3)
        small_terms = jnp.pad(small_terms.reshape(n_dp, n_ctx, vectors * part), ((0, 0), (0, 0), (0, pad)))
        terms = jnp.concatenate(
            [grad_joint.reshape(n_dp, n_ctx, part, cols), small_terms.reshape(n_dp, n_ctx, extra, cols)], axis=2
        ).reshape((2,) * n_bits + (n_ctx, part + extra, cols))
        dp_labels = [("dp", bit) for bit in reversed(dp_bits)]
        terms = halve(terms, dp_labels, [("dp", bit) for bit in dp_bits], spots)

        def terms_for(k):
            return lax.dynamic_index_in_dim(terms, lax.bitwise_xor(me, k), 0, keepdims=False)

        arrived = [terms_for(0)] + [
            swap(terms_for(k).astype(BF16), "ctx", k).astype(F32) for k in range(1, n_ctx)
        ]
        small_sum = sum(item[part:] for item in arrived).reshape(-1)[: vectors * part].reshape(vectors, part)
        sum_joint = jnp.stack([item[:part].reshape(part, 3, group) for item in reorder(arrived, me)], axis=2)
        sum_joint = sum_joint.reshape(part, 3 * width)

        new_joint, first_joint, second_joint = adam_step(
            joint_weight, sum_joint, momentum_joint, variance_joint, RATE_MATRIX, WEIGHT_DECAY
        )
        new_output, first_output, second_output = adam_step(
            output_weight, sum_output, momentum_output, variance_output, RATE_MATRIX, WEIGHT_DECAY
        )
        new_expand, first_expand, second_expand = adam_step(
            expand_weight, sum_expand, momentum_expand, variance_expand, RATE_MATRIX, WEIGHT_DECAY
        )
        new_shrink, first_shrink, second_shrink = adam_step(
            shrink_weight, sum_shrink, momentum_shrink, variance_shrink, RATE_MATRIX, WEIGHT_DECAY
        )
        new_small, first_small, second_small = adam_step(
            small_params, small_sum, momentum_small, variance_small, RATE_VECTOR, 0.0
        )
        return (
            block_output,
            input_grad,
            new_joint,
            new_output,
            new_expand,
            new_shrink,
            first_joint,
            first_output,
            first_expand,
            first_shrink,
            second_joint,
            second_output,
            second_expand,
            second_shrink,
            new_small,
            first_small,
            second_small,
        )

    return per_device


def solution(mesh):
    sizes = {axis: mesh.shape[axis] for axis in ("dp", "ctx")}
    tokens = P("dp", "ctx", None)
    matrix = P(("dp", "ctx"), None)
    table = P(None, ("dp", "ctx"))
    return jax.shard_map(
        build(sizes),
        mesh=mesh,
        in_specs=(tokens, P("dp", "ctx"), tokens) + (matrix,) * 12 + (table,) * 3,
        out_specs=(tokens, tokens) + (matrix,) * 12 + (table,) * 3,
        check_vma=False,
    )
```

```python
import functools

import jax
import jax.numpy as jnp
from jax import lax
from jax.experimental import pallas as pl
from jax.experimental.pallas import tpu as pltpu
from jax.sharding import PartitionSpec as P

HDIM = 64
STEP = 10

NORM_EPSILON = 1e-05
MASKED_SCORE = -1000000000.0
BETA_ONE = 0.9
BETA_TWO = 0.999
ADAM_EPSILON = 1e-08
RATE_MATRIX = 0.05
RATE_VECTOR = 0.3
WEIGHT_DECAY = 0.1
DOCS = 4
GELU_ROOT = 0.7978845608028654
GELU_CUBE = 0.044715
VMEM_BYTES = 56 * 1024 * 1024

BF16 = jnp.bfloat16
F32 = jnp.float32


def norm_parts(values):
    centre = values - jnp.mean(values, axis=-1, keepdims=True)
    scale = lax.rsqrt(jnp.mean(centre * centre, axis=-1, keepdims=True) + NORM_EPSILON)
    return centre * scale, scale


def norm_back(plain, scale, grad, gain):
    grad_plain = grad * gain
    along = jnp.mean(grad_plain * plain, axis=-1, keepdims=True)
    return (grad_plain - jnp.mean(grad_plain, axis=-1, keepdims=True) - plain * along) * scale


def column_sum(values):
    return jnp.sum(values, axis=0, keepdims=True)


def adam_step(weight, gradient, first, second, rate, decay):
    first_new = BETA_ONE * first + (1.0 - BETA_ONE) * gradient
    second_new = BETA_TWO * second + (1.0 - BETA_TWO) * gradient * gradient
    first_hat = first_new / (1.0 - BETA_ONE**STEP)
    second_hat = second_new / (1.0 - BETA_TWO**STEP)
    updated = weight - rate * (first_hat / (jnp.sqrt(second_hat) + ADAM_EPSILON) + decay * weight)
    return (updated, first_new, second_new)


def dot(left, right, dims):
    return lax.dot_general(left, right, (dims, ((), ())), preferred_element_type=F32)


def project_kernel(n_blk, *refs):
    tokens, (params_ref, weight_ref, bias_ref, joint_ref) = refs[:n_blk], refs[n_blk:]
    for place in range(n_blk):
        plain, _ = norm_parts(tokens[place][0].astype(F32))
        normed = (plain * params_ref[0:1, :] + params_ref[1:2, :]).astype(BF16)
        joint = dot(normed, weight_ref[...], ((1,), (0,))) + bias_ref[...]
        joint_ref[place, 0] = joint.astype(BF16)


def project(tokens, params, weight, bias):
    n_blk = len(tokens)
    seqs, blk, width = tokens[0].shape
    cols = weight.shape[1]
    return pl.pallas_call(
        functools.partial(project_kernel, n_blk),
        grid=(seqs,),
        in_specs=[pl.BlockSpec((1, blk, width), lambda s: (s, 0, 0))] * n_blk
        + [
            pl.BlockSpec(params.shape, lambda s: (0, 0)),
            pl.BlockSpec(weight.shape, lambda s: (0, 0)),
            pl.BlockSpec(bias.shape, lambda s: (0, 0)),
        ],
        out_specs=pl.BlockSpec((n_blk, 1, blk, cols), lambda s: (0, s, 0, 0)),
        out_shape=jax.ShapeDtypeStruct((n_blk, seqs, blk, cols), BF16),
        compiler_params=pltpu.CompilerParams(vmem_limit_bytes=VMEM_BYTES),
        cost_estimate=pl.CostEstimate(
            flops=2 * n_blk * seqs * blk * width * cols,
            bytes_accessed=2 * n_blk * seqs * blk * (width + cols),
            transcendentals=0,
        ),
        name="project",
    )(*tokens, params, weight, bias)


def fill_bias(bias, start_ref, n_blk, blk):
    offsets = []
    offset = 0
    for block in range(n_blk):
        keys = (block + 1) * blk
        key_pos = lax.broadcasted_iota(jnp.int32, (keys, blk), 0)
        query_pos = lax.broadcasted_iota(jnp.int32, (keys, blk), 1) + block * blk
        first = start_ref[0, :, block * blk : (block + 1) * blk]
        allowed = (key_pos >= first) & (key_pos <= query_pos)
        bias[offset : offset + keys, :] = jnp.where(allowed, 0.0, MASKED_SCORE)
        offsets.append(offset)
        offset += keys
    return offsets


def bias_rows(n_blk, blk):
    return n_blk * (n_blk + 1) // 2 * blk


def forward_kernel(n_blk, blk, heads, me_ref, joint_ref, start_ref, out_ref, log_ref, joint, bias):
    me = me_ref[0]
    group = heads * HDIM
    for block in range(n_blk):
        joint[block * blk : (block + 1) * blk, :] = joint_ref[lax.bitwise_xor(me, block), 0]
    offsets = fill_bias(bias, start_ref, n_blk, blk)
    tasks = [(block, head) for block in reversed(range(n_blk)) for head in range(heads)]

    def raw_scores(task):
        block, head = task
        low = head * HDIM
        query = joint[block * blk : (block + 1) * blk, low : low + HDIM] * 0.125
        return dot(joint[: (block + 1) * blk, group + low : group + low + HDIM], query, ((1,), (1,)))

    ahead = raw_scores(tasks[0])
    mixed = []
    for number, (block, head) in enumerate(tasks):
        scores = ahead
        if number + 1 < len(tasks):
            ahead = raw_scores(tasks[number + 1])
        keys = (block + 1) * blk
        low = head * HDIM
        scores = scores + bias[offsets[block] : offsets[block] + keys, :]
        top = jnp.max(scores, axis=0, keepdims=True)
        exponent = jnp.exp(scores - top)
        total = jnp.sum(exponent, axis=0, keepdims=True)
        value = joint[:keys, 2 * group + low : 2 * group + low + HDIM]
        mixed.append(dot(value, exponent.astype(BF16), ((0,), (0,))) * (1.0 / total))
        log_ref[0, head : head + 1, block * blk : (block + 1) * blk] = top + jnp.log(total)
        if head == heads - 1:
            out_ref[lax.bitwise_xor(me, block), 0] = jnp.concatenate(mixed, axis=0).T.astype(BF16)
            mixed = []


def attend_forward(me, joint, start):
    n_blk, seqs, blk, cols = joint.shape
    group = cols // 3
    heads = group // HDIM
    length = n_blk * blk
    return pl.pallas_call(
        functools.partial(forward_kernel, n_blk, blk, heads),
        grid_spec=pltpu.PrefetchScalarGridSpec(
            num_scalar_prefetch=1,
            grid=(seqs,),
            in_specs=[
                pl.BlockSpec((n_blk, 1, blk, cols), lambda s, m: (0, s, 0, 0)),
                pl.BlockSpec((1, 1, length), lambda s, m: (s, 0, 0)),
            ],
            out_specs=[
                pl.BlockSpec((n_blk, 1, blk, group), lambda s, m: (0, s, 0, 0)),
                pl.BlockSpec((1, heads, length), lambda s, m: (s, 0, 0)),
            ],
            scratch_shapes=[pltpu.VMEM((length, cols), BF16), pltpu.VMEM((bias_rows(n_blk, blk), blk), F32)],
        ),
        out_shape=[
            jax.ShapeDtypeStruct((n_blk, seqs, blk, group), BF16),
            jax.ShapeDtypeStruct((seqs, heads, length), F32),
        ],
        compiler_params=pltpu.CompilerParams(vmem_limit_bytes=VMEM_BYTES),
        cost_estimate=pl.CostEstimate(
            flops=seqs * heads * length * length * HDIM * 12,
            bytes_accessed=seqs * length * cols * 3,
            transcendentals=seqs * heads * length * length,
        ),
        name="attend_forward",
    )(me, joint, start)


def layer_kernel(
    n_ctx,
    spans,
    me_ref,
    x_ref,
    y_ref,
    *refs,
):
    mixed_refs = refs[:n_ctx]
    rest_ref, params_ref, result_ref, resid_ref, branch_ref, normed_ref, act_ref, pre_ref, mix_ref, sums_ref = refs[n_ctx:]
    me = me_ref[0]
    width = x_ref.shape[-1]
    group = width // n_ctx
    base = width * (1 + spans)

    def output_rows(place):
        first = pl.multiple_of(lax.bitwise_xor(me, place) * group, group)
        return rest_ref[pl.ds(first, group), 0:width]

    def param(row):
        return params_ref[row : row + 1, :]

    upstream = y_ref[0]
    residual = x_ref[0].astype(F32) + param(4)
    for place in range(n_ctx):
        residual = residual + dot(mixed_refs[place][0], output_rows(place), ((1,), (0,)))
    plain, scale = norm_parts(residual)
    normed = (plain * param(5) + param(6)).astype(BF16)
    normed_ref[0] = normed
    result = residual + param(7 + spans)
    grad_normed = jnp.zeros(residual.shape, F32)
    sums = []
    for span in range(spans):
        expand = rest_ref[:, width * (1 + span) : width * (2 + span)]
        shrink = rest_ref[:, base + width * span : base + width * (span + 1)]
        pre = dot(normed, expand, ((1,), (0,))) + param(7 + span)
        square = pre * pre
        bent = jnp.tanh(GELU_ROOT * (pre + GELU_CUBE * (square * pre)))
        half = 0.5 * (1.0 + bent)
        activated = (pre * half).astype(BF16)
        slope = half + (0.5 * pre) * (1.0 - bent * bent) * (GELU_ROOT + (3.0 * GELU_ROOT * GELU_CUBE) * square)
        act_ref[0, :, width * span : width * (span + 1)] = activated
        result = result + dot(activated, shrink, ((1,), (0,)))
        grad_pre = (dot(upstream, shrink, ((1,), (1,))) * slope).astype(BF16)
        pre_ref[0, :, width * span : width * (span + 1)] = grad_pre
        grad_normed = grad_normed + dot(grad_pre, expand, ((1,), (1,)))
        sums.append(column_sum(grad_pre.astype(F32)))
    result_ref[0] = result.astype(BF16)
    gain_sum = column_sum(grad_normed * plain)
    shift_sum = column_sum(grad_normed)
    upstream_wide = upstream.astype(F32)
    grad_resid = upstream_wide + norm_back(plain, scale, grad_normed, param(5))
    resid_ref[0] = grad_resid
    branch = grad_resid.astype(BF16)
    branch_ref[0] = branch
    for place in range(n_ctx):
        mix_ref[place, 0] = dot(branch, output_rows(place), ((1,), (1,))).astype(BF16)
    table = jnp.concatenate(
        [column_sum(branch.astype(F32)), gain_sum, shift_sum] + sums + [column_sum(upstream_wide)], axis=0
    )

    @pl.when(pl.program_id(0) == 0)
    def _():
        sums_ref[...] = table

    @pl.when(pl.program_id(0) > 0)
    def _():
        sums_ref[...] += table


def layer(me, tokens, cotangent, mixed, rest, params):
    n_ctx = len(mixed)
    seqs, blk, width = tokens.shape
    group = width // n_ctx
    spans = (rest.shape[1] // width - 1) // 2
    hidden = spans * width

    def by_seq(*shape):
        return pl.BlockSpec((1,) + shape, lambda s, m: (s,) + (0,) * len(shape))

    def whole(shape):
        return pl.BlockSpec(shape, lambda s, m: (0,) * len(shape), pipeline_mode=pl.Buffered(1))

    return pl.pallas_call(
        functools.partial(layer_kernel, n_ctx, spans),
        grid_spec=pltpu.PrefetchScalarGridSpec(
            num_scalar_prefetch=1,
            grid=(seqs,),
            in_specs=[by_seq(blk, width)] * 2
            + [by_seq(blk, group)] * n_ctx
            + [whole(rest.shape), whole(params.shape)],
            out_specs=[
                by_seq(blk, width),
                by_seq(blk, width),
                by_seq(blk, width),
                by_seq(blk, width),
                by_seq(blk, hidden),
                by_seq(blk, hidden),
                pl.BlockSpec((n_ctx, 1, blk, group), lambda s, m: (0, s, 0, 0)),
                pl.BlockSpec((4 + spans, width), lambda s, m: (0, 0)),
            ],
        ),
        out_shape=[
            jax.ShapeDtypeStruct((seqs, blk, width), BF16),
            jax.ShapeDtypeStruct((seqs, blk, width), F32),
            jax.ShapeDtypeStruct((seqs, blk, width), BF16),
            jax.ShapeDtypeStruct((seqs, blk, width), BF16),
            jax.ShapeDtypeStruct((seqs, blk, hidden), BF16),
            jax.ShapeDtypeStruct((seqs, blk, hidden), BF16),
            jax.ShapeDtypeStruct((n_ctx, seqs, blk, group), BF16),
            jax.ShapeDtypeStruct((4 + spans, width), F32),
        ],
        compiler_params=pltpu.CompilerParams(vmem_limit_bytes=VMEM_BYTES),
        cost_estimate=pl.CostEstimate(
            flops=2 * seqs * blk * width * (2 * width + 4 * hidden),
            bytes_accessed=rest.size * 2 + seqs * blk * (hidden * 4 + width * 14),
            transcendentals=seqs * blk * hidden,
        ),
        name="layer",
    )(me, tokens, cotangent, *mixed, rest, params)


def backward_kernel(
    n_blk, blk, heads, me_ref, joint_ref, *refs
):
    grad_refs = refs[:n_blk]
    start_ref, log_ref, out_ref, joint, grads, bias, totals = refs[n_blk:]
    me = me_ref[0]
    group = heads * HDIM
    for place in range(n_blk):
        rows = pl.ds(pl.multiple_of(lax.bitwise_xor(me, place) * blk, blk), blk)
        joint[rows, :] = joint_ref[place, 0]
        grads[rows, :] = grad_refs[place][0]
    offsets = fill_bias(bias, start_ref, n_blk, blk)
    tasks = [(block, head) for block in reversed(range(n_blk)) for head in range(heads)]

    def products(task):
        block, head = task
        low = head * HDIM
        keys = (block + 1) * blk
        rows = slice(block * blk, keys)
        query = joint[rows, low : low + HDIM] * 0.125
        grad = grads[rows, low : low + HDIM]
        scores = dot(joint[:keys, group + low : group + low + HDIM], query, ((1,), (1,)))
        grad_probs = dot(joint[:keys, 2 * group + low : 2 * group + low + HDIM], grad, ((1,), (1,)))
        zeros = jnp.zeros((blk, HDIM), BF16)
        pair = jnp.concatenate(
            [jnp.concatenate([query, zeros], axis=1), jnp.concatenate([zeros, grad], axis=1)], axis=0
        )
        return scores, grad_probs, pair

    ahead = products(tasks[0])
    grad_queries = []
    for number, (block, head) in enumerate(tasks):
        scores, grad_probs, pair = ahead
        if number + 1 < len(tasks):
            ahead = products(tasks[number + 1])
        keys = (block + 1) * blk
        low = head * HDIM
        scores = scores + bias[offsets[block] : offsets[block] + keys, :]
        probs = jnp.exp(scores - log_ref[0, head : head + 1, block * blk : keys])
        inner = jnp.sum(probs * grad_probs, axis=0, keepdims=True)
        grad_scores = (probs * (grad_probs - inner)).astype(BF16)
        terms = dot(jnp.concatenate([grad_scores, probs.astype(BF16)], axis=1), pair, ((1,), (0,)))
        if block == n_blk - 1:
            totals[head, :keys, :] = terms
        else:
            totals[head, :keys, :] += terms
        key = joint[:keys, group + low : group + low + HDIM]
        grad_queries.append(dot(key, grad_scores, ((0,), (0,))) * 0.125)
        if head == heads - 1:
            out_ref[lax.bitwise_xor(me, block), 0, :, :group] = jnp.concatenate(grad_queries, axis=0).T.astype(BF16)
            grad_queries = []
    for block in range(n_blk):
        rows = slice(block * blk, (block + 1) * blk)
        place = lax.bitwise_xor(me, block)
        sides = [totals[head, rows, :].astype(BF16) for head in range(heads)]
        out_ref[place, 0, :, group:] = jnp.concatenate(
            [side[:, :HDIM] for side in sides] + [side[:, HDIM:] for side in sides], axis=1
        )


def attend_backward(me, joint, grads, start, logs, first, count):
    n_blk, _, blk, cols = joint.shape
    group = cols // 3
    heads = group // HDIM
    length = n_blk * blk
    return pl.pallas_call(
        functools.partial(backward_kernel, n_blk, blk, heads),
        grid_spec=pltpu.PrefetchScalarGridSpec(
            num_scalar_prefetch=1,
            grid=(count,),
            in_specs=[pl.BlockSpec((n_blk, 1, blk, cols), lambda s, m: (0, s + first, 0, 0))]
            + [pl.BlockSpec((1, blk, group), lambda s, m: (s + first, 0, 0))] * n_blk
            + [
                pl.BlockSpec((1, 1, length), lambda s, m: (s + first, 0, 0)),
                pl.BlockSpec((1, heads, length), lambda s, m: (s + first, 0, 0)),
            ],
            out_specs=pl.BlockSpec((n_blk, 1, blk, cols), lambda s, m: (0, s, 0, 0)),
            scratch_shapes=[
                pltpu.VMEM((length, cols), BF16),
                pltpu.VMEM((length, group), BF16),
                pltpu.VMEM((bias_rows(n_blk, blk), blk), F32),
                pltpu.VMEM((heads, length, 2 * HDIM), F32),
            ],
        ),
        out_shape=jax.ShapeDtypeStruct((n_blk, count, blk, cols), BF16),
        compiler_params=pltpu.CompilerParams(vmem_limit_bytes=VMEM_BYTES),
        cost_estimate=pl.CostEstimate(
            flops=count * heads * length * length * HDIM * 30,
            bytes_accessed=count * length * cols * 6,
            transcendentals=count * heads * length * length,
        ),
        name="attend_backward",
    )(me, joint, *grads, start, logs)


def unproject_kernel(n_blk, *refs):
    grad_ref, tokens = refs[0], refs[1 : 1 + n_blk]
    params_ref, weight_ref, share_ref, weight_grad_ref, sums_ref, bias_ref = refs[1 + n_blk :]
    weight_grad = bias_grad = gain_sum = shift_sum = 0.0
    for place in range(n_blk):
        grad = grad_ref[place, 0]
        plain, _ = norm_parts(tokens[place][0].astype(F32))
        normed = (plain * params_ref[0:1, :] + params_ref[1:2, :]).astype(BF16)
        share = dot(grad, weight_ref[...], ((1,), (1,)))
        share_ref[place, 0] = share.astype(BF16)
        gain_sum += column_sum(share * plain)
        shift_sum += column_sum(share)
        bias_grad += column_sum(grad.astype(F32))
        weight_grad += dot(normed, grad, ((0,), (0,)))
    sums = jnp.concatenate([gain_sum, shift_sum], axis=0)

    @pl.when(pl.program_id(0) == 0)
    def _():
        weight_grad_ref[...] = weight_grad
        sums_ref[...] = sums
        bias_ref[...] = bias_grad

    @pl.when(pl.program_id(0) > 0)
    def _():
        weight_grad_ref[...] += weight_grad
        sums_ref[...] += sums
        bias_ref[...] += bias_grad


def unproject(grad, tokens, params, weight, first):
    n_blk, count, blk, cols = grad.shape
    width = tokens[0].shape[-1]
    return pl.pallas_call(
        functools.partial(unproject_kernel, n_blk),
        grid=(count,),
        in_specs=[pl.BlockSpec((n_blk, 1, blk, cols), lambda s: (0, s, 0, 0))]
        + [pl.BlockSpec((1, blk, width), lambda s: (s + first, 0, 0))] * n_blk
        + [pl.BlockSpec(params.shape, lambda s: (0, 0)), pl.BlockSpec(weight.shape, lambda s: (0, 0))],
        out_specs=[
            pl.BlockSpec((n_blk, 1, blk, width), lambda s: (0, s, 0, 0)),
            pl.BlockSpec((width, cols), lambda s: (0, 0)),
            pl.BlockSpec((2, width), lambda s: (0, 0)),
            pl.BlockSpec((1, cols), lambda s: (0, 0)),
        ],
        out_shape=[
            jax.ShapeDtypeStruct((n_blk, count, blk, width), BF16),
            jax.ShapeDtypeStruct((width, cols), F32),
            jax.ShapeDtypeStruct((2, width), F32),
            jax.ShapeDtypeStruct((1, cols), F32),
        ],
        compiler_params=pltpu.CompilerParams(vmem_limit_bytes=VMEM_BYTES),
        cost_estimate=pl.CostEstimate(
            flops=4 * n_blk * count * blk * width * cols,
            bytes_accessed=2 * n_blk * count * blk * (2 * width + cols),
            transcendentals=0,
        ),
        name="unproject",
    )(grad, *tokens, params, weight)


def build(sizes):
    n_dp, n_ctx = sizes["dp"], sizes["ctx"]
    dp_bits = [bit for bit in range(16) if (1 << bit) < n_dp]
    ctx_bits = [bit for bit in range(16) if (1 << bit) < n_ctx]

    def swap(value, axis, mask):
        return lax.ppermute(value, axis, [(place, place ^ mask) for place in range(sizes[axis])])

    def reorder(items, me):
        stacked = jnp.stack(items)
        return [
            lax.dynamic_index_in_dim(stacked, lax.bitwise_xor(me, j), 0, keepdims=False) for j in range(len(items))
        ]

    def halve(value, labels, order, spots):
        labels = list(labels)
        for axis, bit in order:
            pos = labels.index((axis, bit))
            mine = (spots[axis] >> bit) & 1
            send = lax.dynamic_index_in_dim(value, 1 - mine, pos, keepdims=False).astype(BF16)
            keep = lax.dynamic_index_in_dim(value, mine, pos, keepdims=False)
            value = keep + swap(send, axis, 1 << bit).astype(F32)
            labels.pop(pos)
        return value

    def per_device(
        tokens_in,
        segments,
        cotangent,
        joint_weight,
        output_weight,
        expand_weight,
        shrink_weight,
        momentum_joint,
        momentum_output,
        momentum_expand,
        momentum_shrink,
        variance_joint,
        variance_output,
        variance_expand,
        variance_shrink,
        small_params,
        momentum_small,
        variance_small,
    ):
        seqs, stretch, width = tokens_in.shape
        hidden = expand_weight.shape[1]
        spans = hidden // width
        part = joint_weight.shape[0]
        group = width // n_ctx
        cols = 3 * group
        rows = seqs * stretch
        n_dev = n_dp * n_ctx
        vectors = small_params.shape[0]
        me_dp, me = lax.axis_index("dp"), lax.axis_index("ctx")
        spots = {"dp": me_dp, "ctx": me}
        me_arr = me.astype(jnp.int32).reshape(1)

        joint_cast, small_cast, output_cast, expand_cast, shrink_cast = lax.optimization_barrier(
            (
                joint_weight.astype(BF16),
                small_params.astype(BF16),
                output_weight.astype(BF16),
                expand_weight.astype(BF16),
                shrink_weight.astype(BF16),
            )
        )

        blocks, seg_blocks = {0: tokens_in}, {0: segments}
        for bit in reversed(ctx_bits):
            for known in (seg_blocks, blocks):
                known.update({k ^ (1 << bit): swap(value, "ctx", 1 << bit) for k, value in list(known.items())})
        tokens = [blocks[k] for k in range(n_ctx)]
        segs = jnp.concatenate(reorder([seg_blocks[k] for k in range(n_ctx)], me), axis=1)
        start = jnp.zeros_like(segs)
        for number in range(1, DOCS):
            bound = jnp.sum((segs < number).astype(jnp.int32), axis=1, keepdims=True)
            start = jnp.where(segs >= number, bound, start)
        start = start[:, None, :]

        extra = -(-vectors * part // cols)
        pad = extra * cols - vectors * part
        small_rows = jnp.pad(small_cast.reshape(-1), (0, pad)).reshape(extra, cols)
        joint_cols = joint_cast.reshape(part, 3, n_ctx, group)

        def columns_for(k):
            picked = lax.dynamic_index_in_dim(joint_cols, lax.bitwise_xor(me, k), 2, keepdims=False)
            return jnp.concatenate([picked.reshape(part, cols), small_rows], axis=0)

        pieces = [columns_for(0)] + [swap(columns_for(k), "ctx", k) for k in range(1, n_ctx)]
        gathered = jnp.stack(reorder(pieces, me))
        for bit in reversed(dp_bits):
            other = swap(gathered, "dp", 1 << bit)
            upper = ((me_dp >> bit) & 1) == 1
            gathered = jnp.where(upper, jnp.stack([other, gathered]), jnp.stack([gathered, other]))
        n_bits = len(dp_bits)

        expand_wide = expand_cast.reshape(part, n_dev, spans, part).transpose(0, 2, 1, 3).reshape(part, hidden)
        shrink_wide = shrink_cast.reshape(spans, part, width).transpose(1, 0, 2).reshape(part, hidden)
        rest = jnp.concatenate([output_cast, expand_wide, shrink_wide], axis=1)
        rest, gathered = lax.optimization_barrier((rest, gathered))
        rest = lax.all_gather(rest, ("dp", "ctx"), axis=0, tiled=True)

        gathered = gathered.transpose(tuple(reversed(range(n_bits))) + tuple(range(n_bits, n_bits + 3)))
        gathered = gathered.reshape(n_dp, n_ctx, part + extra, cols)
        joint_lo = gathered[:, :, :part].reshape(width, cols)
        small_lo = gathered[:, :, part:].reshape(n_dp, n_ctx, extra * cols)[:, :, : vectors * part]
        params = small_lo.reshape(n_dp, n_ctx, vectors, part).transpose(2, 0, 1, 3).reshape(vectors, width).astype(F32)
        mine_bias = lax.dynamic_slice(params[2:4], (0, me * group), (2, group))
        joint_bias = jnp.concatenate([mine_bias[:1], jnp.zeros((1, group), F32), mine_bias[1:]], axis=1)
        bias_hidden = params[7 : 7 + spans].reshape(n_dev, spans, part).transpose(1, 0, 2).reshape(spans, width)
        params = jnp.concatenate([params[:7], bias_hidden, params[7 + spans :]], axis=0)

        joint = project(tokens, params, joint_lo, joint_bias)
        attended, logs = attend_forward(me_arr, joint, start)
        mixed = [attended[0]] + [swap(attended[k], "ctx", k) for k in range(1, n_ctx)]
        block_output, grad_resid, branch, normed_two, activated, grad_pre, grad_mixed, sums = layer(
            me_arr, tokens_in, cotangent, mixed, rest, params
        )
        grads = [grad_mixed[0]] + [swap(grad_mixed[k], "ctx", k) for k in range(1, n_ctx)]

        upstream = cotangent.reshape(rows, width)
        grad_shrink = dot(activated.reshape(rows, hidden), upstream, ((0,), (0,)))
        grad_expand = dot(normed_two.reshape(rows, width), grad_pre.reshape(rows, hidden), ((0,), (0,)))
        branch = branch.reshape(rows, width)
        grad_output = [dot(item.reshape(rows, group), branch, ((0,), (0,))) for item in mixed]
        grad_output = jnp.concatenate(reorder(grad_output, me), axis=0)

        labels = [("dp", bit) for bit in reversed(dp_bits)] + [("ctx", bit) for bit in reversed(ctx_bits)]
        bit_dims = (2,) * len(labels)
        y_first = [("ctx", ctx_bits[0])] + [("dp", bit) for bit in dp_bits] + [("ctx", bit) for bit in ctx_bits[1:]]
        z_first = [("ctx", ctx_bits[0])] + [("dp", bit) for bit in dp_bits[1:]]
        z_first += [("dp", dp_bits[0])] + [("ctx", bit) for bit in ctx_bits[1:]]
        chains = [
            [grad_shrink.reshape((spans,) + bit_dims + (part, width)), ["span"] + labels, y_first],
            [grad_expand.reshape(bit_dims + (part, hidden)), labels, z_first],
            [grad_output.reshape(bit_dims + (part, width)), labels, y_first],
        ]

        def stage():
            sent = []
            for chain in chains:
                value, names, order = chain
                axis, bit = order[0]
                pos = names.index((axis, bit))
                mine = (spots[axis] >> bit) & 1
                send = lax.dynamic_index_in_dim(value, 1 - mine, pos, keepdims=False).astype(BF16)
                keep = lax.dynamic_index_in_dim(value, mine, pos, keepdims=False)
                sent.append((keep, swap(send, axis, 1 << bit)))
                chain[1] = names[:pos] + names[pos + 1 :]
                chain[2] = order[1:]
            return sent

        def settle(sent, pinned):
            for chain, (keep, got) in zip(chains, sent):
                chain[0] = keep + got.astype(F32)
            out = lax.optimization_barrier((pinned,) + tuple(chain[0] for chain in chains))
            for chain, value in zip(chains, out[1:]):
                chain[0] = value
            return out[0]

        half = max(seqs // 2, 1)
        halves = [(first, half) for first in range(0, seqs, half)]
        sent = stage()
        shares, weight_grads = [], []
        for number, (first, count) in enumerate(halves):
            source = joint
            if number:
                source = settle(sent, joint)
                sent = stage()
            grad_joint = attend_backward(me_arr, source, grads, start, logs, first, count)
            if number == 0:
                grad_joint = settle(sent, grad_joint)
                sent = stage()
            share, weight_grad, norm_sums, bias_sums = unproject(grad_joint, tokens, params, joint_lo, first)
            weight_grads.append((weight_grad, norm_sums, bias_sums))
            known = {k: share[k] for k in range(n_ctx)}
            for bit in ctx_bits:
                mask = 1 << bit
                known = {
                    k: value.astype(F32) + swap(known[k | mask].astype(BF16), "ctx", mask).astype(F32)
                    for k, value in known.items()
                    if not k & mask
                }
            shares.append(known[0])
        weight_grad, norm_sums, bias_sums = [sum(items) for items in zip(*weight_grads)]

        plain, scale = norm_parts(tokens_in.astype(F32))
        input_grad = grad_resid + norm_back(plain, scale, jnp.concatenate(shares, axis=0), params[0])

        placed = lax.dynamic_update_slice(
            jnp.zeros((2, width), F32),
            jnp.concatenate([bias_sums[:, :group], bias_sums[:, 2 * group :]], axis=0),
            (0, me * group),
        )
        sums_hidden = sums[3 : 3 + spans].reshape(spans, n_dev, part).transpose(1, 0, 2).reshape(spans, width)
        grad_small = jnp.concatenate([norm_sums, placed, sums[:3], sums_hidden, sums[3 + spans :]], axis=0)
        small_terms = grad_small.reshape(vectors, n_dp, n_ctx, part).transpose(1, 2, 0, 3)
        small_terms = jnp.pad(small_terms.reshape(n_dp, n_ctx, vectors * part), ((0, 0), (0, 0), (0, pad)))
        terms = jnp.concatenate(
            [weight_grad.reshape(n_dp, n_ctx, part, cols), small_terms.reshape(n_dp, n_ctx, extra, cols)], axis=2
        ).reshape((2,) * n_bits + (n_ctx, part + extra, cols))
        dp_labels = [("dp", bit) for bit in reversed(dp_bits)]
        terms = halve(terms, dp_labels, [("dp", bit) for bit in dp_bits], spots)

        def terms_for(k):
            return lax.dynamic_index_in_dim(terms, lax.bitwise_xor(me, k), 0, keepdims=False)

        arrived = [terms_for(0)] + [
            swap(terms_for(k).astype(BF16), "ctx", k).astype(F32) for k in range(1, n_ctx)
        ]
        small_sum = sum(item[part:] for item in arrived).reshape(-1)[: vectors * part].reshape(vectors, part)
        sum_joint = jnp.stack([item[:part].reshape(part, 3, group) for item in reorder(arrived, me)], axis=2)
        sum_joint = sum_joint.reshape(part, 3 * width)

        for chain, (keep, got) in zip(chains, sent):
            chain[0] = keep + got.astype(F32)
        sum_shrink, sum_expand, sum_output = [halve(value, names, order, spots) for value, names, order in chains]
        sum_shrink = sum_shrink.reshape(spans * part, width)
        sum_expand = sum_expand.reshape(part, spans, n_dev, part).transpose(0, 2, 1, 3).reshape(part, hidden)

        new_joint, first_joint, second_joint = adam_step(
            joint_weight, sum_joint, momentum_joint, variance_joint, RATE_MATRIX, WEIGHT_DECAY
        )
        new_output, first_output, second_output = adam_step(
            output_weight, sum_output, momentum_output, variance_output, RATE_MATRIX, WEIGHT_DECAY
        )
        new_expand, first_expand, second_expand = adam_step(
            expand_weight, sum_expand, momentum_expand, variance_expand, RATE_MATRIX, WEIGHT_DECAY
        )
        new_shrink, first_shrink, second_shrink = adam_step(
            shrink_weight, sum_shrink, momentum_shrink, variance_shrink, RATE_MATRIX, WEIGHT_DECAY
        )
        new_small, first_small, second_small = adam_step(
            small_params, small_sum, momentum_small, variance_small, RATE_VECTOR, 0.0
        )
        return (
            block_output,
            input_grad,
            new_joint,
            new_output,
            new_expand,
            new_shrink,
            first_joint,
            first_output,
            first_expand,
            first_shrink,
            second_joint,
            second_output,
            second_expand,
            second_shrink,
            new_small,
            first_small,
            second_small,
        )

    return per_device


def solution(mesh):
    sizes = {axis: mesh.shape[axis] for axis in ("dp", "ctx")}
    tokens = P("dp", "ctx", None)
    matrix = P(("dp", "ctx"), None)
    table = P(None, ("dp", "ctx"))
    return jax.shard_map(
        build(sizes),
        mesh=mesh,
        in_specs=(tokens, P("dp", "ctx"), tokens) + (matrix,) * 12 + (table,) * 3,
        out_specs=(tokens, tokens) + (matrix,) * 12 + (table,) * 3,
        check_vma=False,
    )
```

```python
import functools

import jax
import jax.numpy as jnp
from jax import lax
from jax.experimental import pallas as pl
from jax.experimental.pallas import tpu as pltpu
from jax.sharding import PartitionSpec as P

HDIM = 64
STEP = 10

NORM_EPSILON = 1e-05
MASKED_SCORE = -1000000000.0
BETA_ONE = 0.9
BETA_TWO = 0.999
ADAM_EPSILON = 1e-08
RATE_MATRIX = 0.05
RATE_VECTOR = 0.3
WEIGHT_DECAY = 0.1
DOCS = 4
GELU_ROOT = 0.7978845608028654
GELU_CUBE = 0.044715
VMEM_BYTES = 56 * 1024 * 1024

BF16 = jnp.bfloat16
F32 = jnp.float32


def norm_parts(values):
    centre = values - jnp.mean(values, axis=-1, keepdims=True)
    scale = lax.rsqrt(jnp.mean(centre * centre, axis=-1, keepdims=True) + NORM_EPSILON)
    return centre * scale, scale


def norm_back(plain, scale, grad, gain):
    grad_plain = grad * gain
    along = jnp.mean(grad_plain * plain, axis=-1, keepdims=True)
    return (grad_plain - jnp.mean(grad_plain, axis=-1, keepdims=True) - plain * along) * scale


def column_sum(values):
    return jnp.sum(values, axis=0, keepdims=True)


def adam_step(weight, gradient, first, second, rate, decay):
    first_new = BETA_ONE * first + (1.0 - BETA_ONE) * gradient
    second_new = BETA_TWO * second + (1.0 - BETA_TWO) * gradient * gradient
    first_hat = first_new / (1.0 - BETA_ONE**STEP)
    second_hat = second_new / (1.0 - BETA_TWO**STEP)
    updated = weight - rate * (first_hat / (jnp.sqrt(second_hat) + ADAM_EPSILON) + decay * weight)
    return (updated, first_new, second_new)


def dot(left, right, dims):
    return lax.dot_general(left, right, (dims, ((), ())), preferred_element_type=F32)


def project_kernel(n_blk, *refs):
    tokens, (params_ref, weight_ref, bias_ref, joint_ref) = refs[:n_blk], refs[n_blk:]
    for place in range(n_blk):
        plain, _ = norm_parts(tokens[place][0].astype(F32))
        normed = (plain * params_ref[0:1, :] + params_ref[1:2, :]).astype(BF16)
        joint = dot(normed, weight_ref[...], ((1,), (0,))) + bias_ref[...]
        joint_ref[place, 0] = joint.astype(BF16)


def project(tokens, params, weight, bias):
    n_blk = len(tokens)
    seqs, blk, width = tokens[0].shape
    cols = weight.shape[1]
    return pl.pallas_call(
        functools.partial(project_kernel, n_blk),
        grid=(seqs,),
        in_specs=[pl.BlockSpec((1, blk, width), lambda s: (s, 0, 0))] * n_blk
        + [
            pl.BlockSpec(params.shape, lambda s: (0, 0)),
            pl.BlockSpec(weight.shape, lambda s: (0, 0)),
            pl.BlockSpec(bias.shape, lambda s: (0, 0)),
        ],
        out_specs=pl.BlockSpec((n_blk, 1, blk, cols), lambda s: (0, s, 0, 0)),
        out_shape=jax.ShapeDtypeStruct((n_blk, seqs, blk, cols), BF16),
        compiler_params=pltpu.CompilerParams(vmem_limit_bytes=VMEM_BYTES),
        cost_estimate=pl.CostEstimate(
            flops=2 * n_blk * seqs * blk * width * cols,
            bytes_accessed=2 * n_blk * seqs * blk * (width + cols),
            transcendentals=0,
        ),
        name="project",
    )(*tokens, params, weight, bias)


def fill_bias(bias, start_ref, n_blk, blk):
    offsets = []
    offset = 0
    for block in range(n_blk):
        keys = (block + 1) * blk
        key_pos = lax.broadcasted_iota(jnp.int32, (keys, blk), 0)
        query_pos = lax.broadcasted_iota(jnp.int32, (keys, blk), 1) + block * blk
        first = start_ref[0, :, block * blk : (block + 1) * blk]
        allowed = (key_pos >= first) & (key_pos <= query_pos)
        bias[offset : offset + keys, :] = jnp.where(allowed, 0.0, MASKED_SCORE)
        offsets.append(offset)
        offset += keys
    return offsets


def bias_rows(n_blk, blk):
    return n_blk * (n_blk + 1) // 2 * blk


def forward_kernel(n_blk, blk, heads, me_ref, joint_ref, start_ref, out_ref, log_ref, joint, bias):
    me = me_ref[0]
    group = heads * HDIM
    for block in range(n_blk):
        joint[block * blk : (block + 1) * blk, :] = joint_ref[lax.bitwise_xor(me, block), 0]
    offsets = fill_bias(bias, start_ref, n_blk, blk)
    tasks = [(block, head) for block in reversed(range(n_blk)) for head in range(heads)]

    def raw_scores(task):
        block, head = task
        low = head * HDIM
        query = joint[block * blk : (block + 1) * blk, low : low + HDIM] * 0.125
        return dot(joint[: (block + 1) * blk, group + low : group + low + HDIM], query, ((1,), (1,)))

    ahead = raw_scores(tasks[0])
    mixed = []
    for number, (block, head) in enumerate(tasks):
        scores = ahead
        if number + 1 < len(tasks):
            ahead = raw_scores(tasks[number + 1])
        keys = (block + 1) * blk
        low = head * HDIM
        scores = scores + bias[offsets[block] : offsets[block] + keys, :]
        top = jnp.max(scores, axis=0, keepdims=True)
        exponent = jnp.exp(scores - top)
        total = jnp.sum(exponent, axis=0, keepdims=True)
        value = joint[:keys, 2 * group + low : 2 * group + low + HDIM]
        mixed.append(dot(value, exponent.astype(BF16), ((0,), (0,))) * (1.0 / total))
        log_ref[0, head : head + 1, block * blk : (block + 1) * blk] = top + jnp.log(total)
        if head == heads - 1:
            out_ref[lax.bitwise_xor(me, block), 0] = jnp.concatenate(mixed, axis=0).T.astype(BF16)
            mixed = []


def attend_forward(me, joint, start):
    n_blk, seqs, blk, cols = joint.shape
    group = cols // 3
    heads = group // HDIM
    length = n_blk * blk
    return pl.pallas_call(
        functools.partial(forward_kernel, n_blk, blk, heads),
        grid_spec=pltpu.PrefetchScalarGridSpec(
            num_scalar_prefetch=1,
            grid=(seqs,),
            in_specs=[
                pl.BlockSpec((n_blk, 1, blk, cols), lambda s, m: (0, s, 0, 0)),
                pl.BlockSpec((1, 1, length), lambda s, m: (s, 0, 0)),
            ],
            out_specs=[
                pl.BlockSpec((n_blk, 1, blk, group), lambda s, m: (0, s, 0, 0)),
                pl.BlockSpec((1, heads, length), lambda s, m: (s, 0, 0)),
            ],
            scratch_shapes=[pltpu.VMEM((length, cols), BF16), pltpu.VMEM((bias_rows(n_blk, blk), blk), F32)],
        ),
        out_shape=[
            jax.ShapeDtypeStruct((n_blk, seqs, blk, group), BF16),
            jax.ShapeDtypeStruct((seqs, heads, length), F32),
        ],
        compiler_params=pltpu.CompilerParams(vmem_limit_bytes=VMEM_BYTES),
        cost_estimate=pl.CostEstimate(
            flops=seqs * heads * length * length * HDIM * 12,
            bytes_accessed=seqs * length * cols * 3,
            transcendentals=seqs * heads * length * length,
        ),
        name="attend_forward",
    )(me, joint, start)


def layer_kernel(
    n_ctx,
    spans,
    me_ref,
    x_ref,
    y_ref,
    *refs,
):
    mixed_refs = refs[:n_ctx]
    rest_ref, params_ref, result_ref, resid_ref, branch_ref, normed_ref, act_ref, pre_ref, mix_ref, sums_ref = refs[n_ctx:]
    me = me_ref[0]
    width = x_ref.shape[-1]
    group = width // n_ctx
    base = width * (1 + spans)

    def output_rows(place):
        first = pl.multiple_of(lax.bitwise_xor(me, place) * group, group)
        return rest_ref[pl.ds(first, group), 0:width]

    def param(row):
        return params_ref[row : row + 1, :]

    upstream = y_ref[0]
    residual = x_ref[0].astype(F32) + param(4)
    for place in range(n_ctx):
        residual = residual + dot(mixed_refs[place][0], output_rows(place), ((1,), (0,)))
    plain, scale = norm_parts(residual)
    normed = (plain * param(5) + param(6)).astype(BF16)
    normed_ref[...] = normed.T
    result = residual + param(7 + spans)
    grad_normed = jnp.zeros(residual.shape, F32)
    sums = []
    for span in range(spans):
        expand = rest_ref[:, width * (1 + span) : width * (2 + span)]
        shrink = rest_ref[:, base + width * span : base + width * (span + 1)]
        pre = dot(normed, expand, ((1,), (0,))) + param(7 + span)
        square = pre * pre
        bent = jnp.tanh(GELU_ROOT * (pre + GELU_CUBE * (square * pre)))
        half = 0.5 * (1.0 + bent)
        activated = (pre * half).astype(BF16)
        slope = half + (0.5 * pre) * (1.0 - bent * bent) * (GELU_ROOT + (3.0 * GELU_ROOT * GELU_CUBE) * square)
        act_ref[width * span : width * (span + 1), :] = activated.T
        result = result + dot(activated, shrink, ((1,), (0,)))
        grad_pre = (dot(upstream, shrink, ((1,), (1,))) * slope).astype(BF16)
        pre_ref[0, :, width * span : width * (span + 1)] = grad_pre
        grad_normed = grad_normed + dot(grad_pre, expand, ((1,), (1,)))
        sums.append(column_sum(grad_pre.astype(F32)))
    result_ref[0] = result.astype(BF16)
    gain_sum = column_sum(grad_normed * plain)
    shift_sum = column_sum(grad_normed)
    upstream_wide = upstream.astype(F32)
    grad_resid = upstream_wide + norm_back(plain, scale, grad_normed, param(5))
    resid_ref[0] = grad_resid
    branch = grad_resid.astype(BF16)
    branch_ref[0] = branch
    for place in range(n_ctx):
        mix_ref[place, 0] = dot(branch, output_rows(place), ((1,), (1,))).astype(BF16)
    table = jnp.concatenate(
        [column_sum(branch.astype(F32)), gain_sum, shift_sum] + sums + [column_sum(upstream_wide)], axis=0
    )

    @pl.when(pl.program_id(0) == 0)
    def _():
        sums_ref[...] = table

    @pl.when(pl.program_id(0) > 0)
    def _():
        sums_ref[...] += table


def layer(me, tokens, cotangent, mixed, rest, params):
    n_ctx = len(mixed)
    seqs, blk, width = tokens.shape
    group = width // n_ctx
    spans = (rest.shape[1] // width - 1) // 2
    hidden = spans * width

    def by_seq(*shape):
        return pl.BlockSpec((1,) + shape, lambda s, m: (s,) + (0,) * len(shape))

    def whole(shape):
        return pl.BlockSpec(shape, lambda s, m: (0,) * len(shape), pipeline_mode=pl.Buffered(1))

    return pl.pallas_call(
        functools.partial(layer_kernel, n_ctx, spans),
        grid_spec=pltpu.PrefetchScalarGridSpec(
            num_scalar_prefetch=1,
            grid=(seqs,),
            in_specs=[by_seq(blk, width)] * 2
            + [by_seq(blk, group)] * n_ctx
            + [whole(rest.shape), whole(params.shape)],
            out_specs=[
                by_seq(blk, width),
                by_seq(blk, width),
                by_seq(blk, width),
                pl.BlockSpec((width, blk), lambda s, m: (0, s)),
                pl.BlockSpec((hidden, blk), lambda s, m: (0, s)),
                by_seq(blk, hidden),
                pl.BlockSpec((n_ctx, 1, blk, group), lambda s, m: (0, s, 0, 0)),
                pl.BlockSpec((4 + spans, width), lambda s, m: (0, 0)),
            ],
        ),
        out_shape=[
            jax.ShapeDtypeStruct((seqs, blk, width), BF16),
            jax.ShapeDtypeStruct((seqs, blk, width), F32),
            jax.ShapeDtypeStruct((seqs, blk, width), BF16),
            jax.ShapeDtypeStruct((width, seqs * blk), BF16),
            jax.ShapeDtypeStruct((hidden, seqs * blk), BF16),
            jax.ShapeDtypeStruct((seqs, blk, hidden), BF16),
            jax.ShapeDtypeStruct((n_ctx, seqs, blk, group), BF16),
            jax.ShapeDtypeStruct((4 + spans, width), F32),
        ],
        compiler_params=pltpu.CompilerParams(vmem_limit_bytes=VMEM_BYTES),
        cost_estimate=pl.CostEstimate(
            flops=2 * seqs * blk * width * (2 * width + 4 * hidden),
            bytes_accessed=rest.size * 2 + seqs * blk * (hidden * 4 + width * 14),
            transcendentals=seqs * blk * hidden,
        ),
        name="layer",
    )(me, tokens, cotangent, *mixed, rest, params)


def backward_kernel(
    n_blk, blk, heads, me_ref, joint_ref, *refs
):
    grad_refs = refs[:n_blk]
    start_ref, log_ref, out_ref, joint, grads, bias, totals = refs[n_blk:]
    me = me_ref[0]
    group = heads * HDIM
    for place in range(n_blk):
        rows = pl.ds(pl.multiple_of(lax.bitwise_xor(me, place) * blk, blk), blk)
        joint[rows, :] = joint_ref[place, 0]
        grads[rows, :] = grad_refs[place][0]
    offsets = fill_bias(bias, start_ref, n_blk, blk)
    tasks = [(block, head) for block in reversed(range(n_blk)) for head in range(heads)]

    def products(task):
        block, head = task
        low = head * HDIM
        keys = (block + 1) * blk
        rows = slice(block * blk, keys)
        query = joint[rows, low : low + HDIM] * 0.125
        grad = grads[rows, low : low + HDIM]
        scores = dot(joint[:keys, group + low : group + low + HDIM], query, ((1,), (1,)))
        grad_probs = dot(joint[:keys, 2 * group + low : 2 * group + low + HDIM], grad, ((1,), (1,)))
        zeros = jnp.zeros((blk, HDIM), BF16)
        pair = jnp.concatenate(
            [jnp.concatenate([query, zeros], axis=1), jnp.concatenate([zeros, grad], axis=1)], axis=0
        )
        return scores, grad_probs, pair

    ahead = products(tasks[0])
    grad_queries = []
    for number, (block, head) in enumerate(tasks):
        scores, grad_probs, pair = ahead
        if number + 1 < len(tasks):
            ahead = products(tasks[number + 1])
        keys = (block + 1) * blk
        low = head * HDIM
        scores = scores + bias[offsets[block] : offsets[block] + keys, :]
        probs = jnp.exp(scores - log_ref[0, head : head + 1, block * blk : keys])
        inner = jnp.sum(probs * grad_probs, axis=0, keepdims=True)
        grad_scores = (probs * (grad_probs - inner)).astype(BF16)
        terms = dot(jnp.concatenate([grad_scores, probs.astype(BF16)], axis=1), pair, ((1,), (0,)))
        if block == n_blk - 1:
            totals[head, :keys, :] = terms
        else:
            totals[head, :keys, :] += terms
        key = joint[:keys, group + low : group + low + HDIM]
        grad_queries.append(dot(key, grad_scores, ((0,), (0,))) * 0.125)
        if head == heads - 1:
            out_ref[lax.bitwise_xor(me, block), 0, :, :group] = jnp.concatenate(grad_queries, axis=0).T.astype(BF16)
            grad_queries = []
    for block in range(n_blk):
        rows = slice(block * blk, (block + 1) * blk)
        place = lax.bitwise_xor(me, block)
        sides = [totals[head, rows, :].astype(BF16) for head in range(heads)]
        out_ref[place, 0, :, group:] = jnp.concatenate(
            [side[:, :HDIM] for side in sides] + [side[:, HDIM:] for side in sides], axis=1
        )


def attend_backward(me, joint, grads, start, logs, first, count):
    n_blk, _, blk, cols = joint.shape
    group = cols // 3
    heads = group // HDIM
    length = n_blk * blk
    return pl.pallas_call(
        functools.partial(backward_kernel, n_blk, blk, heads),
        grid_spec=pltpu.PrefetchScalarGridSpec(
            num_scalar_prefetch=1,
            grid=(count,),
            in_specs=[pl.BlockSpec((n_blk, 1, blk, cols), lambda s, m: (0, s + first, 0, 0))]
            + [pl.BlockSpec((1, blk, group), lambda s, m: (s + first, 0, 0))] * n_blk
            + [
                pl.BlockSpec((1, 1, length), lambda s, m: (s + first, 0, 0)),
                pl.BlockSpec((1, heads, length), lambda s, m: (s + first, 0, 0)),
            ],
            out_specs=pl.BlockSpec((n_blk, 1, blk, cols), lambda s, m: (0, s, 0, 0)),
            scratch_shapes=[
                pltpu.VMEM((length, cols), BF16),
                pltpu.VMEM((length, group), BF16),
                pltpu.VMEM((bias_rows(n_blk, blk), blk), F32),
                pltpu.VMEM((heads, length, 2 * HDIM), F32),
            ],
        ),
        out_shape=jax.ShapeDtypeStruct((n_blk, count, blk, cols), BF16),
        compiler_params=pltpu.CompilerParams(vmem_limit_bytes=VMEM_BYTES),
        cost_estimate=pl.CostEstimate(
            flops=count * heads * length * length * HDIM * 30,
            bytes_accessed=count * length * cols * 6,
            transcendentals=count * heads * length * length,
        ),
        name="attend_backward",
    )(me, joint, *grads, start, logs)


def unproject_kernel(n_blk, *refs):
    grad_ref, tokens = refs[0], refs[1 : 1 + n_blk]
    params_ref, weight_ref, share_ref, weight_grad_ref, sums_ref, bias_ref = refs[1 + n_blk :]
    weight_grad = bias_grad = gain_sum = shift_sum = 0.0
    for place in range(n_blk):
        grad = grad_ref[place, 0]
        plain, _ = norm_parts(tokens[place][0].astype(F32))
        normed = (plain * params_ref[0:1, :] + params_ref[1:2, :]).astype(BF16)
        share = dot(grad, weight_ref[...], ((1,), (1,)))
        share_ref[place, 0] = share.astype(BF16)
        gain_sum += column_sum(share * plain)
        shift_sum += column_sum(share)
        bias_grad += column_sum(grad.astype(F32))
        weight_grad += dot(normed, grad, ((0,), (0,)))
    sums = jnp.concatenate([gain_sum, shift_sum], axis=0)

    @pl.when(pl.program_id(0) == 0)
    def _():
        weight_grad_ref[...] = weight_grad
        sums_ref[...] = sums
        bias_ref[...] = bias_grad

    @pl.when(pl.program_id(0) > 0)
    def _():
        weight_grad_ref[...] += weight_grad
        sums_ref[...] += sums
        bias_ref[...] += bias_grad


def unproject(grad, tokens, params, weight, first):
    n_blk, count, blk, cols = grad.shape
    width = tokens[0].shape[-1]
    return pl.pallas_call(
        functools.partial(unproject_kernel, n_blk),
        grid=(count,),
        in_specs=[pl.BlockSpec((n_blk, 1, blk, cols), lambda s: (0, s, 0, 0))]
        + [pl.BlockSpec((1, blk, width), lambda s: (s + first, 0, 0))] * n_blk
        + [pl.BlockSpec(params.shape, lambda s: (0, 0)), pl.BlockSpec(weight.shape, lambda s: (0, 0))],
        out_specs=[
            pl.BlockSpec((n_blk, 1, blk, width), lambda s: (0, s, 0, 0)),
            pl.BlockSpec((width, cols), lambda s: (0, 0)),
            pl.BlockSpec((2, width), lambda s: (0, 0)),
            pl.BlockSpec((1, cols), lambda s: (0, 0)),
        ],
        out_shape=[
            jax.ShapeDtypeStruct((n_blk, count, blk, width), BF16),
            jax.ShapeDtypeStruct((width, cols), F32),
            jax.ShapeDtypeStruct((2, width), F32),
            jax.ShapeDtypeStruct((1, cols), F32),
        ],
        compiler_params=pltpu.CompilerParams(vmem_limit_bytes=VMEM_BYTES),
        cost_estimate=pl.CostEstimate(
            flops=4 * n_blk * count * blk * width * cols,
            bytes_accessed=2 * n_blk * count * blk * (2 * width + cols),
            transcendentals=0,
        ),
        name="unproject",
    )(grad, *tokens, params, weight)


def build(sizes):
    n_dp, n_ctx = sizes["dp"], sizes["ctx"]
    dp_bits = [bit for bit in range(16) if (1 << bit) < n_dp]
    ctx_bits = [bit for bit in range(16) if (1 << bit) < n_ctx]

    def swap(value, axis, mask):
        return lax.ppermute(value, axis, [(place, place ^ mask) for place in range(sizes[axis])])

    def reorder(items, me):
        stacked = jnp.stack(items)
        return [
            lax.dynamic_index_in_dim(stacked, lax.bitwise_xor(me, j), 0, keepdims=False) for j in range(len(items))
        ]

    def halve(value, labels, order, spots):
        labels = list(labels)
        for axis, bit in order:
            pos = labels.index((axis, bit))
            mine = (spots[axis] >> bit) & 1
            send = lax.dynamic_index_in_dim(value, 1 - mine, pos, keepdims=False).astype(BF16)
            keep = lax.dynamic_index_in_dim(value, mine, pos, keepdims=False)
            value = keep + swap(send, axis, 1 << bit).astype(F32)
            labels.pop(pos)
        return value

    def per_device(
        tokens_in,
        segments,
        cotangent,
        joint_weight,
        output_weight,
        expand_weight,
        shrink_weight,
        momentum_joint,
        momentum_output,
        momentum_expand,
        momentum_shrink,
        variance_joint,
        variance_output,
        variance_expand,
        variance_shrink,
        small_params,
        momentum_small,
        variance_small,
    ):
        seqs, stretch, width = tokens_in.shape
        hidden = expand_weight.shape[1]
        spans = hidden // width
        part = joint_weight.shape[0]
        group = width // n_ctx
        cols = 3 * group
        rows = seqs * stretch
        n_dev = n_dp * n_ctx
        n_bits = len(dp_bits)
        vectors = small_params.shape[0]
        me_dp, me = lax.axis_index("dp"), lax.axis_index("ctx")
        spots = {"dp": me_dp, "ctx": me}
        me_arr = me.astype(jnp.int32).reshape(1)

        joint_cast, small_cast, output_cast, expand_cast, shrink_cast = lax.optimization_barrier(
            (
                joint_weight.astype(BF16),
                small_params.astype(BF16),
                output_weight.astype(BF16),
                expand_weight.astype(BF16),
                shrink_weight.astype(BF16),
            )
        )

        blocks, seg_blocks = {0: tokens_in}, {0: segments}
        for bit in reversed(ctx_bits):
            for known in (seg_blocks, blocks):
                known.update({k ^ (1 << bit): swap(value, "ctx", 1 << bit) for k, value in list(known.items())})
        tokens = [blocks[k] for k in range(n_ctx)]
        segs = jnp.concatenate(reorder([seg_blocks[k] for k in range(n_ctx)], me), axis=1)
        start = jnp.zeros_like(segs)
        for number in range(1, DOCS):
            bound = jnp.sum((segs < number).astype(jnp.int32), axis=1, keepdims=True)
            start = jnp.where(segs >= number, bound, start)
        start = start[:, None, :]

        extra = -(-vectors * part // cols)
        pad = extra * cols - vectors * part
        small_rows = jnp.pad(small_cast.reshape(-1), (0, pad)).reshape(extra, cols)
        joint_cols = joint_cast.reshape(part, 3, n_ctx, group)

        def columns_for(k):
            picked = lax.dynamic_index_in_dim(joint_cols, lax.bitwise_xor(me, k), 2, keepdims=False)
            return jnp.concatenate([picked.reshape(part, cols), small_rows], axis=0)

        pieces = [columns_for(0)] + [swap(columns_for(k), "ctx", k) for k in range(1, n_ctx)]
        gathered = jnp.stack(reorder(pieces, me))
        expand_wide = expand_cast.reshape(part, n_dev, spans, part).transpose(0, 2, 1, 3).reshape(part, hidden)
        shrink_wide = shrink_cast.reshape(spans, part, width).transpose(1, 0, 2).reshape(part, hidden)
        rest = jnp.concatenate([output_cast, expand_wide, shrink_wide], axis=1)
        for bit in reversed(dp_bits):
            if bit == dp_bits[max(n_bits - 2, 0)]:
                rest, gathered, start = lax.optimization_barrier((rest, gathered, start))
                rest = lax.all_gather(rest, ("dp", "ctx"), axis=0, tiled=True)
            if bit == dp_bits[0]:
                gathered, *tokens = lax.optimization_barrier((gathered, *tokens))
            other = swap(gathered, "dp", 1 << bit)
            upper = ((me_dp >> bit) & 1) == 1
            gathered = jnp.where(upper, jnp.stack([other, gathered]), jnp.stack([gathered, other]))

        gathered = gathered.transpose(tuple(reversed(range(n_bits))) + tuple(range(n_bits, n_bits + 3)))
        gathered = gathered.reshape(n_dp, n_ctx, part + extra, cols)
        joint_lo = gathered[:, :, :part].reshape(width, cols)
        small_lo = gathered[:, :, part:].reshape(n_dp, n_ctx, extra * cols)[:, :, : vectors * part]
        params = small_lo.reshape(n_dp, n_ctx, vectors, part).transpose(2, 0, 1, 3).reshape(vectors, width).astype(F32)
        mine_bias = lax.dynamic_slice(params[2:4], (0, me * group), (2, group))
        joint_bias = jnp.concatenate([mine_bias[:1], jnp.zeros((1, group), F32), mine_bias[1:]], axis=1)
        bias_hidden = params[7 : 7 + spans].reshape(n_dev, spans, part).transpose(1, 0, 2).reshape(spans, width)
        params = jnp.concatenate([params[:7], bias_hidden, params[7 + spans :]], axis=0)

        joint = project(tokens, params, joint_lo, joint_bias)
        attended, logs = attend_forward(me_arr, joint, start)
        mixed = [attended[0]] + [swap(attended[k], "ctx", k) for k in range(1, n_ctx)]
        block_output, grad_resid, branch, normed_two, activated, grad_pre, grad_mixed, sums = layer(
            me_arr, tokens_in, cotangent, mixed, rest, params
        )
        grads = [grad_mixed[0]] + [swap(grad_mixed[k], "ctx", k) for k in range(1, n_ctx)]

        activated, grad_pre, normed_two, branch, grads[1] = lax.optimization_barrier(
            (activated, grad_pre, normed_two, branch, grads[1])
        )
        branch = branch.reshape(rows, width)
        grad_shrink = dot(activated, cotangent.reshape(rows, width), ((1,), (0,)))
        grad_expand = dot(normed_two, grad_pre.reshape(rows, hidden), ((1,), (0,)))
        grad_output = [dot(item.reshape(rows, group), branch, ((0,), (0,))) for item in mixed]
        grad_output = jnp.concatenate(reorder(grad_output, me), axis=0)

        labels = [("dp", bit) for bit in reversed(dp_bits)] + [("ctx", bit) for bit in reversed(ctx_bits)]
        bit_dims = (2,) * len(labels)
        core, far = [("ctx", ctx_bits[0])], [("ctx", bit) for bit in ctx_bits[1:]]
        inner = [("dp", bit) for bit in dp_bits]
        chains = [
            [grad_shrink.reshape((spans,) + bit_dims + (part, width)), None, ["span"] + labels, core + inner + far],
            [grad_expand.reshape(bit_dims + (part, hidden)), None, labels, core + far + inner],
            [grad_output.reshape(bit_dims + (part, width)), None, labels, core + far + inner],
        ]

        def split(chain):
            value, _, names, order = chain
            axis, bit = order[0]
            pos = names.index((axis, bit))
            mine = (spots[axis] >> bit) & 1
            chain[0] = lax.dynamic_index_in_dim(value, mine, pos, keepdims=False)
            chain[1] = lax.dynamic_index_in_dim(value, 1 - mine, pos, keepdims=False).astype(BF16)

        def merge(chain):
            _, _, names, order = chain
            axis, bit = order[0]
            got = swap(chain[1], axis, 1 << bit)
            chain[0] = chain[0] + got.astype(F32)
            chain[2] = [name for name in names if name != (axis, bit)]
            chain[3] = order[1:]

        def advance(after, before):
            pinned = lax.optimization_barrier((after,) + tuple(chain[0] for chain in chains))
            for chain, keep in zip(chains, pinned[1:]):
                chain[0] = keep
                merge(chain)
                split(chain)
            out = lax.optimization_barrier(
                (before,) + tuple(chain[0] for chain in chains) + tuple(chain[1] for chain in chains)
            )
            for number, chain in enumerate(chains):
                chain[0], chain[1] = out[1 + number], out[1 + len(chains) + number]
            return pinned[0], out[0]

        for chain in chains:
            split(chain)

        half = max(seqs // 2, 1)
        pending, shares, weight_grads = [], [], []
        source = joint
        for first in range(0, seqs, half):
            after = weight_grads[-1][1] if weight_grads else branch
            _, (source, *held) = advance(after, (source,) + tuple(pending))
            pending = []
            grad_joint = attend_backward(me_arr, source, grads, start, logs, first, half)
            if first:
                grad_joint, _ = advance(grad_joint, start)
            share, weight_grad, norm_sums, bias_sums = unproject(grad_joint, tokens, params, joint_lo, first)
            weight_grads.append((weight_grad, norm_sums, bias_sums))
            if held:
                shares.append(held)
            known = {k: share[k] for k in range(n_ctx)}
            for bit in ctx_bits[:-1]:
                mask = 1 << bit
                known = {
                    k: value.astype(F32) + swap(known[k | mask].astype(BF16), "ctx", mask).astype(F32)
                    for k, value in known.items()
                    if not k & mask
                }
            pending = [known[0], known[1 << ctx_bits[-1]].astype(BF16)]
        shares.append(pending)
        shares = [kept + swap(sent, "ctx", 1 << ctx_bits[-1]).astype(F32) for kept, sent in shares]
        weight_grad, norm_sums, bias_sums = [sum(items) for items in zip(*weight_grads)]

        plain, scale = norm_parts(tokens_in.astype(F32))
        input_grad = grad_resid + norm_back(plain, scale, jnp.concatenate(shares, axis=0), params[0])

        placed = lax.dynamic_update_slice(
            jnp.zeros((2, width), F32),
            jnp.concatenate([bias_sums[:, :group], bias_sums[:, 2 * group :]], axis=0),
            (0, me * group),
        )
        sums_hidden = sums[3 : 3 + spans].reshape(spans, n_dev, part).transpose(1, 0, 2).reshape(spans, width)
        grad_small = jnp.concatenate([norm_sums, placed, sums[:3], sums_hidden, sums[3 + spans :]], axis=0)
        small_terms = grad_small.reshape(vectors, n_dp, n_ctx, part).transpose(1, 2, 0, 3)
        small_terms = jnp.pad(small_terms.reshape(n_dp, n_ctx, vectors * part), ((0, 0), (0, 0), (0, pad)))
        terms = jnp.concatenate(
            [weight_grad.reshape(n_dp, n_ctx, part, cols), small_terms.reshape(n_dp, n_ctx, extra, cols)], axis=2
        ).reshape((2,) * n_bits + (n_ctx, part + extra, cols))
        dp_labels = [("dp", bit) for bit in reversed(dp_bits)]
        terms = halve(terms, dp_labels, [("dp", bit) for bit in dp_bits], spots)

        def terms_for(k):
            return lax.dynamic_index_in_dim(terms, lax.bitwise_xor(me, k), 0, keepdims=False)

        arrived = [terms_for(0)] + [
            swap(terms_for(k).astype(BF16), "ctx", k).astype(F32) for k in range(1, n_ctx)
        ]
        small_sum = sum(item[part:] for item in arrived).reshape(-1)[: vectors * part].reshape(vectors, part)
        sum_joint = jnp.stack([item[:part].reshape(part, 3, group) for item in reorder(arrived, me)], axis=2)
        sum_joint = sum_joint.reshape(part, 3 * width)

        for chain in chains:
            merge(chain)
            while chain[3]:
                split(chain)
                merge(chain)
        sum_shrink, sum_expand, sum_output = [chain[0] for chain in chains]
        sum_shrink = sum_shrink.reshape(spans * part, width)
        sum_expand = sum_expand.reshape(part, spans, n_dev, part).transpose(0, 2, 1, 3).reshape(part, hidden)

        new_joint, first_joint, second_joint = adam_step(
            joint_weight, sum_joint, momentum_joint, variance_joint, RATE_MATRIX, WEIGHT_DECAY
        )
        new_output, first_output, second_output = adam_step(
            output_weight, sum_output, momentum_output, variance_output, RATE_MATRIX, WEIGHT_DECAY
        )
        new_expand, first_expand, second_expand = adam_step(
            expand_weight, sum_expand, momentum_expand, variance_expand, RATE_MATRIX, WEIGHT_DECAY
        )
        new_shrink, first_shrink, second_shrink = adam_step(
            shrink_weight, sum_shrink, momentum_shrink, variance_shrink, RATE_MATRIX, WEIGHT_DECAY
        )
        new_small, first_small, second_small = adam_step(
            small_params, small_sum, momentum_small, variance_small, RATE_VECTOR, 0.0
        )
        return (
            block_output,
            input_grad,
            new_joint,
            new_output,
            new_expand,
            new_shrink,
            first_joint,
            first_output,
            first_expand,
            first_shrink,
            second_joint,
            second_output,
            second_expand,
            second_shrink,
            new_small,
            first_small,
            second_small,
        )

    return per_device


def solution(mesh):
    sizes = {axis: mesh.shape[axis] for axis in ("dp", "ctx")}
    tokens = P("dp", "ctx", None)
    matrix = P(("dp", "ctx"), None)
    table = P(None, ("dp", "ctx"))
    return jax.shard_map(
        build(sizes),
        mesh=mesh,
        in_specs=(tokens, P("dp", "ctx"), tokens) + (matrix,) * 12 + (table,) * 3,
        out_specs=(tokens, tokens) + (matrix,) * 12 + (table,) * 3,
        check_vma=False,
    )
```

```python
import functools

import jax
import jax.numpy as jnp
from jax import lax
from jax.experimental import pallas as pl
from jax.experimental.pallas import tpu as pltpu
from jax.sharding import PartitionSpec as P

HDIM = 64
STEP = 10

NORM_EPSILON = 1e-05
MASKED_SCORE = -1000000000.0
BETA_ONE = 0.9
BETA_TWO = 0.999
ADAM_EPSILON = 1e-08
RATE_MATRIX = 0.05
RATE_VECTOR = 0.3
WEIGHT_DECAY = 0.1
DOCS = 4
GELU_ROOT = 0.7978845608028654
GELU_CUBE = 0.044715
VMEM_BYTES = 56 * 1024 * 1024
COST = pl.CostEstimate(flops=20_000_000_000, bytes_accessed=1_000_000, transcendentals=0)

BF16 = jnp.bfloat16
F32 = jnp.float32


def norm_parts(values):
    centre = values - jnp.mean(values, axis=-1, keepdims=True)
    scale = lax.rsqrt(jnp.mean(centre * centre, axis=-1, keepdims=True) + NORM_EPSILON)
    return centre * scale, scale


def norm_back(plain, scale, grad, gain):
    grad_plain = grad * gain
    along = jnp.mean(grad_plain * plain, axis=-1, keepdims=True)
    return (grad_plain - jnp.mean(grad_plain, axis=-1, keepdims=True) - plain * along) * scale


def column_sum(values):
    return jnp.sum(values, axis=0, keepdims=True)


def adam_step(weight, gradient, first, second, rate, decay):
    first_new = BETA_ONE * first + (1.0 - BETA_ONE) * gradient
    second_new = BETA_TWO * second + (1.0 - BETA_TWO) * gradient * gradient
    first_hat = first_new / (1.0 - BETA_ONE**STEP)
    second_hat = second_new / (1.0 - BETA_TWO**STEP)
    updated = weight - rate * (first_hat / (jnp.sqrt(second_hat) + ADAM_EPSILON) + decay * weight)
    return (updated, first_new, second_new)


def dot(left, right, dims):
    return lax.dot_general(left, right, (dims, ((), ())), preferred_element_type=F32)


def project_kernel(n_blk, *refs):
    tokens, (params_ref, weight_ref, bias_ref, joint_ref) = refs[:n_blk], refs[n_blk:]
    for place in range(n_blk):
        plain, _ = norm_parts(tokens[place][0].astype(F32))
        normed = (plain * params_ref[0:1, :] + params_ref[1:2, :]).astype(BF16)
        joint = dot(normed, weight_ref[...], ((1,), (0,))) + bias_ref[...]
        joint_ref[place, 0] = joint.astype(BF16)


def project(tokens, params, weight, bias):
    n_blk = len(tokens)
    seqs, blk, width = tokens[0].shape
    cols = weight.shape[1]
    return pl.pallas_call(
        functools.partial(project_kernel, n_blk),
        grid=(seqs,),
        in_specs=[pl.BlockSpec((1, blk, width), lambda s: (s, 0, 0))] * n_blk
        + [
            pl.BlockSpec(params.shape, lambda s: (0, 0)),
            pl.BlockSpec(weight.shape, lambda s: (0, 0)),
            pl.BlockSpec(bias.shape, lambda s: (0, 0)),
        ],
        out_specs=pl.BlockSpec((n_blk, 1, blk, cols), lambda s: (0, s, 0, 0)),
        out_shape=jax.ShapeDtypeStruct((n_blk, seqs, blk, cols), BF16),
        compiler_params=pltpu.CompilerParams(vmem_limit_bytes=VMEM_BYTES),
        cost_estimate=COST,
        name="project",
    )(*tokens, params, weight, bias)


def fill_bias(bias, start_ref, n_blk, blk):
    offsets = []
    offset = 0
    for block in range(n_blk):
        keys = (block + 1) * blk
        key_pos = lax.broadcasted_iota(jnp.int32, (keys, blk), 0)
        query_pos = lax.broadcasted_iota(jnp.int32, (keys, blk), 1) + block * blk
        first = start_ref[0, :, block * blk : (block + 1) * blk]
        allowed = (key_pos >= first) & (key_pos <= query_pos)
        bias[offset : offset + keys, :] = jnp.where(allowed, 0.0, MASKED_SCORE)
        offsets.append(offset)
        offset += keys
    return offsets


def bias_rows(n_blk, blk):
    return n_blk * (n_blk + 1) // 2 * blk


def forward_kernel(n_blk, blk, heads, me_ref, joint_ref, start_ref, out_ref, log_ref, joint, bias):
    me = me_ref[0]
    group = heads * HDIM
    for block in range(n_blk):
        joint[block * blk : (block + 1) * blk, :] = joint_ref[lax.bitwise_xor(me, block), 0]
    offsets = fill_bias(bias, start_ref, n_blk, blk)
    tasks = [(block, head) for block in reversed(range(n_blk)) for head in range(heads)]

    def raw_scores(task):
        block, head = task
        low = head * HDIM
        query = joint[block * blk : (block + 1) * blk, low : low + HDIM] * 0.125
        return dot(joint[: (block + 1) * blk, group + low : group + low + HDIM], query, ((1,), (1,)))

    ahead = raw_scores(tasks[0])
    mixed = []
    for number, (block, head) in enumerate(tasks):
        scores = ahead
        if number + 1 < len(tasks):
            ahead = raw_scores(tasks[number + 1])
        keys = (block + 1) * blk
        low = head * HDIM
        scores = scores + bias[offsets[block] : offsets[block] + keys, :]
        top = jnp.max(scores, axis=0, keepdims=True)
        exponent = jnp.exp(scores - top)
        total = jnp.sum(exponent, axis=0, keepdims=True)
        value = joint[:keys, 2 * group + low : 2 * group + low + HDIM]
        mixed.append(dot(value, exponent.astype(BF16), ((0,), (0,))) * (1.0 / total))
        log_ref[0, head : head + 1, block * blk : (block + 1) * blk] = top + jnp.log(total)
        if head == heads - 1:
            out_ref[lax.bitwise_xor(me, block), 0] = jnp.concatenate(mixed, axis=0).T.astype(BF16)
            mixed = []


def attend_forward(me, joint, start):
    n_blk, seqs, blk, cols = joint.shape
    group = cols // 3
    heads = group // HDIM
    length = n_blk * blk
    return pl.pallas_call(
        functools.partial(forward_kernel, n_blk, blk, heads),
        grid_spec=pltpu.PrefetchScalarGridSpec(
            num_scalar_prefetch=1,
            grid=(seqs,),
            in_specs=[
                pl.BlockSpec((n_blk, 1, blk, cols), lambda s, m: (0, s, 0, 0)),
                pl.BlockSpec((1, 1, length), lambda s, m: (s, 0, 0)),
            ],
            out_specs=[
                pl.BlockSpec((n_blk, 1, blk, group), lambda s, m: (0, s, 0, 0)),
                pl.BlockSpec((1, heads, length), lambda s, m: (s, 0, 0)),
            ],
            scratch_shapes=[pltpu.VMEM((length, cols), BF16), pltpu.VMEM((bias_rows(n_blk, blk), blk), F32)],
        ),
        out_shape=[
            jax.ShapeDtypeStruct((n_blk, seqs, blk, group), BF16),
            jax.ShapeDtypeStruct((seqs, heads, length), F32),
        ],
        compiler_params=pltpu.CompilerParams(vmem_limit_bytes=VMEM_BYTES),
        cost_estimate=COST,
        name="attend_forward",
    )(me, joint, start)


def layer_kernel(
    n_ctx,
    spans,
    me_ref,
    x_ref,
    y_ref,
    *refs,
):
    mixed_refs = refs[:n_ctx]
    mine_ref, other_ref, params_ref = refs[n_ctx : n_ctx + 3]
    result_ref, resid_ref, branch_ref, normed_ref, act_ref, pre_ref, mix_ref, sums_ref = refs[n_ctx + 3 : n_ctx + 11]
    rest_ref, sems = refs[n_ctx + 11 :]
    me = me_ref[0]
    width = x_ref.shape[-1]
    group = width // n_ctx
    side = width // 2
    inner = spans // 2

    @pl.when(pl.program_id(0) == 0)
    def _():
        core = lax.bitwise_and(me, 1)
        mine = pltpu.make_async_copy(mine_ref, rest_ref.at[core], sems.at[0])
        other = pltpu.make_async_copy(other_ref, rest_ref.at[1 - core], sems.at[1])
        mine.start()
        other.start()
        mine.wait()
        other.wait()

    def output_rows(place, half):
        first = pl.multiple_of(lax.bitwise_xor(me, place) * group, group)
        return rest_ref[half, pl.ds(first, group), 0:side]

    def param(row):
        return params_ref[row : row + 1, :]

    upstream = y_ref[0]
    mixed = [ref[0] for ref in mixed_refs]
    sides = [
        sum(dot(mixed[place], output_rows(place, half), ((1,), (0,))) for place in range(n_ctx)) for half in range(2)
    ]
    residual = x_ref[0].astype(F32) + (jnp.concatenate(sides, axis=1) + param(4))
    plain, scale = norm_parts(residual)
    normed = (plain * param(5) + param(6)).astype(BF16)
    normed_ref[...] = normed.T
    result = residual + param(7 + spans)
    grad_normed = jnp.zeros(residual.shape, F32)
    sums = []
    for span in range(spans):
        half, low = span // inner, side + width * (span % inner)
        expand = rest_ref[half, :, low : low + width]
        shrink = rest_ref[half, :, low + width * inner : low + width * (inner + 1)]
        pre = dot(normed, expand, ((1,), (0,))) + param(7 + span)
        square = pre * pre
        bent = jnp.tanh(GELU_ROOT * (pre + GELU_CUBE * (square * pre)))
        half = 0.5 * (1.0 + bent)
        activated = (pre * half).astype(BF16)
        slope = half + (0.5 * pre) * (1.0 - bent * bent) * (GELU_ROOT + (3.0 * GELU_ROOT * GELU_CUBE) * square)
        act_ref[width * span : width * (span + 1), :] = activated.T
        result = result + dot(activated, shrink, ((1,), (0,)))
        grad_pre = (dot(upstream, shrink, ((1,), (1,))) * slope).astype(BF16)
        pre_ref[0, :, width * span : width * (span + 1)] = grad_pre
        grad_normed = grad_normed + dot(grad_pre, expand, ((1,), (1,)))
        sums.append(column_sum(grad_pre.astype(F32)))
    result_ref[0] = result.astype(BF16)
    gain_sum = column_sum(grad_normed * plain)
    shift_sum = column_sum(grad_normed)
    upstream_wide = upstream.astype(F32)
    grad_resid = upstream_wide + norm_back(plain, scale, grad_normed, param(5))
    resid_ref[0] = grad_resid
    branch = grad_resid.astype(BF16)
    branch_ref[0] = branch
    for place in range(n_ctx):
        mix = dot(branch[:, :side], output_rows(place, 0), ((1,), (1,)))
        mix_ref[place, 0] = (mix + dot(branch[:, side:], output_rows(place, 1), ((1,), (1,)))).astype(BF16)
    table = jnp.concatenate(
        [column_sum(branch.astype(F32)), gain_sum, shift_sum] + sums + [column_sum(upstream_wide)], axis=0
    )

    @pl.when(pl.program_id(0) == 0)
    def _():
        sums_ref[...] = table

    @pl.when(pl.program_id(0) > 0)
    def _():
        sums_ref[...] += table


def layer(me, tokens, cotangent, mixed, mine, other, params):
    n_ctx = len(mixed)
    seqs, blk, width = tokens.shape
    group = width // n_ctx
    spans = (2 * mine.shape[1] // width - 1) // 2
    hidden = spans * width

    def by_seq(*shape):
        return pl.BlockSpec((1,) + shape, lambda s, m: (s,) + (0,) * len(shape))

    def whole(shape):
        return pl.BlockSpec(shape, lambda s, m: (0,) * len(shape), pipeline_mode=pl.Buffered(1))

    return pl.pallas_call(
        functools.partial(layer_kernel, n_ctx, spans),
        grid_spec=pltpu.PrefetchScalarGridSpec(
            num_scalar_prefetch=1,
            grid=(seqs,),
            in_specs=[by_seq(blk, width)] * 2
            + [by_seq(blk, group)] * n_ctx
            + [pl.BlockSpec(memory_space=pl.ANY)] * 2
            + [whole(params.shape)],
            out_specs=[
                by_seq(blk, width),
                by_seq(blk, width),
                by_seq(blk, width),
                pl.BlockSpec((width, blk), lambda s, m: (0, s)),
                pl.BlockSpec((hidden, blk), lambda s, m: (0, s)),
                by_seq(blk, hidden),
                pl.BlockSpec((n_ctx, 1, blk, group), lambda s, m: (0, s, 0, 0)),
                pl.BlockSpec((4 + spans, width), lambda s, m: (0, 0)),
            ],
            scratch_shapes=[pltpu.VMEM((2,) + mine.shape, BF16), pltpu.SemaphoreType.DMA((2,))],
        ),
        out_shape=[
            jax.ShapeDtypeStruct((seqs, blk, width), BF16),
            jax.ShapeDtypeStruct((seqs, blk, width), F32),
            jax.ShapeDtypeStruct((seqs, blk, width), BF16),
            jax.ShapeDtypeStruct((width, seqs * blk), BF16),
            jax.ShapeDtypeStruct((hidden, seqs * blk), BF16),
            jax.ShapeDtypeStruct((seqs, blk, hidden), BF16),
            jax.ShapeDtypeStruct((n_ctx, seqs, blk, group), BF16),
            jax.ShapeDtypeStruct((4 + spans, width), F32),
        ],
        compiler_params=pltpu.CompilerParams(vmem_limit_bytes=VMEM_BYTES),
        cost_estimate=COST,
        name="layer",
    )(me, tokens, cotangent, *mixed, mine, other, params)


def backward_kernel(
    n_blk, blk, heads, me_ref, joint_ref, *refs
):
    grad_refs = refs[:n_blk]
    start_ref, log_ref, out_ref, joint, grads, bias, totals = refs[n_blk:]
    me = me_ref[0]
    group = heads * HDIM
    for place in range(n_blk):
        rows = pl.ds(pl.multiple_of(lax.bitwise_xor(me, place) * blk, blk), blk)
        joint[rows, :] = joint_ref[place, 0]
        grads[rows, :] = grad_refs[place][0]
    offsets = fill_bias(bias, start_ref, n_blk, blk)
    tasks = [(block, head) for block in reversed(range(n_blk)) for head in range(heads)]

    def products(task):
        block, head = task
        low = head * HDIM
        keys = (block + 1) * blk
        rows = slice(block * blk, keys)
        query = joint[rows, low : low + HDIM] * 0.125
        grad = grads[rows, low : low + HDIM]
        scores = dot(joint[:keys, group + low : group + low + HDIM], query, ((1,), (1,)))
        grad_probs = dot(joint[:keys, 2 * group + low : 2 * group + low + HDIM], grad, ((1,), (1,)))
        zeros = jnp.zeros((blk, HDIM), BF16)
        pair = jnp.concatenate(
            [jnp.concatenate([query, zeros], axis=1), jnp.concatenate([zeros, grad], axis=1)], axis=0
        )
        return scores, grad_probs, pair

    ahead = products(tasks[0])
    grad_queries = []
    for number, (block, head) in enumerate(tasks):
        scores, grad_probs, pair = ahead
        if number + 1 < len(tasks):
            ahead = products(tasks[number + 1])
        keys = (block + 1) * blk
        low = head * HDIM
        scores = scores + bias[offsets[block] : offsets[block] + keys, :]
        probs = jnp.exp(scores - log_ref[0, head : head + 1, block * blk : keys])
        inner = jnp.sum(probs * grad_probs, axis=0, keepdims=True)
        grad_scores = (probs * (grad_probs - inner)).astype(BF16)
        terms = dot(jnp.concatenate([grad_scores, probs.astype(BF16)], axis=1), pair, ((1,), (0,)))
        if block == n_blk - 1:
            totals[head, :keys, :] = terms
        else:
            totals[head, :keys, :] += terms
        key = joint[:keys, group + low : group + low + HDIM]
        grad_queries.append(dot(key, grad_scores, ((0,), (0,))) * 0.125)
        if head == heads - 1:
            out_ref[lax.bitwise_xor(me, block), 0, :, :group] = jnp.concatenate(grad_queries, axis=0).T.astype(BF16)
            grad_queries = []
    for block in range(n_blk):
        rows = slice(block * blk, (block + 1) * blk)
        place = lax.bitwise_xor(me, block)
        sides = [totals[head, rows, :].astype(BF16) for head in range(heads)]
        out_ref[place, 0, :, group:] = jnp.concatenate(
            [side[:, :HDIM] for side in sides] + [side[:, HDIM:] for side in sides], axis=1
        )


def attend_backward(me, joint, grads, start, logs, first):
    n_blk, count, blk, cols = joint.shape
    group = cols // 3
    heads = group // HDIM
    length = n_blk * blk
    return pl.pallas_call(
        functools.partial(backward_kernel, n_blk, blk, heads),
        grid_spec=pltpu.PrefetchScalarGridSpec(
            num_scalar_prefetch=1,
            grid=(count,),
            in_specs=[pl.BlockSpec((n_blk, 1, blk, cols), lambda s, m: (0, s, 0, 0))]
            + [pl.BlockSpec((1, blk, group), lambda s, m: (s + first, 0, 0))] * n_blk
            + [
                pl.BlockSpec((1, 1, length), lambda s, m: (s, 0, 0)),
                pl.BlockSpec((1, heads, length), lambda s, m: (s, 0, 0)),
            ],
            out_specs=pl.BlockSpec((n_blk, 1, blk, cols), lambda s, m: (0, s, 0, 0)),
            scratch_shapes=[
                pltpu.VMEM((length, cols), BF16),
                pltpu.VMEM((length, group), BF16),
                pltpu.VMEM((bias_rows(n_blk, blk), blk), F32),
                pltpu.VMEM((heads, length, 2 * HDIM), F32),
            ],
        ),
        out_shape=jax.ShapeDtypeStruct((n_blk, count, blk, cols), BF16),
        compiler_params=pltpu.CompilerParams(vmem_limit_bytes=VMEM_BYTES),
        cost_estimate=COST,
        name="attend_backward",
    )(me, joint, *grads, start, logs)


def unproject_kernel(n_blk, *refs):
    grad_ref, tokens = refs[0], refs[1 : 1 + n_blk]
    params_ref, weight_ref = refs[1 + n_blk : 3 + n_blk]
    earlier = refs[3 + n_blk : -4]
    share_ref, weight_grad_ref, sums_ref, bias_ref = refs[-4:]
    weight_grad = bias_grad = gain_sum = shift_sum = 0.0
    for place in range(n_blk):
        grad = grad_ref[place, 0]
        plain, _ = norm_parts(tokens[place][0].astype(F32))
        normed = (plain * params_ref[0:1, :] + params_ref[1:2, :]).astype(BF16)
        share = dot(grad, weight_ref[...], ((1,), (1,)))
        share_ref[place, 0] = share.astype(BF16)
        gain_sum += column_sum(share * plain)
        shift_sum += column_sum(share)
        bias_grad += column_sum(grad.astype(F32))
        weight_grad += dot(normed, grad, ((0,), (0,)))
    values = [weight_grad, jnp.concatenate([gain_sum, shift_sum], axis=0), bias_grad]
    totals = [weight_grad_ref, sums_ref, bias_ref]

    @pl.when(pl.program_id(0) == 0)
    def _():
        for number, (total, value) in enumerate(zip(totals, values)):
            total[...] = value + earlier[number][...] if earlier else value

    @pl.when(pl.program_id(0) > 0)
    def _():
        for total, value in zip(totals, values):
            total[...] += value


def unproject(grad, tokens, params, weight, earlier):
    n_blk, count, blk, cols = grad.shape
    width = tokens[0].shape[-1]

    def whole(shape):
        return pl.BlockSpec(shape, lambda s: (0, 0))

    return pl.pallas_call(
        functools.partial(unproject_kernel, n_blk),
        grid=(count,),
        in_specs=[pl.BlockSpec((n_blk, 1, blk, cols), lambda s: (0, s, 0, 0))]
        + [pl.BlockSpec((1, blk, width), lambda s: (s, 0, 0))] * n_blk
        + [whole(params.shape), whole(weight.shape)]
        + [whole(item.shape) for item in earlier],
        out_specs=[
            pl.BlockSpec((n_blk, 1, blk, width), lambda s: (0, s, 0, 0)),
            whole((width, cols)),
            whole((2, width)),
            whole((1, cols)),
        ],
        out_shape=[
            jax.ShapeDtypeStruct((n_blk, count, blk, width), BF16),
            jax.ShapeDtypeStruct((width, cols), F32),
            jax.ShapeDtypeStruct((2, width), F32),
            jax.ShapeDtypeStruct((1, cols), F32),
        ],
        compiler_params=pltpu.CompilerParams(vmem_limit_bytes=VMEM_BYTES),
        cost_estimate=COST,
        name="unproject",
    )(grad, *tokens, params, weight, *earlier)


def build(sizes):
    n_dp, n_ctx = sizes["dp"], sizes["ctx"]
    dp_bits = [bit for bit in range(16) if (1 << bit) < n_dp]
    ctx_bits = [bit for bit in range(16) if (1 << bit) < n_ctx]

    def swap(value, axis, mask):
        return lax.ppermute(value, axis, [(place, place ^ mask) for place in range(sizes[axis])])

    def reorder(items, me):
        stacked = jnp.stack(items)
        return [
            lax.dynamic_index_in_dim(stacked, lax.bitwise_xor(me, j), 0, keepdims=False) for j in range(len(items))
        ]

    def per_device(
        tokens_in,
        segments,
        cotangent,
        joint_weight,
        output_weight,
        expand_weight,
        shrink_weight,
        momentum_joint,
        momentum_output,
        momentum_expand,
        momentum_shrink,
        variance_joint,
        variance_output,
        variance_expand,
        variance_shrink,
        small_params,
        momentum_small,
        variance_small,
    ):
        seqs, stretch, width = tokens_in.shape
        hidden = expand_weight.shape[1]
        spans = hidden // width
        part = joint_weight.shape[0]
        group = width // n_ctx
        cols = 3 * group
        rows = seqs * stretch
        n_dev = n_dp * n_ctx
        n_bits = len(dp_bits)
        vectors = small_params.shape[0]
        me_dp, me = lax.axis_index("dp"), lax.axis_index("ctx")
        spots = {"dp": me_dp, "ctx": me}
        me_arr = me.astype(jnp.int32).reshape(1)

        joint_cast, small_cast, output_cast, expand_cast, shrink_cast = lax.optimization_barrier(
            (
                joint_weight.astype(BF16),
                small_params.astype(BF16),
                output_weight.astype(BF16),
                expand_weight.astype(BF16),
                shrink_weight.astype(BF16),
            )
        )

        seg_blocks = {0: segments}
        for bit in reversed(ctx_bits):
            seg_blocks.update({k ^ (1 << bit): swap(value, "ctx", 1 << bit) for k, value in list(seg_blocks.items())})
        segs = jnp.concatenate(reorder([seg_blocks[k] for k in range(n_ctx)], me), axis=1)
        start = jnp.zeros_like(segs)
        for number in range(1, DOCS):
            bound = jnp.sum((segs < number).astype(jnp.int32), axis=1, keepdims=True)
            start = jnp.where(segs >= number, bound, start)
        start = start[:, None, :]

        small_cols = small_cast.T
        joint_cols = joint_cast.reshape(part, 3, n_ctx, group)

        def columns_for(k):
            picked = lax.dynamic_index_in_dim(joint_cols, lax.bitwise_xor(me, k), 2, keepdims=False)
            return jnp.concatenate([picked.reshape(part, cols), small_cols], axis=1)

        pieces = [columns_for(0)] + [swap(columns_for(k), "ctx", k) for k in range(1, n_ctx)]
        gathered = jnp.stack(reorder(pieces, me))

        expand_wide = expand_cast.reshape(part, n_dev, spans, part).transpose(0, 2, 1, 3).reshape(part, hidden)
        shrink_wide = shrink_cast.reshape(spans, part, width).transpose(1, 0, 2).reshape(part, hidden)
        sides = [
            jnp.concatenate([item[:, h * size // 2 : (h + 1) * size // 2] for item, size in wide], axis=1)
            for wide in [((output_cast, width), (expand_wide, hidden), (shrink_wide, hidden))]
            for h in range(2)
        ]
        pair = me & 1
        rest_own = jnp.where(pair == 1, sides[1], sides[0])
        rest_got = swap(jnp.where(pair == 1, sides[0], sides[1]), "ctx", 1)
        rest = jnp.where(
            pair == 1,
            jnp.concatenate([rest_got, rest_own], axis=0),
            jnp.concatenate([rest_own, rest_got], axis=0),
        )
        pairs = [
            [d * n_ctx + c * 2 + p for d in range(n_dp) for c in range(n_ctx // 2)] for p in range(2)
        ]

        half = max(seqs // 2, 1)
        firsts = list(range(0, seqs, half))
        tokens = [{0: tokens_in[first : first + half]} for first in firsts]
        near, far_bits = 1, [bit for bit in reversed(ctx_bits) if bit]

        def fetch_far(blocks):
            for bit in far_bits:
                blocks.update({k ^ (1 << bit): swap(value, "ctx", 1 << bit) for k, value in list(blocks.items())})

        fetch_far(tokens[0])
        for step, bit in enumerate(reversed(dp_bits)):
            other = swap(gathered, "dp", 1 << bit)
            upper = ((me_dp >> bit) & 1) == 1
            gathered = jnp.where(upper, jnp.stack([other, gathered]), jnp.stack([gathered, other]))
            if step == 0:
                names = sorted(tokens[0])
                gathered, rest, start, later, *held = lax.optimization_barrier(
                    (gathered, rest, start, [blocks[0] for blocks in tokens[1:]]) + tuple(tokens[0][k] for k in names)
                )
                tokens[0] = dict(zip(names, held))
                for blocks, value in zip(tokens[1:], later):
                    blocks[0] = value
                    fetch_far(blocks)
                rest = lax.all_gather(rest, ("dp", "ctx"), axis=0, tiled=True, axis_index_groups=pairs)
            elif step == n_bits - 2:
                flat = [(number, k) for number, blocks in enumerate(tokens) for k in sorted(blocks)]
                gathered, *held = lax.optimization_barrier((gathered,) + tuple(tokens[n][k] for n, k in flat))
                for (number, k), value in zip(flat, held):
                    tokens[number][k] = value
        for blocks in tokens:
            blocks.update({k ^ near: swap(value, "ctx", near) for k, value in list(blocks.items())})
        tokens = [[blocks[k] for k in range(n_ctx)] for blocks in tokens]

        gathered = gathered.transpose(tuple(reversed(range(n_bits))) + tuple(range(n_bits, n_bits + 3)))
        gathered = gathered.reshape(width, cols + vectors)
        joint_lo = gathered[:, :cols]
        params = gathered[:, cols:].T.astype(F32)
        mine_bias = lax.dynamic_slice(params[2:4], (0, me * group), (2, group))
        joint_bias = jnp.concatenate([mine_bias[:1], jnp.zeros((1, group), F32), mine_bias[1:]], axis=1)
        bias_hidden = params[7 : 7 + spans].reshape(n_dev, spans, part).transpose(1, 0, 2).reshape(spans, width)
        params = jnp.concatenate([params[:7], bias_hidden, params[7 + spans :]], axis=0)

        joints, logs, mixed, waiting = [], [], [], None
        starts = [start[first : first + half] for first in firsts]
        for number in range(len(firsts)):
            joint = project(tokens[number], params, joint_lo, joint_bias)
            if waiting is not None:
                waiting, joint = lax.optimization_barrier((waiting, joint))
                waiting = [waiting[0]] + [swap(waiting[k], "ctx", k) for k in range(1, n_ctx)]
            attended, log = attend_forward(me_arr, joint, starts[number])
            if waiting is not None:
                waiting, attended = lax.optimization_barrier((waiting, attended))
                mixed.append(waiting)
            waiting = [attended[k] for k in range(n_ctx)]
            joints.append(joint)
            logs.append(log)
        waiting, rest = lax.optimization_barrier((waiting, rest))
        rest_other = swap(rest, "ctx", 1)
        mixed.append([waiting[0]] + [swap(waiting[k], "ctx", k) for k in range(1, n_ctx)])
        mixed = [jnp.concatenate(items, axis=0) for items in zip(*mixed)]
        block_output, grad_resid, branch, normed_two, activated, grad_pre, grad_mixed, sums = layer(
            me_arr, tokens_in, cotangent, mixed, rest, rest_other, params
        )
        grads = [grad_mixed[0]] + [swap(grad_mixed[k], "ctx", k) for k in range(1, n_ctx)]

        activated, grad_pre, normed_two, branch, grads[1] = lax.optimization_barrier(
            (activated, grad_pre, normed_two, branch, grads[1])
        )
        branch = branch.reshape(rows, width)
        grad_shrink = dot(activated, cotangent.reshape(rows, width), ((1,), (0,)))
        grad_expand = dot(normed_two, grad_pre.reshape(rows, hidden), ((1,), (0,)))
        grad_output = [dot(item.reshape(rows, group), branch, ((0,), (0,))) for item in mixed]
        grad_output = jnp.concatenate(reorder(grad_output, me), axis=0)

        labels = [("dp", bit) for bit in reversed(dp_bits)] + [("ctx", bit) for bit in reversed(ctx_bits)]
        bit_dims = (2,) * len(labels)
        core, far = [("ctx", ctx_bits[0])], [("ctx", bit) for bit in ctx_bits[1:]]
        inner = [("dp", bit) for bit in dp_bits]
        chains = [
            [grad_shrink.reshape((spans,) + bit_dims + (part, width)), None, ["span"] + labels, core + inner + far],
            [grad_expand.reshape(bit_dims + (part, hidden)), None, labels, core + far + inner],
            [grad_output.reshape(bit_dims + (part, width)), None, labels, core + far + inner],
        ]

        def split(chain):
            value, _, names, order = chain
            axis, bit = order[0]
            pos = names.index((axis, bit))
            mine = (spots[axis] >> bit) & 1
            chain[0] = lax.dynamic_index_in_dim(value, mine, pos, keepdims=False)
            chain[1] = lax.dynamic_index_in_dim(value, 1 - mine, pos, keepdims=False).astype(BF16)

        def fetch(chain):
            axis, bit = chain[3][0]
            return swap(chain[1], axis, 1 << bit)

        def merge(chain, got):
            _, _, names, order = chain
            chain[0] = chain[0] + got.astype(F32)
            chain[2] = [name for name in names if name != order[0]]
            chain[3] = order[1:]

        def advance(after, before):
            if len(chains[0][3]) < 2:
                return after, before
            after, keeps, gots = lax.optimization_barrier(
                (after, [chain[0] for chain in chains], [fetch(chain) for chain in chains])
            )
            for chain, keep, got in zip(chains, keeps, gots):
                chain[0] = keep
                merge(chain, got)
                split(chain)
            before, keeps, sends = lax.optimization_barrier(
                (before, [chain[0] for chain in chains], [chain[1] for chain in chains])
            )
            for chain, keep, send in zip(chains, keeps, sends):
                chain[0], chain[1] = keep, send
            return after, before

        for chain in chains:
            split(chain)

        top = 1 << ctx_bits[-1]
        pending, shares, earlier = None, [], ()
        for number, first in enumerate(firsts):
            _, (source, pending) = advance(earlier[1] if earlier else branch, (joints[number], pending))
            grad_joint = attend_backward(me_arr, source, grads, starts[number], logs[number], first)
            if pending:
                pending[1] = swap(pending[1], "ctx", top)
            (grad_joint, pending), _ = advance((grad_joint, pending), start)
            if pending:
                shares.append(pending[0] + pending[1].astype(F32))
            share, *earlier = unproject(grad_joint, tokens[number], params, joint_lo, earlier)
            known = {k: share[k] for k in range(n_ctx)}
            for bit in ctx_bits[:-1]:
                mask = 1 << bit
                known = {
                    k: value.astype(F32) + swap(known[k | mask].astype(BF16), "ctx", mask).astype(F32)
                    for k, value in known.items()
                    if not k & mask
                }
            pending = [known[0], known[top].astype(BF16)]
        shares.append(pending[0] + swap(pending[1], "ctx", top).astype(F32))
        weight_grad, norm_sums, bias_sums = earlier

        plain, scale = norm_parts(tokens_in.astype(F32))
        input_grad = grad_resid + norm_back(plain, scale, jnp.concatenate(shares, axis=0), params[0])

        placed = lax.dynamic_update_slice(
            jnp.zeros((2, width), F32),
            jnp.concatenate([bias_sums[:, :group], bias_sums[:, 2 * group :]], axis=0),
            (0, me * group),
        )
        sums_hidden = sums[3 : 3 + spans].reshape(spans, n_dev, part).transpose(1, 0, 2).reshape(spans, width)
        grad_small = jnp.concatenate([norm_sums, placed, sums[:3], sums_hidden, sums[3 + spans :]], axis=0)
        terms = jnp.concatenate([weight_grad, grad_small.T], axis=1).reshape(n_dp, n_ctx, part, cols + vectors)
        total = lax.dynamic_index_in_dim(terms, me_dp, 0, keepdims=False)
        if n_dp <= 8:
            sent = [
                lax.dynamic_index_in_dim(terms, lax.bitwise_xor(me_dp, j), 0, keepdims=False).astype(BF16)
                for j in range(1, n_dp)
            ]
            for j, item in enumerate(sent):
                total = total + swap(item, "dp", j + 1).astype(F32)
        else:
            terms = terms.reshape((2,) * n_bits + (n_ctx, part, cols + vectors))
            chain = [terms, None, [("dp", bit) for bit in reversed(dp_bits)], inner]
            while chain[3]:
                split(chain)
                merge(chain, fetch(chain))
            total = chain[0]

        def terms_for(k):
            return lax.dynamic_index_in_dim(total, lax.bitwise_xor(me, k), 0, keepdims=False)

        arrived = [terms_for(0)] + [
            swap(terms_for(k).astype(BF16), "ctx", k).astype(F32) for k in range(1, n_ctx)
        ]
        small_sum = sum(item[:, cols:] for item in arrived).T
        sum_joint = jnp.stack([item[:, :cols].reshape(part, 3, group) for item in reorder(arrived, me)], axis=2)
        sum_joint = sum_joint.reshape(part, 3 * width)

        for chain in chains:
            merge(chain, fetch(chain))
            while chain[3]:
                split(chain)
                merge(chain, fetch(chain))
        sum_shrink, sum_expand, sum_output = [chain[0] for chain in chains]
        sum_shrink = sum_shrink.reshape(spans * part, width)
        sum_expand = sum_expand.reshape(part, spans, n_dev, part).transpose(0, 2, 1, 3).reshape(part, hidden)

        new_joint, first_joint, second_joint = adam_step(
            joint_weight, sum_joint, momentum_joint, variance_joint, RATE_MATRIX, WEIGHT_DECAY
        )
        new_output, first_output, second_output = adam_step(
            output_weight, sum_output, momentum_output, variance_output, RATE_MATRIX, WEIGHT_DECAY
        )
        new_expand, first_expand, second_expand = adam_step(
            expand_weight, sum_expand, momentum_expand, variance_expand, RATE_MATRIX, WEIGHT_DECAY
        )
        new_shrink, first_shrink, second_shrink = adam_step(
            shrink_weight, sum_shrink, momentum_shrink, variance_shrink, RATE_MATRIX, WEIGHT_DECAY
        )
        new_small, first_small, second_small = adam_step(
            small_params, small_sum, momentum_small, variance_small, RATE_VECTOR, 0.0
        )
        return (
            block_output,
            input_grad,
            new_joint,
            new_output,
            new_expand,
            new_shrink,
            first_joint,
            first_output,
            first_expand,
            first_shrink,
            second_joint,
            second_output,
            second_expand,
            second_shrink,
            new_small,
            first_small,
            second_small,
        )

    return per_device


def solution(mesh):
    sizes = {axis: mesh.shape[axis] for axis in ("dp", "ctx")}
    tokens = P("dp", "ctx", None)
    matrix = P(("dp", "ctx"), None)
    table = P(None, ("dp", "ctx"))
    return jax.shard_map(
        build(sizes),
        mesh=mesh,
        in_specs=(tokens, P("dp", "ctx"), tokens) + (matrix,) * 12 + (table,) * 3,
        out_specs=(tokens, tokens) + (matrix,) * 12 + (table,) * 3,
        check_vma=False,
    )
```

```python
import functools

import jax
import jax.numpy as jnp
from jax import lax
from jax.experimental import pallas as pl
from jax.experimental.pallas import tpu as pltpu
from jax.sharding import PartitionSpec as P

HDIM = 64
STEP = 10

NORM_EPSILON = 1e-05
MASKED_SCORE = -1000000000.0
BETA_ONE = 0.9
BETA_TWO = 0.999
ADAM_EPSILON = 1e-08
RATE_MATRIX = 0.05
RATE_VECTOR = 0.3
WEIGHT_DECAY = 0.1
DOCS = 4
GELU_ROOT = 0.7978845608028654
GELU_CUBE = 0.044715
VMEM_BYTES = 56 * 1024 * 1024
COST = pl.CostEstimate(flops=20_000_000_000, bytes_accessed=1_000_000, transcendentals=0)

BF16 = jnp.bfloat16
F32 = jnp.float32


def norm_parts(values):
    centre = values - jnp.mean(values, axis=-1, keepdims=True)
    scale = lax.rsqrt(jnp.mean(centre * centre, axis=-1, keepdims=True) + NORM_EPSILON)
    return centre * scale, scale


def norm_back(plain, scale, grad, gain):
    grad_plain = grad * gain
    along = jnp.mean(grad_plain * plain, axis=-1, keepdims=True)
    return (grad_plain - jnp.mean(grad_plain, axis=-1, keepdims=True) - plain * along) * scale


def column_sum(values):
    return jnp.sum(values, axis=0, keepdims=True)


def adam_step(weight, gradient, first, second, rate, decay):
    first_new = BETA_ONE * first + (1.0 - BETA_ONE) * gradient
    second_new = BETA_TWO * second + (1.0 - BETA_TWO) * gradient * gradient
    first_hat = first_new / (1.0 - BETA_ONE**STEP)
    second_hat = second_new / (1.0 - BETA_TWO**STEP)
    updated = weight - rate * (first_hat / (jnp.sqrt(second_hat) + ADAM_EPSILON) + decay * weight)
    return (updated, first_new, second_new)


def dot(left, right, dims):
    return lax.dot_general(left, right, (dims, ((), ())), preferred_element_type=F32)


def project_kernel(n_blk, *refs):
    tokens, (params_ref, weight_ref, bias_ref, joint_ref) = refs[:n_blk], refs[n_blk:]
    for place in range(n_blk):
        plain, _ = norm_parts(tokens[place][0].astype(F32))
        normed = (plain * params_ref[0:1, :] + params_ref[1:2, :]).astype(BF16)
        joint = dot(normed, weight_ref[...], ((1,), (0,))) + bias_ref[...]
        joint_ref[place, 0] = joint.astype(BF16)


def project(tokens, params, weight, bias):
    n_blk = len(tokens)
    seqs, blk, width = tokens[0].shape
    cols = weight.shape[1]
    return pl.pallas_call(
        functools.partial(project_kernel, n_blk),
        grid=(seqs,),
        in_specs=[pl.BlockSpec((1, blk, width), lambda s: (s, 0, 0))] * n_blk
        + [
            pl.BlockSpec(params.shape, lambda s: (0, 0)),
            pl.BlockSpec(weight.shape, lambda s: (0, 0)),
            pl.BlockSpec(bias.shape, lambda s: (0, 0)),
        ],
        out_specs=pl.BlockSpec((n_blk, 1, blk, cols), lambda s: (0, s, 0, 0)),
        out_shape=jax.ShapeDtypeStruct((n_blk, seqs, blk, cols), BF16),
        compiler_params=pltpu.CompilerParams(vmem_limit_bytes=VMEM_BYTES),
        cost_estimate=COST,
        name="project",
    )(*tokens, params, weight, bias)


def fill_bias(bias, start_ref, n_blk, blk):
    offsets = []
    offset = 0
    for block in range(n_blk):
        keys = (block + 1) * blk
        key_pos = lax.broadcasted_iota(jnp.int32, (keys, blk), 0)
        query_pos = lax.broadcasted_iota(jnp.int32, (keys, blk), 1) + block * blk
        first = start_ref[0, :, block * blk : (block + 1) * blk]
        allowed = (key_pos >= first) & (key_pos <= query_pos)
        bias[offset : offset + keys, :] = jnp.where(allowed, 0.0, MASKED_SCORE)
        offsets.append(offset)
        offset += keys
    return offsets


def bias_rows(n_blk, blk):
    return n_blk * (n_blk + 1) // 2 * blk


def forward_kernel(n_blk, blk, heads, me_ref, joint_ref, start_ref, *refs):
    out_refs, (log_ref, joint, bias, out) = refs[:n_blk], refs[n_blk:]
    me = me_ref[0]
    group = heads * HDIM
    for block in range(n_blk):
        joint[block * blk : (block + 1) * blk, :] = joint_ref[lax.bitwise_xor(me, block), 0]
    offsets = fill_bias(bias, start_ref, n_blk, blk)
    tasks = [(block, head) for block in reversed(range(n_blk)) for head in range(heads)]

    def raw_scores(task):
        block, head = task
        low = head * HDIM
        query = joint[block * blk : (block + 1) * blk, low : low + HDIM] * 0.125
        return dot(joint[: (block + 1) * blk, group + low : group + low + HDIM], query, ((1,), (1,)))

    ahead = raw_scores(tasks[0])
    mixed = []
    for number, (block, head) in enumerate(tasks):
        scores = ahead
        if number + 1 < len(tasks):
            ahead = raw_scores(tasks[number + 1])
        keys = (block + 1) * blk
        low = head * HDIM
        scores = scores + bias[offsets[block] : offsets[block] + keys, :]
        top = jnp.max(scores, axis=0, keepdims=True)
        exponent = jnp.exp(scores - top)
        total = jnp.sum(exponent, axis=0, keepdims=True)
        value = joint[:keys, 2 * group + low : 2 * group + low + HDIM]
        mixed.append(dot(value, exponent.astype(BF16), ((0,), (0,))) * (1.0 / total))
        log_ref[0, head : head + 1, block * blk : (block + 1) * blk] = top + jnp.log(total)
        if head == heads - 1:
            out[lax.bitwise_xor(me, block)] = jnp.concatenate(mixed, axis=0).T.astype(BF16)
            mixed = []
    for place in range(n_blk):
        out_refs[place][0] = out[place]


def attend_forward(me, joint, start):
    n_blk, seqs, blk, cols = joint.shape
    group = cols // 3
    heads = group // HDIM
    length = n_blk * blk
    return pl.pallas_call(
        functools.partial(forward_kernel, n_blk, blk, heads),
        grid_spec=pltpu.PrefetchScalarGridSpec(
            num_scalar_prefetch=1,
            grid=(seqs,),
            in_specs=[
                pl.BlockSpec((n_blk, 1, blk, cols), lambda s, m: (0, s, 0, 0)),
                pl.BlockSpec((1, 1, length), lambda s, m: (s, 0, 0)),
            ],
            out_specs=[pl.BlockSpec((1, blk, group), lambda s, m: (s, 0, 0))] * n_blk
            + [pl.BlockSpec((1, heads, length), lambda s, m: (s, 0, 0))],
            scratch_shapes=[
                pltpu.VMEM((length, cols), BF16),
                pltpu.VMEM((bias_rows(n_blk, blk), blk), F32),
                pltpu.VMEM((n_blk, blk, group), BF16),
            ],
        ),
        out_shape=[jax.ShapeDtypeStruct((seqs, blk, group), BF16)] * n_blk
        + [jax.ShapeDtypeStruct((seqs, heads, length), F32)],
        compiler_params=pltpu.CompilerParams(vmem_limit_bytes=VMEM_BYTES),
        cost_estimate=COST,
        name="attend_forward",
    )(me, joint, start)


def layer_kernel(
    n_ctx,
    spans,
    me_ref,
    x_ref,
    y_ref,
    *refs,
):
    mixed_refs = refs[:n_ctx]
    mine_ref, other_ref, params_ref = refs[n_ctx : n_ctx + 3]
    result_ref, resid_ref, branch_ref, normed_ref, act_ref, pre_ref = refs[n_ctx + 3 : n_ctx + 9]
    mix_refs = refs[n_ctx + 9 : 2 * n_ctx + 9]
    sums_ref, rest_ref, sems = refs[2 * n_ctx + 9 :]
    me = me_ref[0]
    width = x_ref.shape[-1]
    group = width // n_ctx
    side = width // 2
    inner = spans // 2

    @pl.when(pl.program_id(0) == 0)
    def _():
        core = lax.bitwise_and(me, 1)
        mine = pltpu.make_async_copy(mine_ref, rest_ref.at[core], sems.at[0])
        other = pltpu.make_async_copy(other_ref, rest_ref.at[1 - core], sems.at[1])
        mine.start()
        other.start()
        mine.wait()
        other.wait()

    def output_rows(place, half):
        first = pl.multiple_of(lax.bitwise_xor(me, place) * group, group)
        return rest_ref[half, pl.ds(first, group), 0:side]

    def param(row):
        return params_ref[row : row + 1, :]

    upstream = y_ref[0]
    mixed = [ref[0] for ref in mixed_refs]
    sides = [
        sum(dot(mixed[place], output_rows(place, half), ((1,), (0,))) for place in range(n_ctx)) for half in range(2)
    ]
    residual = x_ref[0].astype(F32) + (jnp.concatenate(sides, axis=1) + param(4))
    plain, scale = norm_parts(residual)
    normed = (plain * param(5) + param(6)).astype(BF16)
    normed_ref[...] = normed.T
    result = residual + param(7 + spans)
    grad_normed = jnp.zeros(residual.shape, F32)
    sums = []
    for span in range(spans):
        half, low = span // inner, side + width * (span % inner)
        expand = rest_ref[half, :, low : low + width]
        shrink = rest_ref[half, :, low + width * inner : low + width * (inner + 1)]
        pre = dot(normed, expand, ((1,), (0,))) + param(7 + span)
        square = pre * pre
        bent = jnp.tanh(GELU_ROOT * (pre + GELU_CUBE * (square * pre)))
        half = 0.5 * (1.0 + bent)
        activated = (pre * half).astype(BF16)
        slope = half + (0.5 * pre) * (1.0 - bent * bent) * (GELU_ROOT + (3.0 * GELU_ROOT * GELU_CUBE) * square)
        act_ref[width * span : width * (span + 1), :] = activated.T
        result = result + dot(activated, shrink, ((1,), (0,)))
        grad_pre = (dot(upstream, shrink, ((1,), (1,))) * slope).astype(BF16)
        pre_ref[0, :, width * span : width * (span + 1)] = grad_pre
        grad_normed = grad_normed + dot(grad_pre, expand, ((1,), (1,)))
        sums.append(column_sum(grad_pre.astype(F32)))
    result_ref[0] = result.astype(BF16)
    gain_sum = column_sum(grad_normed * plain)
    shift_sum = column_sum(grad_normed)
    upstream_wide = upstream.astype(F32)
    grad_resid = upstream_wide + norm_back(plain, scale, grad_normed, param(5))
    resid_ref[0] = grad_resid
    branch = grad_resid.astype(BF16)
    branch_ref[0] = branch
    for place in range(n_ctx):
        mix = dot(branch[:, :side], output_rows(place, 0), ((1,), (1,)))
        mix_refs[place][0] = (mix + dot(branch[:, side:], output_rows(place, 1), ((1,), (1,)))).astype(BF16)
    table = jnp.concatenate(
        [column_sum(branch.astype(F32)), gain_sum, shift_sum] + sums + [column_sum(upstream_wide)], axis=0
    )

    @pl.when(pl.program_id(0) == 0)
    def _():
        sums_ref[...] = table

    @pl.when(pl.program_id(0) > 0)
    def _():
        sums_ref[...] += table


def layer(me, tokens, cotangent, mixed, mine, other, params):
    n_ctx = len(mixed)
    seqs, blk, width = tokens.shape
    group = width // n_ctx
    spans = (2 * mine.shape[1] // width - 1) // 2
    hidden = spans * width

    def by_seq(*shape):
        return pl.BlockSpec((1,) + shape, lambda s, m: (s,) + (0,) * len(shape))

    def whole(shape):
        return pl.BlockSpec(shape, lambda s, m: (0,) * len(shape), pipeline_mode=pl.Buffered(1))

    return pl.pallas_call(
        functools.partial(layer_kernel, n_ctx, spans),
        grid_spec=pltpu.PrefetchScalarGridSpec(
            num_scalar_prefetch=1,
            grid=(seqs,),
            in_specs=[by_seq(blk, width)] * 2
            + [by_seq(blk, group)] * n_ctx
            + [pl.BlockSpec(memory_space=pl.ANY)] * 2
            + [whole(params.shape)],
            out_specs=[
                by_seq(blk, width),
                by_seq(blk, width),
                by_seq(blk, width),
                pl.BlockSpec((width, blk), lambda s, m: (0, s)),
                pl.BlockSpec((hidden, blk), lambda s, m: (0, s)),
                by_seq(blk, hidden),
            ]
            + [by_seq(blk, group)] * n_ctx
            + [pl.BlockSpec((4 + spans, width), lambda s, m: (0, 0))],
            scratch_shapes=[pltpu.VMEM((2,) + mine.shape, BF16), pltpu.SemaphoreType.DMA((2,))],
        ),
        out_shape=[
            jax.ShapeDtypeStruct((seqs, blk, width), BF16),
            jax.ShapeDtypeStruct((seqs, blk, width), F32),
            jax.ShapeDtypeStruct((seqs, blk, width), BF16),
            jax.ShapeDtypeStruct((width, seqs * blk), BF16),
            jax.ShapeDtypeStruct((hidden, seqs * blk), BF16),
            jax.ShapeDtypeStruct((seqs, blk, hidden), BF16),
        ]
        + [jax.ShapeDtypeStruct((seqs, blk, group), BF16)] * n_ctx
        + [jax.ShapeDtypeStruct((4 + spans, width), F32)],
        compiler_params=pltpu.CompilerParams(vmem_limit_bytes=VMEM_BYTES),
        cost_estimate=COST,
        name="layer",
    )(me, tokens, cotangent, *mixed, mine, other, params)


def backward_kernel(
    n_blk, blk, heads, me_ref, joint_ref, *refs
):
    grad_refs = refs[:n_blk]
    start_ref, log_ref, out_ref, joint, grads, bias, totals = refs[n_blk:]
    me = me_ref[0]
    group = heads * HDIM
    for place in range(n_blk):
        rows = pl.ds(pl.multiple_of(lax.bitwise_xor(me, place) * blk, blk), blk)
        joint[rows, :] = joint_ref[place, 0]
        grads[rows, :] = grad_refs[place][0]
    offsets = fill_bias(bias, start_ref, n_blk, blk)
    tasks = [(block, head) for block in reversed(range(n_blk)) for head in range(heads)]

    def products(task):
        block, head = task
        low = head * HDIM
        keys = (block + 1) * blk
        rows = slice(block * blk, keys)
        query = joint[rows, low : low + HDIM] * 0.125
        grad = grads[rows, low : low + HDIM]
        scores = dot(joint[:keys, group + low : group + low + HDIM], query, ((1,), (1,)))
        grad_probs = dot(joint[:keys, 2 * group + low : 2 * group + low + HDIM], grad, ((1,), (1,)))
        zeros = jnp.zeros((blk, HDIM), BF16)
        pair = jnp.concatenate(
            [jnp.concatenate([query, zeros], axis=1), jnp.concatenate([zeros, grad], axis=1)], axis=0
        )
        return scores, grad_probs, pair

    ahead = products(tasks[0])
    grad_queries = []
    for number, (block, head) in enumerate(tasks):
        scores, grad_probs, pair = ahead
        if number + 1 < len(tasks):
            ahead = products(tasks[number + 1])
        keys = (block + 1) * blk
        low = head * HDIM
        scores = scores + bias[offsets[block] : offsets[block] + keys, :]
        probs = jnp.exp(scores - log_ref[0, head : head + 1, block * blk : keys])
        inner = jnp.sum(probs * grad_probs, axis=0, keepdims=True)
        grad_scores = (probs * (grad_probs - inner)).astype(BF16)
        terms = dot(jnp.concatenate([grad_scores, probs.astype(BF16)], axis=1), pair, ((1,), (0,)))
        if block == n_blk - 1:
            totals[head, :keys, :] = terms
        else:
            totals[head, :keys, :] += terms
        key = joint[:keys, group + low : group + low + HDIM]
        grad_queries.append(dot(key, grad_scores, ((0,), (0,))) * 0.125)
        if head == heads - 1:
            out_ref[lax.bitwise_xor(me, block), 0, :, :group] = jnp.concatenate(grad_queries, axis=0).T.astype(BF16)
            grad_queries = []
    for block in range(n_blk):
        rows = slice(block * blk, (block + 1) * blk)
        place = lax.bitwise_xor(me, block)
        sides = [totals[head, rows, :].astype(BF16) for head in range(heads)]
        out_ref[place, 0, :, group:] = jnp.concatenate(
            [side[:, :HDIM] for side in sides] + [side[:, HDIM:] for side in sides], axis=1
        )


def attend_backward(me, joint, grads, start, logs, first):
    n_blk, count, blk, cols = joint.shape
    group = cols // 3
    heads = group // HDIM
    length = n_blk * blk
    return pl.pallas_call(
        functools.partial(backward_kernel, n_blk, blk, heads),
        grid_spec=pltpu.PrefetchScalarGridSpec(
            num_scalar_prefetch=1,
            grid=(count,),
            in_specs=[pl.BlockSpec((n_blk, 1, blk, cols), lambda s, m: (0, s, 0, 0))]
            + [pl.BlockSpec((1, blk, group), lambda s, m: (s + first, 0, 0))] * n_blk
            + [
                pl.BlockSpec((1, 1, length), lambda s, m: (s, 0, 0)),
                pl.BlockSpec((1, heads, length), lambda s, m: (s, 0, 0)),
            ],
            out_specs=pl.BlockSpec((n_blk, 1, blk, cols), lambda s, m: (0, s, 0, 0)),
            scratch_shapes=[
                pltpu.VMEM((length, cols), BF16),
                pltpu.VMEM((length, group), BF16),
                pltpu.VMEM((bias_rows(n_blk, blk), blk), F32),
                pltpu.VMEM((heads, length, 2 * HDIM), F32),
            ],
        ),
        out_shape=jax.ShapeDtypeStruct((n_blk, count, blk, cols), BF16),
        compiler_params=pltpu.CompilerParams(vmem_limit_bytes=VMEM_BYTES),
        cost_estimate=COST,
        name="attend_backward",
    )(me, joint, *grads, start, logs)


def unproject_kernel(n_blk, me_ref, *refs):
    grad_ref, tokens = refs[0], refs[1 : 1 + n_blk]
    params_ref, weight_ref, earlier_ref, kept_ref, sent_ref, terms_ref = refs[1 + n_blk :]
    cols = grad_ref.shape[-1]
    group = cols // 3
    vectors = params_ref.shape[0]
    width = params_ref.shape[1]
    weight_grad = bias_grad = gain_sum = shift_sum = 0.0
    for place in range(n_blk):
        grad = grad_ref[place, 0]
        plain, _ = norm_parts(tokens[place][0].astype(F32))
        normed = (plain * params_ref[0:1, :] + params_ref[1:2, :]).astype(BF16)
        share = dot(grad, weight_ref[...], ((1,), (1,)))
        (sent_ref if place % 2 else kept_ref)[place // 2, 0] = share.astype(BF16)
        gain_sum += column_sum(share * plain)
        shift_sum += column_sum(share)
        bias_grad += column_sum(grad.astype(F32))
        weight_grad += dot(normed, grad, ((0,), (0,)))

    def placed(values):
        return jnp.concatenate([jnp.where(me_ref[0] == j, values, 0.0) for j in range(n_blk)], axis=1)

    table = jnp.concatenate(
        [gain_sum, shift_sum, placed(bias_grad[:, :group]), placed(bias_grad[:, 2 * group :])]
        + [jnp.zeros((vectors - 4, width), F32)],
        axis=0,
    ).T

    @pl.when(pl.program_id(0) == 0)
    def _():
        terms_ref[:, :cols] = weight_grad + earlier_ref[:, :cols]
        terms_ref[:, cols:] = table + earlier_ref[:, cols:]

    @pl.when(pl.program_id(0) > 0)
    def _():
        terms_ref[:, :cols] += weight_grad
        terms_ref[:, cols:] += table


def unproject(me, grad, tokens, params, weight, earlier):
    n_blk, count, blk, cols = grad.shape
    width = tokens[0].shape[-1]

    def whole(shape):
        return pl.BlockSpec(shape, lambda s, m: (0, 0))

    part = pl.BlockSpec((n_blk // 2, 1, blk, width), lambda s, m: (0, s, 0, 0))
    return pl.pallas_call(
        functools.partial(unproject_kernel, n_blk),
        grid_spec=pltpu.PrefetchScalarGridSpec(
            num_scalar_prefetch=1,
            grid=(count,),
            in_specs=[pl.BlockSpec((n_blk, 1, blk, cols), lambda s, m: (0, s, 0, 0))]
            + [pl.BlockSpec((1, blk, width), lambda s, m: (s, 0, 0))] * n_blk
            + [whole(params.shape), whole(weight.shape), whole(earlier.shape)],
            out_specs=[part, part, whole(earlier.shape)],
        ),
        out_shape=[jax.ShapeDtypeStruct((n_blk // 2, count, blk, width), BF16)] * 2
        + [jax.ShapeDtypeStruct(earlier.shape, F32)],
        compiler_params=pltpu.CompilerParams(vmem_limit_bytes=VMEM_BYTES),
        cost_estimate=COST,
        name="unproject",
    )(me, grad, *tokens, params, weight, earlier)


def finish_kernel(n_ctx, me_ref, *refs):
    pieces, refs = refs[:n_ctx], refs[n_ctx:]
    states, outs, held = refs[:6], refs[6:12], refs[12]
    for place in range(n_ctx):
        held[place] = pieces[place][...].astype(F32)
    vectors = states[3].shape[0]
    cols = held.shape[-1] - vectors
    group = cols // 3
    groups = [held[lax.bitwise_xor(me_ref[0], j)] for j in range(n_ctx)]
    gradient = jnp.concatenate(
        [item[:, third * group : (third + 1) * group] for third in range(3) for item in groups], axis=1
    )
    small = sum(item[:, cols:] for item in groups).T
    results = adam_step(states[0][...], gradient, states[1][...], states[2][...], RATE_MATRIX, WEIGHT_DECAY)
    results += adam_step(states[3][...], small, states[4][...], states[5][...], RATE_VECTOR, 0.0)
    for out, result in zip(outs, results):
        out[...] = result


def finish(me, pieces, states):
    n_ctx = len(pieces)
    return pl.pallas_call(
        functools.partial(finish_kernel, n_ctx),
        in_specs=[pl.BlockSpec(memory_space=pltpu.SMEM)] + [pl.BlockSpec(memory_space=pltpu.VMEM)] * (n_ctx + 6),
        out_specs=[pl.BlockSpec(memory_space=pltpu.VMEM)] * 6,
        out_shape=[jax.ShapeDtypeStruct(item.shape, F32) for item in states],
        scratch_shapes=[pltpu.VMEM((n_ctx,) + pieces[0].shape, F32)],
        compiler_params=pltpu.CompilerParams(vmem_limit_bytes=VMEM_BYTES),
        name="finish",
    )(me, *pieces, *states)


def build(sizes):
    n_dp, n_ctx = sizes["dp"], sizes["ctx"]
    dp_bits = [bit for bit in range(16) if (1 << bit) < n_dp]
    ctx_bits = [bit for bit in range(16) if (1 << bit) < n_ctx]

    def swap(value, axis, mask):
        return lax.ppermute(value, axis, [(place, place ^ mask) for place in range(sizes[axis])])

    def reorder(items, me):
        stacked = jnp.stack(items)
        return [
            lax.dynamic_index_in_dim(stacked, lax.bitwise_xor(me, j), 0, keepdims=False) for j in range(len(items))
        ]

    def per_device(
        tokens_in,
        segments,
        cotangent,
        joint_weight,
        output_weight,
        expand_weight,
        shrink_weight,
        momentum_joint,
        momentum_output,
        momentum_expand,
        momentum_shrink,
        variance_joint,
        variance_output,
        variance_expand,
        variance_shrink,
        small_params,
        momentum_small,
        variance_small,
    ):
        seqs, stretch, width = tokens_in.shape
        hidden = expand_weight.shape[1]
        spans = hidden // width
        part = joint_weight.shape[0]
        group = width // n_ctx
        cols = 3 * group
        rows = seqs * stretch
        n_dev = n_dp * n_ctx
        n_bits = len(dp_bits)
        vectors = small_params.shape[0]
        me_dp, me = lax.axis_index("dp"), lax.axis_index("ctx")
        spots = {"dp": me_dp, "ctx": me}
        me_arr = me.astype(jnp.int32).reshape(1)

        joint_cast, small_cast = lax.optimization_barrier((joint_weight.astype(BF16), small_params.astype(BF16)))
        output_cast, expand_cast, shrink_cast = lax.optimization_barrier(
            (output_weight.astype(BF16), expand_weight.astype(BF16), shrink_weight.astype(BF16))
        )

        seg_blocks = {0: segments}
        for bit in reversed(ctx_bits):
            seg_blocks.update({k ^ (1 << bit): swap(value, "ctx", 1 << bit) for k, value in list(seg_blocks.items())})
        segs = jnp.concatenate(reorder([seg_blocks[k] for k in range(n_ctx)], me), axis=1)
        start = jnp.zeros_like(segs)
        for number in range(1, DOCS):
            bound = jnp.sum((segs < number).astype(jnp.int32), axis=1, keepdims=True)
            start = jnp.where(segs >= number, bound, start)
        start = start[:, None, :]

        small_cols = small_cast.T
        joint_cols = joint_cast.reshape(part, 3, n_ctx, group)

        def columns_for(k):
            picked = lax.dynamic_index_in_dim(joint_cols, lax.bitwise_xor(me, k), 2, keepdims=False)
            return jnp.concatenate([picked.reshape(part, cols), small_cols], axis=1)

        pieces = [columns_for(0)] + [swap(columns_for(k), "ctx", k) for k in range(1, n_ctx)]

        expand_wide = expand_cast.reshape(part, n_dev, spans, part).transpose(0, 2, 1, 3).reshape(part, hidden)
        shrink_wide = shrink_cast.reshape(spans, part, width).transpose(1, 0, 2).reshape(part, hidden)
        sides = [
            jnp.concatenate([item[:, h * size // 2 : (h + 1) * size // 2] for item, size in wide], axis=1)
            for wide in [((output_cast, width), (expand_wide, hidden), (shrink_wide, hidden))]
            for h in range(2)
        ]
        pair = me & 1
        rest_own = jnp.where(pair == 1, sides[1], sides[0])
        rest_got = swap(jnp.where(pair == 1, sides[0], sides[1]), "ctx", 1)
        rest = jnp.where(
            pair == 1,
            jnp.concatenate([rest_got, rest_own], axis=0),
            jnp.concatenate([rest_own, rest_got], axis=0),
        )
        rest = lax.all_gather(rest, ("dp", "ctx"), axis=0, tiled=True, axis_index_groups=[
            [d * n_ctx + c * 2 + p for d in range(n_dp) for c in range(n_ctx // 2)] for p in range(2)
        ])

        half = max(seqs // 2, 1)
        firsts = list(range(0, seqs, half))
        tokens = [{0: tokens_in[first : first + half]} for first in firsts]
        near, far_bits = 1, [bit for bit in reversed(ctx_bits) if bit]

        def fetch_far(blocks):
            for bit in far_bits:
                blocks.update({k ^ (1 << bit): swap(value, "ctx", 1 << bit) for k, value in list(blocks.items())})

        fetch_far(tokens[0])
        names = sorted(tokens[0])
        pieces, start, later, held = lax.optimization_barrier(
            (pieces, start, [blocks[0] for blocks in tokens[1:]], [tokens[0][k] for k in names])
        )
        tokens[0] = dict(zip(names, held))
        for blocks, value in zip(tokens[1:], later):
            blocks[0] = value
            fetch_far(blocks)
        gathered = jnp.stack(reorder(pieces, me))
        for step, bit in enumerate(reversed(dp_bits)):
            other = swap(gathered, "dp", 1 << bit)
            upper = ((me_dp >> bit) & 1) == 1
            gathered = jnp.where(upper, jnp.stack([other, gathered]), jnp.stack([gathered, other]))
            if step == max(n_bits - 2, 0):
                flat = [(number, k) for number, blocks in enumerate(tokens) for k in sorted(blocks)]
                gathered, *held = lax.optimization_barrier((gathered,) + tuple(tokens[n][k] for n, k in flat))
                for (number, k), value in zip(flat, held):
                    tokens[number][k] = value
        for blocks in tokens:
            blocks.update({k ^ near: swap(value, "ctx", near) for k, value in list(blocks.items())})
        tokens = [[blocks[k] for k in range(n_ctx)] for blocks in tokens]

        gathered = gathered.transpose(tuple(reversed(range(n_bits))) + tuple(range(n_bits, n_bits + 3)))
        gathered = gathered.reshape(width, cols + vectors)
        joint_lo = gathered[:, :cols]
        params = gathered[:, cols:].T.astype(F32)
        mine_bias = lax.dynamic_slice(params[2:4], (0, me * group), (2, group))
        joint_bias = jnp.concatenate([mine_bias[:1], jnp.zeros((1, group), F32), mine_bias[1:]], axis=1)
        bias_hidden = params[7 : 7 + spans].reshape(n_dev, spans, part).transpose(1, 0, 2).reshape(spans, width)
        params = jnp.concatenate([params[:7], bias_hidden, params[7 + spans :]], axis=0)

        joints, logs, mixed, waiting = [], [], [], None
        starts = [start[first : first + half] for first in firsts]
        for number in range(len(firsts)):
            joint = project(tokens[number], params, joint_lo, joint_bias)
            if waiting is not None:
                waiting, joint = lax.optimization_barrier((waiting, joint))
                waiting = [waiting[0]] + [swap(waiting[k], "ctx", k) for k in range(1, n_ctx)]
            *attended, log = attend_forward(me_arr, joint, starts[number])
            if waiting is not None:
                waiting, attended = lax.optimization_barrier((waiting, attended))
                mixed.append(waiting)
            waiting = attended
            joints.append(joint)
            logs.append(log)
        waiting, rest = lax.optimization_barrier((waiting, rest))
        rest_other = swap(rest, "ctx", 1)
        mixed.append([waiting[0]] + [swap(waiting[k], "ctx", k) for k in range(1, n_ctx)])
        mixed = [jnp.concatenate(items, axis=0) for items in zip(*mixed)]
        block_output, grad_resid, branch, normed_two, activated, grad_pre, *grad_mixed, sums = layer(
            me_arr, tokens_in, cotangent, mixed, rest, rest_other, params
        )
        grads = [grad_mixed[0]] + [swap(grad_mixed[k], "ctx", k) for k in range(1, n_ctx)]

        activated, grad_pre, normed_two, branch, grads[1] = lax.optimization_barrier(
            (activated, grad_pre, normed_two, branch, grads[1])
        )
        branch = branch.reshape(rows, width)
        upstream = cotangent.reshape(rows, width)
        grad_pre = grad_pre.reshape(rows, hidden)
        labels = [("dp", bit) for bit in reversed(dp_bits)] + [("ctx", bit) for bit in reversed(ctx_bits)]
        bit_dims = (2,) * len(labels)
        core, far = [("ctx", ctx_bits[0])], [("ctx", bit) for bit in ctx_bits[1:]]
        low, high = [("dp", dp_bits[0])], [("dp", bit) for bit in dp_bits[1:]]
        cut = (spans - 1) * width
        grad_shrink = dot(activated[:cut], upstream, ((1,), (0,))).reshape((spans - 1,) + bit_dims + (part, width))
        grad_expand = dot(normed_two, grad_pre[:, :cut], ((1,), (0,))).reshape(bit_dims + (part, cut))
        grad_output = [dot(item.reshape(rows, group), branch, ((0,), (0,))) for item in mixed]
        grad_output = jnp.concatenate(reorder(grad_output, me), axis=0)
        grad_last = jnp.stack(
            [
                dot(activated[cut:], upstream, ((1,), (0,))),
                dot(normed_two, grad_pre[:, cut:], ((1,), (0,))),
                grad_output,
            ]
        ).reshape((3,) + bit_dims + (part, width))
        grad_shrink, grad_expand, grad_last, grads = lax.optimization_barrier(
            (grad_shrink, grad_expand, grad_last, grads)
        )
        chains = [
            [grad_shrink, None, ["unit"] + labels, core + low + high + far],
            [grad_expand, None, labels, core + far + low + high],
            [grad_last, None, ["unit"] + labels, core + high[:1] + far + low + high[1:]],
        ]

        def split(chain):
            value, _, names, order = chain
            axis, bit = order[0]
            pos = names.index((axis, bit))
            mine = (spots[axis] >> bit) & 1
            chain[0] = lax.dynamic_index_in_dim(value, mine, pos, keepdims=False)
            chain[1] = lax.dynamic_index_in_dim(value, 1 - mine, pos, keepdims=False).astype(BF16)

        def fetch(chain):
            axis, bit = chain[3][0]
            return swap(chain[1], axis, 1 << bit)

        def merge(chain, got):
            _, _, names, order = chain
            chain[0] = chain[0] + got.astype(F32)
            chain[2] = [name for name in names if name != order[0]]
            chain[3] = order[1:]

        def advance(after, before):
            if len(chains[0][3]) < 2:
                return after, before
            after, keeps, gots = lax.optimization_barrier(
                (after, [chain[0] for chain in chains], [fetch(chain) for chain in chains])
            )
            for chain, keep, got in zip(chains, keeps, gots):
                chain[0] = keep
                merge(chain, got)
                split(chain)
            before, keeps, sends = lax.optimization_barrier(
                (before, [chain[0] for chain in chains], [chain[1] for chain in chains])
            )
            for chain, keep, send in zip(chains, keeps, sends):
                chain[0], chain[1] = keep, send
            return after, before

        for chain in chains:
            split(chain)

        sums_hidden = sums[3 : 3 + spans].reshape(spans, n_dev, part).transpose(1, 0, 2).reshape(spans, width)
        table = jnp.concatenate([jnp.zeros((4, width), F32), sums[:3], sums_hidden, sums[3 + spans :]], axis=0)
        terms = jnp.concatenate([jnp.zeros((width, cols), F32), table.T], axis=1)
        pending, shares = None, []
        for number, first in enumerate(firsts):
            _, (source, pending) = advance(terms if number else branch, (joints[number], pending))
            grad_joint = attend_backward(me_arr, source, grads, starts[number], logs[number], first)
            if pending:
                pending[1] = [swap(value, "ctx", 1 << bit) for value, bit in zip(pending[1], ctx_bits[1:])]
            (grad_joint, pending), _ = advance((grad_joint, pending), start)
            if pending:
                shares.append(sum((value.astype(F32) for value in pending[1]), pending[0]))
            kept, sent, terms = unproject(me_arr, grad_joint, tokens[number], params, joint_lo, terms)
            if number < len(firsts) - 1:
                joined = kept.astype(F32) + swap(sent, "ctx", 1).astype(F32)
                pending = [joined[0], [joined[1 << (bit - 1)].astype(BF16) for bit in ctx_bits[1:]]]

        terms = terms.reshape((2,) * n_bits + (n_ctx, part, cols + vectors))
        chain = [terms, None, [("dp", bit) for bit in reversed(dp_bits)], low + high]
        split(chain)
        got, sent, kept = lax.optimization_barrier((fetch(chain), swap(sent, "ctx", 1), kept))
        merge(chain, got)
        joined = kept.astype(F32) + sent.astype(F32)
        crossing = [swap(joined[1 << (bit - 1)].astype(BF16), "ctx", 1 << bit) for bit in ctx_bits[1:]]
        if n_dp <= 8:
            items = chain[0].reshape(n_dp // 2, n_ctx, part, cols + vectors)
            spot = me_dp >> 1
            total = lax.dynamic_index_in_dim(items, spot, 0, keepdims=False)
            sent = [
                lax.dynamic_index_in_dim(items, lax.bitwise_xor(spot, j), 0, keepdims=False).astype(BF16)
                for j in range(1, n_dp // 2)
            ]
            gots = [swap(item, "dp", 2 * (j + 1)) for j, item in enumerate(sent)]
            total, gots, crossing = lax.optimization_barrier((total, gots, crossing))
            total = sum((item.astype(F32) for item in gots), total)
        else:
            while chain[3]:
                split(chain)
                merge(chain, fetch(chain))
            total = chain[0]
        shares.append(sum((value.astype(F32) for value in crossing), joined[0]))

        def terms_for(k):
            return lax.dynamic_index_in_dim(total, lax.bitwise_xor(me, k), 0, keepdims=False)

        sent = lax.optimization_barrier([terms_for(k).astype(BF16) for k in range(1, n_ctx)])
        arrived = [terms_for(0)] + [swap(item, "ctx", k + 1) for k, item in enumerate(sent)]
        new_joint, first_joint, second_joint, new_small, first_small, second_small = finish(
            me_arr,
            arrived,
            (joint_weight, momentum_joint, variance_joint, small_params, momentum_small, variance_small),
        )

        plain, scale = norm_parts(tokens_in.astype(F32))
        input_grad = grad_resid + norm_back(plain, scale, jnp.concatenate(shares, axis=0), params[0])

        for chain in chains:
            merge(chain, fetch(chain))
            while chain[3]:
                split(chain)
                merge(chain, fetch(chain))
        last_shrink, last_expand, sum_output = chains[2][0]
        sum_shrink = jnp.concatenate([chains[0][0].reshape(cut // n_dev, width), last_shrink], axis=0)
        sum_expand = jnp.concatenate([chains[1][0], last_expand], axis=1)
        sum_expand = sum_expand.reshape(part, spans, n_dev, part).transpose(0, 2, 1, 3).reshape(part, hidden)

        new_output, first_output, second_output = adam_step(
            output_weight, sum_output, momentum_output, variance_output, RATE_MATRIX, WEIGHT_DECAY
        )
        new_expand, first_expand, second_expand = adam_step(
            expand_weight, sum_expand, momentum_expand, variance_expand, RATE_MATRIX, WEIGHT_DECAY
        )
        new_shrink, first_shrink, second_shrink = adam_step(
            shrink_weight, sum_shrink, momentum_shrink, variance_shrink, RATE_MATRIX, WEIGHT_DECAY
        )
        return (
            block_output,
            input_grad,
            new_joint,
            new_output,
            new_expand,
            new_shrink,
            first_joint,
            first_output,
            first_expand,
            first_shrink,
            second_joint,
            second_output,
            second_expand,
            second_shrink,
            new_small,
            first_small,
            second_small,
        )

    return per_device


def solution(mesh):
    sizes = {axis: mesh.shape[axis] for axis in ("dp", "ctx")}
    tokens = P("dp", "ctx", None)
    matrix = P(("dp", "ctx"), None)
    table = P(None, ("dp", "ctx"))
    return jax.shard_map(
        build(sizes),
        mesh=mesh,
        in_specs=(tokens, P("dp", "ctx"), tokens) + (matrix,) * 12 + (table,) * 3,
        out_specs=(tokens, tokens) + (matrix,) * 12 + (table,) * 3,
        check_vma=False,
    )
```

```python
import functools

import jax
import jax.numpy as jnp
from jax import lax
from jax.experimental import pallas as pl
from jax.experimental.pallas import tpu as pltpu
from jax.sharding import PartitionSpec as P

HDIM = 64
STEP = 10

NORM_EPSILON = 1e-05
MASKED_SCORE = -1000000000.0
BETA_ONE = 0.9
BETA_TWO = 0.999
ADAM_EPSILON = 1e-08
RATE_MATRIX = 0.05
RATE_VECTOR = 0.3
WEIGHT_DECAY = 0.1
DOCS = 4
GELU_ROOT = 0.7978845608028654
GELU_CUBE = 0.044715
VMEM_BYTES = 56 * 1024 * 1024
COST = pl.CostEstimate(flops=20_000_000_000, bytes_accessed=1_000_000, transcendentals=0)

BF16 = jnp.bfloat16
F32 = jnp.float32


def norm_parts(values):
    centre = values - jnp.mean(values, axis=-1, keepdims=True)
    scale = lax.rsqrt(jnp.mean(centre * centre, axis=-1, keepdims=True) + NORM_EPSILON)
    return centre * scale, scale


def norm_back(plain, scale, grad, gain):
    grad_plain = grad * gain
    along = jnp.mean(grad_plain * plain, axis=-1, keepdims=True)
    return (grad_plain - jnp.mean(grad_plain, axis=-1, keepdims=True) - plain * along) * scale


def column_sum(values):
    return jnp.sum(values, axis=0, keepdims=True)


def adam_step(weight, gradient, first, second, rate, decay):
    first_new = BETA_ONE * first + (1.0 - BETA_ONE) * gradient
    second_new = BETA_TWO * second + (1.0 - BETA_TWO) * gradient * gradient
    first_hat = first_new / (1.0 - BETA_ONE**STEP)
    second_hat = second_new / (1.0 - BETA_TWO**STEP)
    updated = weight - rate * (first_hat / (jnp.sqrt(second_hat) + ADAM_EPSILON) + decay * weight)
    return (updated, first_new, second_new)


def dot(left, right, dims):
    return lax.dot_general(left, right, (dims, ((), ())), preferred_element_type=F32)


def project_kernel(n_blk, *refs):
    tokens, (params_ref, weight_ref, bias_ref, joint_ref, normed_ref) = refs[:n_blk], refs[n_blk:]
    for place in range(n_blk):
        plain, _ = norm_parts(tokens[place][0].astype(F32))
        normed = (plain * params_ref[0:1, :] + params_ref[1:2, :]).astype(BF16)
        normed_ref[place, 0] = normed
        joint = dot(normed, weight_ref[...], ((1,), (0,))) + bias_ref[...]
        joint_ref[place, 0] = joint.astype(BF16)


def project(tokens, params, weight, bias):
    n_blk = len(tokens)
    seqs, blk, width = tokens[0].shape
    cols = weight.shape[1]
    return pl.pallas_call(
        functools.partial(project_kernel, n_blk),
        grid=(seqs,),
        in_specs=[pl.BlockSpec((1, blk, width), lambda s: (s, 0, 0))] * n_blk
        + [
            pl.BlockSpec(params.shape, lambda s: (0, 0)),
            pl.BlockSpec(weight.shape, lambda s: (0, 0)),
            pl.BlockSpec(bias.shape, lambda s: (0, 0)),
        ],
        out_specs=[pl.BlockSpec((n_blk, 1, blk, size), lambda s: (0, s, 0, 0)) for size in (cols, width)],
        out_shape=[jax.ShapeDtypeStruct((n_blk, seqs, blk, size), BF16) for size in (cols, width)],
        compiler_params=pltpu.CompilerParams(vmem_limit_bytes=VMEM_BYTES),
        cost_estimate=COST,
        name="project",
    )(*tokens, params, weight, bias)


def fill_bias(bias, start_ref, n_blk, blk):
    offsets = []
    offset = 0
    for block in range(n_blk):
        keys = (block + 1) * blk
        key_pos = lax.broadcasted_iota(jnp.int32, (keys, blk), 0)
        query_pos = lax.broadcasted_iota(jnp.int32, (keys, blk), 1) + block * blk
        first = start_ref[0, :, block * blk : (block + 1) * blk]
        allowed = (key_pos >= first) & (key_pos <= query_pos)
        bias[offset : offset + keys, :] = jnp.where(allowed, 0.0, MASKED_SCORE)
        offsets.append(offset)
        offset += keys
    return offsets


def bias_rows(n_blk, blk):
    return n_blk * (n_blk + 1) // 2 * blk


def forward_kernel(n_blk, blk, heads, me_ref, joint_ref, start_ref, *refs):
    out_refs, (log_ref, joint, bias, out) = refs[:n_blk], refs[n_blk:]
    me = me_ref[0]
    group = heads * HDIM
    for block in range(n_blk):
        joint[block * blk : (block + 1) * blk, :] = joint_ref[lax.bitwise_xor(me, block), 0]
    offsets = fill_bias(bias, start_ref, n_blk, blk)
    tasks = [(block, head) for block in reversed(range(n_blk)) for head in range(heads)]

    def raw_scores(task):
        block, head = task
        low = head * HDIM
        query = joint[block * blk : (block + 1) * blk, low : low + HDIM] * 0.125
        return dot(joint[: (block + 1) * blk, group + low : group + low + HDIM], query, ((1,), (1,)))

    ahead = raw_scores(tasks[0])
    mixed = []
    for number, (block, head) in enumerate(tasks):
        scores = ahead
        if number + 1 < len(tasks):
            ahead = raw_scores(tasks[number + 1])
        keys = (block + 1) * blk
        low = head * HDIM
        scores = scores + bias[offsets[block] : offsets[block] + keys, :]
        top = jnp.max(scores, axis=0, keepdims=True)
        exponent = jnp.exp(scores - top)
        total = jnp.sum(exponent, axis=0, keepdims=True)
        value = joint[:keys, 2 * group + low : 2 * group + low + HDIM]
        mixed.append(dot(value, exponent.astype(BF16), ((0,), (0,))) * (1.0 / total))
        log_ref[0, head : head + 1, block * blk : (block + 1) * blk] = top + jnp.log(total)
        if head == heads - 1:
            out[lax.bitwise_xor(me, block)] = jnp.concatenate(mixed, axis=0).T.astype(BF16)
            mixed = []
    for place in range(n_blk):
        out_refs[place][0] = out[place]


def attend_forward(me, joint, start):
    n_blk, seqs, blk, cols = joint.shape
    group = cols // 3
    heads = group // HDIM
    length = n_blk * blk
    return pl.pallas_call(
        functools.partial(forward_kernel, n_blk, blk, heads),
        grid_spec=pltpu.PrefetchScalarGridSpec(
            num_scalar_prefetch=1,
            grid=(seqs,),
            in_specs=[
                pl.BlockSpec((n_blk, 1, blk, cols), lambda s, m: (0, s, 0, 0)),
                pl.BlockSpec((1, 1, length), lambda s, m: (s, 0, 0)),
            ],
            out_specs=[pl.BlockSpec((1, blk, group), lambda s, m: (s, 0, 0))] * n_blk
            + [pl.BlockSpec((1, heads, length), lambda s, m: (s, 0, 0))],
            scratch_shapes=[
                pltpu.VMEM((length, cols), BF16),
                pltpu.VMEM((bias_rows(n_blk, blk), blk), F32),
                pltpu.VMEM((n_blk, blk, group), BF16),
            ],
        ),
        out_shape=[jax.ShapeDtypeStruct((seqs, blk, group), BF16)] * n_blk
        + [jax.ShapeDtypeStruct((seqs, heads, length), F32)],
        compiler_params=pltpu.CompilerParams(vmem_limit_bytes=VMEM_BYTES),
        cost_estimate=COST,
        name="attend_forward",
    )(me, joint, start)


def layer_kernel(
    n_ctx,
    spans,
    me_ref,
    x_ref,
    y_ref,
    *refs,
):
    mixed_refs = refs[:n_ctx]
    mine_ref, other_ref, params_ref = refs[n_ctx : n_ctx + 3]
    result_ref, resid_ref, branch_ref, normed_ref, act_ref, pre_ref = refs[n_ctx + 3 : n_ctx + 9]
    mix_refs = refs[n_ctx + 9 : 2 * n_ctx + 9]
    sums_ref, rest_ref, sems = refs[2 * n_ctx + 9 :]
    me = me_ref[0]
    width = x_ref.shape[-1]
    group = width // n_ctx
    side = width // 2
    inner = spans // 2

    @pl.when(pl.program_id(0) == 0)
    def _():
        core = lax.bitwise_and(me, 1)
        mine = pltpu.make_async_copy(mine_ref, rest_ref.at[core], sems.at[0])
        other = pltpu.make_async_copy(other_ref, rest_ref.at[1 - core], sems.at[1])
        mine.start()
        other.start()
        mine.wait()
        other.wait()

    def output_rows(place, half):
        first = pl.multiple_of(lax.bitwise_xor(me, place) * group, group)
        return rest_ref[half, pl.ds(first, group), 0:side]

    def param(row):
        return params_ref[row : row + 1, :]

    upstream = y_ref[0]
    mixed = [ref[0] for ref in mixed_refs]
    sides = [
        sum(dot(mixed[place], output_rows(place, half), ((1,), (0,))) for place in range(n_ctx)) for half in range(2)
    ]
    residual = x_ref[0].astype(F32) + (jnp.concatenate(sides, axis=1) + param(4))
    plain, scale = norm_parts(residual)
    normed = (plain * param(5) + param(6)).astype(BF16)
    normed_ref[...] = normed.T
    result = residual + param(7 + spans)
    grad_normed = jnp.zeros(residual.shape, F32)
    sums = []
    for span in range(spans):
        half, low = span // inner, side + width * (span % inner)
        expand = rest_ref[half, :, low : low + width]
        shrink = rest_ref[half, :, low + width * inner : low + width * (inner + 1)]
        pre = dot(normed, expand, ((1,), (0,))) + param(7 + span)
        square = pre * pre
        bent = jnp.tanh(GELU_ROOT * (pre + GELU_CUBE * (square * pre)))
        half = 0.5 * (1.0 + bent)
        activated = (pre * half).astype(BF16)
        slope = half + (0.5 * pre) * (1.0 - bent * bent) * (GELU_ROOT + (3.0 * GELU_ROOT * GELU_CUBE) * square)
        act_ref[width * span : width * (span + 1), :] = activated.T
        result = result + dot(activated, shrink, ((1,), (0,)))
        grad_pre = (dot(upstream, shrink, ((1,), (1,))) * slope).astype(BF16)
        pre_ref[0, :, width * span : width * (span + 1)] = grad_pre
        grad_normed = grad_normed + dot(grad_pre, expand, ((1,), (1,)))
        sums.append(column_sum(grad_pre.astype(F32)))
    result_ref[0] = result.astype(BF16)
    gain_sum = column_sum(grad_normed * plain)
    shift_sum = column_sum(grad_normed)
    upstream_wide = upstream.astype(F32)
    grad_resid = upstream_wide + norm_back(plain, scale, grad_normed, param(5))
    resid_ref[0] = grad_resid
    branch = grad_resid.astype(BF16)
    branch_ref[0] = branch
    for place in range(n_ctx):
        mix = dot(branch[:, :side], output_rows(place, 0), ((1,), (1,)))
        mix_refs[place][0] = (mix + dot(branch[:, side:], output_rows(place, 1), ((1,), (1,)))).astype(BF16)
    table = jnp.concatenate(
        [column_sum(branch.astype(F32)), gain_sum, shift_sum] + sums + [column_sum(upstream_wide)], axis=0
    )

    @pl.when(pl.program_id(0) == 0)
    def _():
        sums_ref[...] = table

    @pl.when(pl.program_id(0) > 0)
    def _():
        sums_ref[...] += table


def layer(me, tokens, cotangent, mixed, mine, other, params):
    n_ctx = len(mixed)
    seqs, blk, width = tokens.shape
    group = width // n_ctx
    spans = (2 * mine.shape[1] // width - 1) // 2
    hidden = spans * width

    def by_seq(*shape):
        return pl.BlockSpec((1,) + shape, lambda s, m: (s,) + (0,) * len(shape))

    def whole(shape):
        return pl.BlockSpec(shape, lambda s, m: (0,) * len(shape), pipeline_mode=pl.Buffered(1))

    return pl.pallas_call(
        functools.partial(layer_kernel, n_ctx, spans),
        grid_spec=pltpu.PrefetchScalarGridSpec(
            num_scalar_prefetch=1,
            grid=(seqs,),
            in_specs=[by_seq(blk, width)] * 2
            + [by_seq(blk, group)] * n_ctx
            + [pl.BlockSpec(memory_space=pl.ANY)] * 2
            + [whole(params.shape)],
            out_specs=[
                by_seq(blk, width),
                by_seq(blk, width),
                by_seq(blk, width),
                pl.BlockSpec((width, blk), lambda s, m: (0, s)),
                pl.BlockSpec((hidden, blk), lambda s, m: (0, s)),
                by_seq(blk, hidden),
            ]
            + [by_seq(blk, group)] * n_ctx
            + [pl.BlockSpec((4 + spans, width), lambda s, m: (0, 0))],
            scratch_shapes=[pltpu.VMEM((2,) + mine.shape, BF16), pltpu.SemaphoreType.DMA((2,))],
        ),
        out_shape=[
            jax.ShapeDtypeStruct((seqs, blk, width), BF16),
            jax.ShapeDtypeStruct((seqs, blk, width), F32),
            jax.ShapeDtypeStruct((seqs, blk, width), BF16),
            jax.ShapeDtypeStruct((width, seqs * blk), BF16),
            jax.ShapeDtypeStruct((hidden, seqs * blk), BF16),
            jax.ShapeDtypeStruct((seqs, blk, hidden), BF16),
        ]
        + [jax.ShapeDtypeStruct((seqs, blk, group), BF16)] * n_ctx
        + [jax.ShapeDtypeStruct((4 + spans, width), F32)],
        compiler_params=pltpu.CompilerParams(vmem_limit_bytes=VMEM_BYTES),
        cost_estimate=COST,
        name="layer",
    )(me, tokens, cotangent, *mixed, mine, other, params)


def backward_kernel(
    n_blk, blk, heads, me_ref, joint_ref, *refs
):
    grad_refs = refs[:n_blk]
    start_ref, log_ref, out_ref, joint, grads, bias, totals = refs[n_blk:]
    me = me_ref[0]
    group = heads * HDIM
    for place in range(n_blk):
        rows = pl.ds(pl.multiple_of(lax.bitwise_xor(me, place) * blk, blk), blk)
        joint[rows, :] = joint_ref[place, 0]
        grads[rows, :] = grad_refs[place][0]
    offsets = fill_bias(bias, start_ref, n_blk, blk)
    tasks = [(block, head) for block in reversed(range(n_blk)) for head in range(heads)]

    def products(task):
        block, head = task
        low = head * HDIM
        keys = (block + 1) * blk
        rows = slice(block * blk, keys)
        query = joint[rows, low : low + HDIM] * 0.125
        grad = grads[rows, low : low + HDIM]
        scores = dot(joint[:keys, group + low : group + low + HDIM], query, ((1,), (1,)))
        grad_probs = dot(joint[:keys, 2 * group + low : 2 * group + low + HDIM], grad, ((1,), (1,)))
        zeros = jnp.zeros((blk, HDIM), BF16)
        pair = jnp.concatenate(
            [jnp.concatenate([query, zeros], axis=1), jnp.concatenate([zeros, grad], axis=1)], axis=0
        )
        return scores, grad_probs, pair

    ahead = products(tasks[0])
    grad_queries = []
    for number, (block, head) in enumerate(tasks):
        scores, grad_probs, pair = ahead
        if number + 1 < len(tasks):
            ahead = products(tasks[number + 1])
        keys = (block + 1) * blk
        low = head * HDIM
        scores = scores + bias[offsets[block] : offsets[block] + keys, :]
        probs = jnp.exp(scores - log_ref[0, head : head + 1, block * blk : keys])
        inner = jnp.sum(probs * grad_probs, axis=0, keepdims=True)
        grad_scores = (probs * (grad_probs - inner)).astype(BF16)
        terms = dot(jnp.concatenate([grad_scores, probs.astype(BF16)], axis=1), pair, ((1,), (0,)))
        if block == n_blk - 1:
            totals[head, :keys, :] = terms
        else:
            totals[head, :keys, :] += terms
        key = joint[:keys, group + low : group + low + HDIM]
        grad_queries.append(dot(key, grad_scores, ((0,), (0,))) * 0.125)
        if head == heads - 1:
            out_ref[lax.bitwise_xor(me, block), 0, :, :group] = jnp.concatenate(grad_queries, axis=0).T.astype(BF16)
            grad_queries = []
    for block in range(n_blk):
        rows = slice(block * blk, (block + 1) * blk)
        place = lax.bitwise_xor(me, block)
        sides = [totals[head, rows, :].astype(BF16) for head in range(heads)]
        out_ref[place, 0, :, group:] = jnp.concatenate(
            [side[:, :HDIM] for side in sides] + [side[:, HDIM:] for side in sides], axis=1
        )


def attend_backward(me, joint, grads, start, logs, first):
    n_blk, count, blk, cols = joint.shape
    group = cols // 3
    heads = group // HDIM
    length = n_blk * blk
    return pl.pallas_call(
        functools.partial(backward_kernel, n_blk, blk, heads),
        grid_spec=pltpu.PrefetchScalarGridSpec(
            num_scalar_prefetch=1,
            grid=(count,),
            in_specs=[pl.BlockSpec((n_blk, 1, blk, cols), lambda s, m: (0, s, 0, 0))]
            + [pl.BlockSpec((1, blk, group), lambda s, m: (s + first, 0, 0))] * n_blk
            + [
                pl.BlockSpec((1, 1, length), lambda s, m: (s, 0, 0)),
                pl.BlockSpec((1, heads, length), lambda s, m: (s, 0, 0)),
            ],
            out_specs=pl.BlockSpec((n_blk, 1, blk, cols), lambda s, m: (0, s, 0, 0)),
            scratch_shapes=[
                pltpu.VMEM((length, cols), BF16),
                pltpu.VMEM((length, group), BF16),
                pltpu.VMEM((bias_rows(n_blk, blk), blk), F32),
                pltpu.VMEM((heads, length, 2 * HDIM), F32),
            ],
        ),
        out_shape=jax.ShapeDtypeStruct((n_blk, count, blk, cols), BF16),
        compiler_params=pltpu.CompilerParams(vmem_limit_bytes=VMEM_BYTES),
        cost_estimate=COST,
        name="attend_backward",
    )(me, joint, *grads, start, logs)


def unproject_kernel(n_blk, last, me_ref, grad_ref, normed_ref, params_ref, weight_ref, earlier_ref, earlier_bias_ref, *outs):
    kept_ref, sent_ref, terms_ref, bias_ref = outs
    blk, cols = grad_ref.shape[2:]
    group = cols // 3
    vectors, width = params_ref.shape
    grad = grad_ref[...].reshape(n_blk * blk, cols)
    share = dot(grad, weight_ref[...], ((1,), (1,))).astype(BF16)
    for place in range(n_blk):
        (sent_ref if place % 2 else kept_ref)[place // 2, 0] = share[place * blk : (place + 1) * blk]
    weight_grad = dot(normed_ref[...].reshape(n_blk * blk, width), grad, ((0,), (0,)))
    bias_grad = column_sum(grad.astype(F32))

    @pl.when(pl.program_id(0) == 0)
    def _():
        terms_ref[:, :cols] = weight_grad + earlier_ref[:, :cols]
        terms_ref[:, cols:] = earlier_ref[:, cols:]
        bias_ref[...] = bias_grad + earlier_bias_ref[...]

    @pl.when(pl.program_id(0) > 0)
    def _():
        terms_ref[:, :cols] += weight_grad
        bias_ref[...] += bias_grad

    if not last:
        return

    @pl.when(pl.program_id(0) == pl.num_programs(0) - 1)
    def _():
        weight = weight_ref[...].astype(F32)
        bias = bias_ref[...]
        columns = params_ref[...].T
        shift_sum = jnp.sum(weight * bias, axis=1, keepdims=True)
        gain_sum = jnp.sum(weight * terms_ref[:, :cols], axis=1, keepdims=True)
        gain_sum = (gain_sum - columns[:, 1:2] * shift_sum) / columns[:, 0:1]

        def placed(values):
            return jnp.concatenate([jnp.where(me_ref[0] == j, values, 0.0) for j in range(n_blk)], axis=1)

        table = jnp.concatenate(
            [placed(bias[:, :group]), placed(bias[:, 2 * group :]), jnp.zeros((vectors - 4, width), F32)], axis=0
        ).T
        terms_ref[:, cols:] += jnp.concatenate([gain_sum, shift_sum, table], axis=1)


def unproject(me, grad, normed, params, weight, earlier, bias, last):
    n_blk, count, blk, cols = grad.shape
    width = normed.shape[-1]

    def whole(shape):
        return pl.BlockSpec(shape, lambda s, m: (0, 0))

    def by_seq(parts, size):
        return pl.BlockSpec((parts, 1, blk, size), lambda s, m: (0, s, 0, 0))

    return pl.pallas_call(
        functools.partial(unproject_kernel, n_blk, last),
        grid_spec=pltpu.PrefetchScalarGridSpec(
            num_scalar_prefetch=1,
            grid=(count,),
            in_specs=[by_seq(n_blk, cols), by_seq(n_blk, width)]
            + [whole(params.shape), whole(weight.shape), whole(earlier.shape), whole(bias.shape)],
            out_specs=[by_seq(n_blk // 2, width)] * 2 + [whole(earlier.shape), whole(bias.shape)],
        ),
        out_shape=[jax.ShapeDtypeStruct((n_blk // 2, count, blk, width), BF16)] * 2
        + [jax.ShapeDtypeStruct(earlier.shape, F32), jax.ShapeDtypeStruct(bias.shape, F32)],
        compiler_params=pltpu.CompilerParams(vmem_limit_bytes=VMEM_BYTES),
        cost_estimate=COST,
        name="unproject",
    )(me, grad, normed, params, weight, earlier, bias)


def weigh_kernel(n_ctx, last, me_ref, act_ref, pre_ref, normed_ref, up_ref, branch_ref, *refs):
    mixed_refs, outs, total = refs[:n_ctx], refs[n_ctx : n_ctx + 6], refs[-1]
    step = pl.program_id(0)
    me = me_ref[0]
    core = lax.bitwise_and(me, 1)
    per_group = total.shape[0] // n_ctx

    @pl.when((step < last) | (step == 2 * last))
    def _():
        total[...] = dot(act_ref[...], up_ref[...], ((1,), (0,))).reshape(total.shape)

    @pl.when(((step >= last) & (step < 2 * last)) | (step == 2 * last + 1))
    def _():
        total[...] = dot(normed_ref[...], pre_ref[...], ((1,), (0,))).reshape(total.shape)

    @pl.when(step == 2 * last + 2)
    def _():
        for place in range(n_ctx):
            value = dot(mixed_refs[place][...], branch_ref[...], ((0,), (0,)))
            total[pl.ds(lax.bitwise_xor(me, place) * per_group, per_group)] = value.reshape(
                (per_group,) + total.shape[1:]
            )

    bounds = (0, last, 2 * last, 2 * last + 3)
    for number in range(3):
        keep_ref, send_ref = outs[2 * number : 2 * number + 2]

        @pl.when((step >= bounds[number]) & (step < bounds[number + 1]))
        def _():
            keep_ref[0] = total[:, core]
            send_ref[0] = total[:, 1 - core].astype(BF16)


def weigh(me, activated, grad_pre, normed, upstream, branch, mixed, part):
    hidden, rows = activated.shape
    width = normed.shape[0]
    n_ctx = len(mixed)
    last = hidden // width - 1
    pairs = width // (2 * part)

    def whole(shape):
        return pl.BlockSpec(shape, lambda s, m: (0, 0), pipeline_mode=pl.Buffered(1))

    def units(count, begin):
        return pl.BlockSpec(
            (1, pairs, part, width), lambda s, m: (jnp.clip(s - begin, 0, count - 1), 0, 0, 0)
        )

    counts = ((last, 0), (last, last), (3, 2 * last))
    return pl.pallas_call(
        functools.partial(weigh_kernel, n_ctx, last),
        grid_spec=pltpu.PrefetchScalarGridSpec(
            num_scalar_prefetch=1,
            grid=(2 * last + 3,),
            in_specs=[
                pl.BlockSpec((width, rows), lambda s, m: (jnp.where(s < 2 * last, jnp.minimum(s, last - 1), last), 0)),
                pl.BlockSpec((rows, width), lambda s, m: (0, jnp.clip(s - last, 0, last))),
                whole(normed.shape),
                whole(upstream.shape),
                whole(branch.shape),
            ]
            + [whole(item.shape) for item in mixed],
            out_specs=[units(*item) for item in counts for _ in range(2)],
            scratch_shapes=[pltpu.VMEM((pairs, 2, part, width), F32)],
        ),
        out_shape=[
            jax.ShapeDtypeStruct((count, pairs, part, width), dtype) for count, _ in counts for dtype in (F32, BF16)
        ],
        compiler_params=pltpu.CompilerParams(vmem_limit_bytes=VMEM_BYTES),
        cost_estimate=COST,
        name="weigh",
    )(me, activated, grad_pre, normed, upstream, branch, *mixed)


def update_kernel(n_dev, *refs):
    sums = [refs[c][...] + refs[3 + c][...].astype(F32) for c in range(3)]
    states, outs = refs[6:15], refs[15:]
    spans = sums[0].shape[0] + 1
    part = sums[0].shape[1]
    shrink = jnp.concatenate([sums[0][i] for i in range(spans - 1)] + [sums[2][0]], axis=0)
    units = [sums[1][i] for i in range(spans - 1)] + [sums[2][1]]
    expand = jnp.concatenate(
        [units[span][:, place * part : (place + 1) * part] for place in range(n_dev) for span in range(spans)], axis=1
    )
    for number, gradient in enumerate((sums[2][2], expand, shrink)):
        weight, first, second = [ref[...] for ref in states[3 * number : 3 * number + 3]]
        results = adam_step(weight, gradient, first, second, RATE_MATRIX, WEIGHT_DECAY)
        for out, result in zip(outs[3 * number : 3 * number + 3], results):
            out[...] = result


def update(keeps, gots, states, n_dev):
    vmem = pl.BlockSpec(memory_space=pltpu.VMEM)
    return pl.pallas_call(
        functools.partial(update_kernel, n_dev),
        in_specs=[vmem] * 15,
        out_specs=[vmem] * 9,
        out_shape=[jax.ShapeDtypeStruct(item.shape, F32) for item in states],
        compiler_params=pltpu.CompilerParams(vmem_limit_bytes=VMEM_BYTES),
        name="update",
    )(*keeps, *gots, *states)


def finish_kernel(n_ctx, me_ref, *refs):
    pieces, refs = refs[:n_ctx], refs[n_ctx:]
    states, outs, held = refs[:6], refs[6:12], refs[12]
    for place in range(n_ctx):
        held[place] = pieces[place][...].astype(F32)
    vectors = states[3].shape[0]
    cols = held.shape[-1] - vectors
    group = cols // 3
    groups = [held[lax.bitwise_xor(me_ref[0], j)] for j in range(n_ctx)]
    gradient = jnp.concatenate(
        [item[:, third * group : (third + 1) * group] for third in range(3) for item in groups], axis=1
    )
    small = sum(item[:, cols:] for item in groups).T
    results = adam_step(states[0][...], gradient, states[1][...], states[2][...], RATE_MATRIX, WEIGHT_DECAY)
    results += adam_step(states[3][...], small, states[4][...], states[5][...], RATE_VECTOR, 0.0)
    for out, result in zip(outs, results):
        out[...] = result


def finish(me, pieces, states):
    n_ctx = len(pieces)
    return pl.pallas_call(
        functools.partial(finish_kernel, n_ctx),
        in_specs=[pl.BlockSpec(memory_space=pltpu.SMEM)] + [pl.BlockSpec(memory_space=pltpu.VMEM)] * (n_ctx + 6),
        out_specs=[pl.BlockSpec(memory_space=pltpu.VMEM)] * 6,
        out_shape=[jax.ShapeDtypeStruct(item.shape, F32) for item in states],
        scratch_shapes=[pltpu.VMEM((n_ctx,) + pieces[0].shape, F32)],
        compiler_params=pltpu.CompilerParams(vmem_limit_bytes=VMEM_BYTES),
        name="finish",
    )(me, *pieces, *states)


def build(sizes):
    n_dp, n_ctx = sizes["dp"], sizes["ctx"]
    dp_bits = [bit for bit in range(16) if (1 << bit) < n_dp]
    ctx_bits = [bit for bit in range(16) if (1 << bit) < n_ctx]

    def swap(value, axis, mask):
        return lax.ppermute(value, axis, [(place, place ^ mask) for place in range(sizes[axis])])

    def reorder(items, me):
        stacked = jnp.stack(items)
        return [
            lax.dynamic_index_in_dim(stacked, lax.bitwise_xor(me, j), 0, keepdims=False) for j in range(len(items))
        ]

    def per_device(
        tokens_in,
        segments,
        cotangent,
        joint_weight,
        output_weight,
        expand_weight,
        shrink_weight,
        momentum_joint,
        momentum_output,
        momentum_expand,
        momentum_shrink,
        variance_joint,
        variance_output,
        variance_expand,
        variance_shrink,
        small_params,
        momentum_small,
        variance_small,
    ):
        seqs, stretch, width = tokens_in.shape
        hidden = expand_weight.shape[1]
        spans = hidden // width
        part = joint_weight.shape[0]
        group = width // n_ctx
        cols = 3 * group
        rows = seqs * stretch
        n_dev = n_dp * n_ctx
        n_bits = len(dp_bits)
        vectors = small_params.shape[0]
        me_dp, me = lax.axis_index("dp"), lax.axis_index("ctx")
        spots = {"dp": me_dp, "ctx": me}
        me_arr = me.astype(jnp.int32).reshape(1)

        joint_cast, small_cast = lax.optimization_barrier((joint_weight.astype(BF16), small_params.astype(BF16)))
        output_cast, expand_cast, shrink_cast = lax.optimization_barrier(
            (output_weight.astype(BF16), expand_weight.astype(BF16), shrink_weight.astype(BF16))
        )

        seg_blocks = {0: segments}
        for bit in reversed(ctx_bits):
            seg_blocks.update({k ^ (1 << bit): swap(value, "ctx", 1 << bit) for k, value in list(seg_blocks.items())})
        segs = jnp.concatenate(reorder([seg_blocks[k] for k in range(n_ctx)], me), axis=1)
        start = jnp.zeros_like(segs)
        for number in range(1, DOCS):
            bound = jnp.sum((segs < number).astype(jnp.int32), axis=1, keepdims=True)
            start = jnp.where(segs >= number, bound, start)
        start = start[:, None, :]

        small_cols = small_cast.T
        joint_cols = joint_cast.reshape(part, 3, n_ctx, group)

        def columns_for(k):
            picked = lax.dynamic_index_in_dim(joint_cols, lax.bitwise_xor(me, k), 2, keepdims=False)
            return jnp.concatenate([picked.reshape(part, cols), small_cols], axis=1)

        pieces = [columns_for(0)] + [swap(columns_for(k), "ctx", k) for k in range(1, n_ctx)]

        expand_wide = expand_cast.reshape(part, n_dev, spans, part).transpose(0, 2, 1, 3).reshape(part, hidden)
        shrink_wide = shrink_cast.reshape(spans, part, width).transpose(1, 0, 2).reshape(part, hidden)
        sides = [
            jnp.concatenate([item[:, h * size // 2 : (h + 1) * size // 2] for item, size in wide], axis=1)
            for wide in [((output_cast, width), (expand_wide, hidden), (shrink_wide, hidden))]
            for h in range(2)
        ]
        pair = me & 1
        rest_own = jnp.where(pair == 1, sides[1], sides[0])
        rest_got = swap(jnp.where(pair == 1, sides[0], sides[1]), "ctx", 1)
        rest = jnp.where(
            pair == 1,
            jnp.concatenate([rest_got, rest_own], axis=0),
            jnp.concatenate([rest_own, rest_got], axis=0),
        )
        rest = lax.all_gather(rest, ("dp", "ctx"), axis=0, tiled=True, axis_index_groups=[
            [d * n_ctx + c * 2 + p for d in range(n_dp) for c in range(n_ctx // 2)] for p in range(2)
        ])

        half = max(seqs // 2, 1)
        firsts = list(range(0, seqs, half))
        near, far_bits = 1, [bit for bit in reversed(ctx_bits) if bit]

        def fetch_far(blocks):
            for bit in far_bits:
                blocks.update({k ^ (1 << bit): swap(value, "ctx", 1 << bit) for k, value in list(blocks.items())})

        names = range(0, n_ctx, 2)
        ahead = {0: tokens_in[:1]}
        fetch_far(ahead)
        pieces, start, later, held = lax.optimization_barrier(
            (pieces, start, [tokens_in[1:half], tokens_in[half:]], [ahead[k] for k in names])
        )
        others = [{0: later[0]}, {0: later[1]}]
        for blocks in others:
            if blocks[0].shape[0]:
                fetch_far(blocks)
        first_half = {k: item for k, item in zip(names, held)}
        if half > 1:
            first_half = {k: jnp.concatenate([first_half[k], others[0][k]], axis=0) for k in names}
        tokens = [first_half, others[1]]
        for blocks, first in zip(tokens, firsts):
            blocks[0] = tokens_in[first : first + half]
        gathered = jnp.stack(reorder(pieces, me))
        for step, bit in enumerate(reversed(dp_bits)):
            other = swap(gathered, "dp", 1 << bit)
            upper = ((me_dp >> bit) & 1) == 1
            gathered = jnp.where(upper, jnp.stack([other, gathered]), jnp.stack([gathered, other]))
            if step == max(n_bits - 2, 0):
                flat = [(number, k) for number, blocks in enumerate(tokens) for k in sorted(blocks) if k]
                gathered, *held = lax.optimization_barrier((gathered,) + tuple(tokens[n][k] for n, k in flat))
                for (number, k), value in zip(flat, held):
                    tokens[number][k] = value
        for blocks in tokens:
            blocks.update({k ^ near: swap(value, "ctx", near) for k, value in list(blocks.items())})
        tokens = [[blocks[k] for k in range(n_ctx)] for blocks in tokens]

        gathered = gathered.transpose(tuple(reversed(range(n_bits))) + tuple(range(n_bits, n_bits + 3)))
        gathered = gathered.reshape(width, cols + vectors)
        joint_lo = gathered[:, :cols]
        params = gathered[:, cols:].T.astype(F32)
        mine_bias = lax.dynamic_slice(params[2:4], (0, me * group), (2, group))
        joint_bias = jnp.concatenate([mine_bias[:1], jnp.zeros((1, group), F32), mine_bias[1:]], axis=1)
        bias_hidden = params[7 : 7 + spans].reshape(n_dev, spans, part).transpose(1, 0, 2).reshape(spans, width)
        params = jnp.concatenate([params[:7], bias_hidden, params[7 + spans :]], axis=0)

        joints, normeds, logs, mixed, waiting = [], [], [], [], None
        starts = [start[first : first + half] for first in firsts]
        for number in range(len(firsts)):
            joint, normed = project(tokens[number], params, joint_lo, joint_bias)
            normeds.append(normed)
            if waiting is not None:
                waiting, joint = lax.optimization_barrier((waiting, joint))
                waiting = [waiting[0]] + [swap(waiting[k], "ctx", k) for k in range(1, n_ctx)]
            *attended, log = attend_forward(me_arr, joint, starts[number])
            if waiting is not None:
                waiting, attended = lax.optimization_barrier((waiting, attended))
                mixed.append(waiting)
            waiting = attended
            joints.append(joint)
            logs.append(log)
        waiting, rest = lax.optimization_barrier((waiting, rest))
        rest_other = swap(rest, "ctx", 1)
        mixed.append([waiting[0]] + [swap(waiting[k], "ctx", k) for k in range(1, n_ctx)])
        mixed = [jnp.concatenate(items, axis=0) for items in zip(*mixed)]
        block_output, grad_resid, branch, normed_two, activated, grad_pre, *grad_mixed, sums = layer(
            me_arr, tokens_in, cotangent, mixed, rest, rest_other, params
        )
        grads = [grad_mixed[0]] + [swap(grad_mixed[k], "ctx", k) for k in range(1, n_ctx)]

        activated, grad_pre, normed_two, branch, grads[1] = lax.optimization_barrier(
            (activated, grad_pre, normed_two, branch, grads[1])
        )
        branch = branch.reshape(rows, width)
        upstream = cotangent.reshape(rows, width)
        grad_pre = grad_pre.reshape(rows, hidden)
        labels = [("dp", bit) for bit in reversed(dp_bits)] + [("ctx", bit) for bit in reversed(ctx_bits)]
        bit_dims = (2,) * len(labels)
        core, far = [("ctx", ctx_bits[0])], [("ctx", bit) for bit in ctx_bits[1:]]
        low, high = [("dp", dp_bits[0])], [("dp", bit) for bit in dp_bits[1:]]
        mixed = [item.reshape(rows, group) for item in mixed]
        orders = [core + low + high + far, core + far + low + high, core + high[:1] + far + low + high[1:]]
        if part % 8 == 0:
            halves = weigh(me_arr, activated, grad_pre, normed_two, upstream, branch, mixed, part)
            halves, grads = lax.optimization_barrier((halves, grads))
            names = ["unit"] + [label for label in labels if label not in core]
            halves = [item.reshape(item.shape[:1] + bit_dims[1:] + (part, width)) for item in halves]
            chains = [[halves[2 * c], halves[2 * c + 1], names, orders[c]] for c in range(3)]
        else:
            grad_shrink = dot(activated, upstream, ((1,), (0,))).reshape(spans, width, width)
            grad_expand = dot(normed_two, grad_pre, ((1,), (0,))).reshape(width, spans, width).transpose(1, 0, 2)
            grad_output = jnp.concatenate(reorder([dot(item, branch, ((0,), (0,))) for item in mixed], me), axis=0)
            units = [
                grad_shrink[:-1],
                grad_expand[:-1],
                jnp.stack([grad_shrink[-1], grad_expand[-1], grad_output]),
            ]
            chains = [
                [item.reshape(item.shape[:1] + bit_dims + (part, width)), None, ["unit"] + labels, order]
                for item, order in zip(units, orders)
            ]

        def split(chain):
            value, _, names, order = chain
            axis, bit = order[0]
            pos = names.index((axis, bit))
            mine = (spots[axis] >> bit) & 1
            chain[0] = lax.dynamic_index_in_dim(value, mine, pos, keepdims=False)
            chain[1] = lax.dynamic_index_in_dim(value, 1 - mine, pos, keepdims=False).astype(BF16)

        def fetch(chain):
            axis, bit = chain[3][0]
            return swap(chain[1], axis, 1 << bit)

        def merge(chain, got):
            _, _, names, order = chain
            chain[0] = chain[0] + got.astype(F32)
            chain[2] = [name for name in names if name != order[0]]
            chain[3] = order[1:]

        def advance(after, before):
            if len(chains[0][3]) < 2:
                return after, before
            after, keeps, gots = lax.optimization_barrier(
                (after, [chain[0] for chain in chains], [fetch(chain) for chain in chains])
            )
            for chain, keep, got in zip(chains, keeps, gots):
                chain[0] = keep
                merge(chain, got)
                split(chain)
            before, keeps, sends = lax.optimization_barrier(
                (before, [chain[0] for chain in chains], [chain[1] for chain in chains])
            )
            for chain, keep, send in zip(chains, keeps, sends):
                chain[0], chain[1] = keep, send
            return after, before

        if part % 8:
            for chain in chains:
                split(chain)

        sums_hidden = sums[3 : 3 + spans].reshape(spans, n_dev, part).transpose(1, 0, 2).reshape(spans, width)
        table = jnp.concatenate([jnp.zeros((4, width), F32), sums[:3], sums_hidden, sums[3 + spans :]], axis=0)
        terms = jnp.concatenate([jnp.zeros((width, cols), F32), table.T], axis=1)
        pending, shares = None, []
        bias_sums = jnp.zeros((1, cols), F32)
        for number, first in enumerate(firsts):
            _, (source, pending) = advance(terms if number else branch, (joints[number], pending))
            grad_joint = attend_backward(me_arr, source, grads, starts[number], logs[number], first)
            if pending:
                pending[1] = [swap(value, "ctx", 1 << bit) for value, bit in zip(pending[1], ctx_bits[1:])]
            (grad_joint, pending), _ = advance((grad_joint, pending), start)
            if pending:
                shares.append(sum((value.astype(F32) for value in pending[1]), pending[0]))
            kept, sent, terms, bias_sums = unproject(
                me_arr, grad_joint, normeds[number], params, joint_lo, terms, bias_sums, number == len(firsts) - 1
            )
            if number < len(firsts) - 1:
                joined = kept.astype(F32) + swap(sent, "ctx", 1).astype(F32)
                pending = [joined[0], [joined[1 << (bit - 1)].astype(BF16) for bit in ctx_bits[1:]]]

        terms = terms.reshape((2,) * n_bits + (n_ctx, part, cols + vectors))
        chain = [terms, None, [("dp", bit) for bit in reversed(dp_bits)], low + high]
        split(chain)
        got, sent, kept = lax.optimization_barrier((fetch(chain), swap(sent, "ctx", 1), kept))
        merge(chain, got)
        joined = kept.astype(F32) + sent.astype(F32)
        crossing = [swap(joined[1 << (bit - 1)].astype(BF16), "ctx", 1 << bit) for bit in ctx_bits[1:]]
        if n_dp <= 8:
            items = chain[0].reshape(n_dp // 2, n_ctx, part, cols + vectors)
            spot = me_dp >> 1
            total = lax.dynamic_index_in_dim(items, spot, 0, keepdims=False)
            sent = [
                lax.dynamic_index_in_dim(items, lax.bitwise_xor(spot, j), 0, keepdims=False).astype(BF16)
                for j in range(1, n_dp // 2)
            ]
            gots = [swap(item, "dp", 2 * (j + 1)) for j, item in enumerate(sent)]
            total, gots, crossing = lax.optimization_barrier((total, gots, crossing))
            total = sum((item.astype(F32) for item in gots), total)
        else:
            while chain[3]:
                split(chain)
                merge(chain, fetch(chain))
            total = chain[0]
        shares.append(sum((value.astype(F32) for value in crossing), joined[0]))

        def terms_for(k):
            return lax.dynamic_index_in_dim(total, lax.bitwise_xor(me, k), 0, keepdims=False)

        sent = lax.optimization_barrier([terms_for(k).astype(BF16) for k in range(1, n_ctx)])
        arrived = [terms_for(0)] + [swap(item, "ctx", k + 1) for k, item in enumerate(sent)]
        new_joint, first_joint, second_joint, new_small, first_small, second_small = finish(
            me_arr,
            arrived,
            (joint_weight, momentum_joint, variance_joint, small_params, momentum_small, variance_small),
        )

        plain, scale = norm_parts(tokens_in.astype(F32))
        input_grad = grad_resid + norm_back(plain, scale, jnp.concatenate(shares, axis=0), params[0])

        while len(chains[0][3]) > 1:
            for chain in chains:
                merge(chain, fetch(chain))
                split(chain)
        states = (
            (output_weight, momentum_output, variance_output)
            + (expand_weight, momentum_expand, variance_expand)
            + (shrink_weight, momentum_shrink, variance_shrink)
        )
        if part % 8 == 0:
            updated = update([chain[0] for chain in chains], [fetch(chain) for chain in chains], states, n_dev)
        else:
            for chain in chains:
                merge(chain, fetch(chain))
            last_shrink, last_expand, sum_output = chains[2][0]
            sum_shrink = jnp.concatenate([*chains[0][0], last_shrink], axis=0)
            sum_expand = jnp.stack([*chains[1][0], last_expand], axis=1)
            sum_expand = sum_expand.reshape(part, spans, n_dev, part).transpose(0, 2, 1, 3).reshape(part, hidden)
            updated = []
            for number, gradient in enumerate((sum_output, sum_expand, sum_shrink)):
                weight, first, second = states[3 * number : 3 * number + 3]
                updated += adam_step(weight, gradient, first, second, RATE_MATRIX, WEIGHT_DECAY)
        new_output, first_output, second_output = updated[:3]
        new_expand, first_expand, second_expand = updated[3:6]
        new_shrink, first_shrink, second_shrink = updated[6:]
        return (
            block_output,
            input_grad,
            new_joint,
            new_output,
            new_expand,
            new_shrink,
            first_joint,
            first_output,
            first_expand,
            first_shrink,
            second_joint,
            second_output,
            second_expand,
            second_shrink,
            new_small,
            first_small,
            second_small,
        )

    return per_device


def solution(mesh):
    sizes = {axis: mesh.shape[axis] for axis in ("dp", "ctx")}
    tokens = P("dp", "ctx", None)
    matrix = P(("dp", "ctx"), None)
    table = P(None, ("dp", "ctx"))
    return jax.shard_map(
        build(sizes),
        mesh=mesh,
        in_specs=(tokens, P("dp", "ctx"), tokens) + (matrix,) * 12 + (table,) * 3,
        out_specs=(tokens, tokens) + (matrix,) * 12 + (table,) * 3,
        check_vma=False,
    )
```

```python
import functools

import jax
import jax.numpy as jnp
from jax import lax
from jax.experimental import pallas as pl
from jax.experimental.pallas import tpu as pltpu
from jax.sharding import PartitionSpec as P

HDIM = 64
STEP = 10

NORM_EPSILON = 1e-05
MASKED_SCORE = -1000000000.0
BETA_ONE = 0.9
BETA_TWO = 0.999
ADAM_EPSILON = 1e-08
RATE_MATRIX = 0.05
RATE_VECTOR = 0.3
WEIGHT_DECAY = 0.1
DOCS = 4
GELU_ROOT = 0.7978845608028654
GELU_CUBE = 0.044715
VMEM_BYTES = 56 * 1024 * 1024
COST = pl.CostEstimate(flops=20_000_000_000, bytes_accessed=1_000_000, transcendentals=0)

BF16 = jnp.bfloat16
F32 = jnp.float32


def norm_parts(values):
    centre = values - jnp.mean(values, axis=-1, keepdims=True)
    scale = lax.rsqrt(jnp.mean(centre * centre, axis=-1, keepdims=True) + NORM_EPSILON)
    return centre * scale, scale


def norm_back(plain, scale, grad, gain):
    grad_plain = grad * gain
    along = jnp.mean(grad_plain * plain, axis=-1, keepdims=True)
    return (grad_plain - jnp.mean(grad_plain, axis=-1, keepdims=True) - plain * along) * scale


def column_sum(values):
    return jnp.sum(values, axis=0, keepdims=True)


def adam_step(weight, gradient, first, second, rate, decay):
    first_new = BETA_ONE * first + (1.0 - BETA_ONE) * gradient
    second_new = BETA_TWO * second + (1.0 - BETA_TWO) * gradient * gradient
    first_hat = first_new / (1.0 - BETA_ONE**STEP)
    second_hat = second_new / (1.0 - BETA_TWO**STEP)
    updated = weight - rate * (first_hat / (jnp.sqrt(second_hat) + ADAM_EPSILON) + decay * weight)
    return (updated, first_new, second_new)


def dot(left, right, dims):
    return lax.dot_general(left, right, (dims, ((), ())), preferred_element_type=F32)


def project_kernel(n_blk, *refs):
    tokens, (params_ref, weight_ref, bias_ref, joint_ref, normed_ref) = refs[:n_blk], refs[n_blk:]
    for place in range(n_blk):
        plain, _ = norm_parts(tokens[place][0].astype(F32))
        normed = (plain * params_ref[0:1, :] + params_ref[1:2, :]).astype(BF16)
        normed_ref[place, 0] = normed
        joint = dot(normed, weight_ref[...], ((1,), (0,))) + bias_ref[...]
        joint_ref[place, 0] = joint.astype(BF16)


def project(tokens, params, weight, bias):
    n_blk = len(tokens)
    seqs, blk, width = tokens[0].shape
    cols = weight.shape[1]
    return pl.pallas_call(
        functools.partial(project_kernel, n_blk),
        grid=(seqs,),
        in_specs=[pl.BlockSpec((1, blk, width), lambda s: (s, 0, 0))] * n_blk
        + [
            pl.BlockSpec(params.shape, lambda s: (0, 0)),
            pl.BlockSpec(weight.shape, lambda s: (0, 0)),
            pl.BlockSpec(bias.shape, lambda s: (0, 0)),
        ],
        out_specs=[pl.BlockSpec((n_blk, 1, blk, size), lambda s: (0, s, 0, 0)) for size in (cols, width)],
        out_shape=[jax.ShapeDtypeStruct((n_blk, seqs, blk, size), BF16) for size in (cols, width)],
        compiler_params=pltpu.CompilerParams(vmem_limit_bytes=VMEM_BYTES),
        cost_estimate=COST,
        name="project",
    )(*tokens, params, weight, bias)


def fill_bias(bias, start_ref, n_blk, blk):
    offsets = []
    offset = 0
    for block in range(n_blk):
        keys = (block + 1) * blk
        key_pos = lax.broadcasted_iota(jnp.int32, (keys, blk), 0)
        query_pos = lax.broadcasted_iota(jnp.int32, (keys, blk), 1) + block * blk
        first = start_ref[0, :, block * blk : (block + 1) * blk]
        allowed = (key_pos >= first) & (key_pos <= query_pos)
        bias[offset : offset + keys, :] = jnp.where(allowed, 0.0, MASKED_SCORE)
        offsets.append(offset)
        offset += keys
    return offsets


def bias_rows(n_blk, blk):
    return n_blk * (n_blk + 1) // 2 * blk


def forward_kernel(n_blk, blk, heads, me_ref, joint_ref, start_ref, *refs):
    out_refs, (log_ref, joint, bias, out) = refs[:n_blk], refs[n_blk:]
    me = me_ref[0]
    group = heads * HDIM
    for block in range(n_blk):
        joint[block * blk : (block + 1) * blk, :] = joint_ref[lax.bitwise_xor(me, block), 0]
    offsets = fill_bias(bias, start_ref, n_blk, blk)
    tasks = [(block, head) for block in reversed(range(n_blk)) for head in range(heads)]

    def raw_scores(task):
        block, head = task
        low = head * HDIM
        query = joint[block * blk : (block + 1) * blk, low : low + HDIM] * 0.125
        return dot(joint[: (block + 1) * blk, group + low : group + low + HDIM], query, ((1,), (1,)))

    ahead = raw_scores(tasks[0])
    mixed = []
    for number, (block, head) in enumerate(tasks):
        scores = ahead
        if number + 1 < len(tasks):
            ahead = raw_scores(tasks[number + 1])
        keys = (block + 1) * blk
        low = head * HDIM
        scores = scores + bias[offsets[block] : offsets[block] + keys, :]
        top = jnp.max(scores, axis=0, keepdims=True)
        exponent = jnp.exp(scores - top)
        total = jnp.sum(exponent, axis=0, keepdims=True)
        value = joint[:keys, 2 * group + low : 2 * group + low + HDIM]
        mixed.append(dot(value, exponent.astype(BF16), ((0,), (0,))) * (1.0 / total))
        log_ref[0, head : head + 1, block * blk : (block + 1) * blk] = top + jnp.log(total)
        if head == heads - 1:
            out[lax.bitwise_xor(me, block)] = jnp.concatenate(mixed, axis=0).T.astype(BF16)
            mixed = []
    for place in range(n_blk):
        out_refs[place][0] = out[place]


def attend_forward(me, joint, start):
    n_blk, seqs, blk, cols = joint.shape
    group = cols // 3
    heads = group // HDIM
    length = n_blk * blk
    return pl.pallas_call(
        functools.partial(forward_kernel, n_blk, blk, heads),
        grid_spec=pltpu.PrefetchScalarGridSpec(
            num_scalar_prefetch=1,
            grid=(seqs,),
            in_specs=[
                pl.BlockSpec((n_blk, 1, blk, cols), lambda s, m: (0, s, 0, 0)),
                pl.BlockSpec((1, 1, length), lambda s, m: (s, 0, 0)),
            ],
            out_specs=[pl.BlockSpec((1, blk, group), lambda s, m: (s, 0, 0))] * n_blk
            + [pl.BlockSpec((1, heads, length), lambda s, m: (s, 0, 0))],
            scratch_shapes=[
                pltpu.VMEM((length, cols), BF16),
                pltpu.VMEM((bias_rows(n_blk, blk), blk), F32),
                pltpu.VMEM((n_blk, blk, group), BF16),
            ],
        ),
        out_shape=[jax.ShapeDtypeStruct((seqs, blk, group), BF16)] * n_blk
        + [jax.ShapeDtypeStruct((seqs, heads, length), F32)],
        compiler_params=pltpu.CompilerParams(vmem_limit_bytes=VMEM_BYTES),
        cost_estimate=COST,
        name="attend_forward",
    )(me, joint, start)


def layer_kernel(
    n_ctx,
    spans,
    me_ref,
    x_ref,
    y_ref,
    *refs,
):
    mixed_refs = refs[:n_ctx]
    mine_ref, other_ref, params_ref = refs[n_ctx : n_ctx + 3]
    result_ref, resid_ref, branch_ref, normed_ref, act_ref, pre_ref = refs[n_ctx + 3 : n_ctx + 9]
    mix_refs = refs[n_ctx + 9 : 2 * n_ctx + 9]
    sums_ref, rest_ref, sems = refs[2 * n_ctx + 9 :]
    me = me_ref[0]
    width = x_ref.shape[-1]
    group = width // n_ctx
    side = width // 2
    inner = spans // 2

    @pl.when(pl.program_id(0) == 0)
    def _():
        core = lax.bitwise_and(me, 1)
        mine = pltpu.make_async_copy(mine_ref, rest_ref.at[core], sems.at[0])
        other = pltpu.make_async_copy(other_ref, rest_ref.at[1 - core], sems.at[1])
        mine.start()
        other.start()
        mine.wait()
        other.wait()

    def output_rows(place, half):
        first = pl.multiple_of(lax.bitwise_xor(me, place) * group, group)
        return rest_ref[half, pl.ds(first, group), 0:side]

    def param(row):
        return params_ref[row : row + 1, :]

    upstream = y_ref[0]
    mixed = [ref[0] for ref in mixed_refs]
    sides = [
        sum(dot(mixed[place], output_rows(place, half), ((1,), (0,))) for place in range(n_ctx)) for half in range(2)
    ]
    residual = x_ref[0].astype(F32) + (jnp.concatenate(sides, axis=1) + param(4))
    plain, scale = norm_parts(residual)
    normed = (plain * param(5) + param(6)).astype(BF16)
    normed_ref[...] = normed.T
    result = residual + param(7 + spans)
    grad_normed = jnp.zeros(residual.shape, F32)
    sums = []
    for span in range(spans):
        half, low = span // inner, side + width * (span % inner)
        expand = rest_ref[half, :, low : low + width]
        shrink = rest_ref[half, :, low + width * inner : low + width * (inner + 1)]
        pre = dot(normed, expand, ((1,), (0,))) + param(7 + span)
        square = pre * pre
        bent = jnp.tanh(GELU_ROOT * (pre + GELU_CUBE * (square * pre)))
        half = 0.5 * (1.0 + bent)
        activated = (pre * half).astype(BF16)
        slope = half + (0.5 * pre) * (1.0 - bent * bent) * (GELU_ROOT + (3.0 * GELU_ROOT * GELU_CUBE) * square)
        act_ref[width * span : width * (span + 1), :] = activated.T
        result = result + dot(activated, shrink, ((1,), (0,)))
        grad_pre = (dot(upstream, shrink, ((1,), (1,))) * slope).astype(BF16)
        pre_ref[0, :, width * span : width * (span + 1)] = grad_pre
        grad_normed = grad_normed + dot(grad_pre, expand, ((1,), (1,)))
        sums.append(column_sum(grad_pre.astype(F32)))
    result_ref[0] = result.astype(BF16)
    gain_sum = column_sum(grad_normed * plain)
    shift_sum = column_sum(grad_normed)
    upstream_wide = upstream.astype(F32)
    grad_resid = upstream_wide + norm_back(plain, scale, grad_normed, param(5))
    resid_ref[0] = grad_resid
    branch = grad_resid.astype(BF16)
    branch_ref[0] = branch
    for place in range(n_ctx):
        mix = dot(branch[:, :side], output_rows(place, 0), ((1,), (1,)))
        mix_refs[place][0] = (mix + dot(branch[:, side:], output_rows(place, 1), ((1,), (1,)))).astype(BF16)
    table = jnp.concatenate(
        [column_sum(branch.astype(F32)), gain_sum, shift_sum] + sums + [column_sum(upstream_wide)], axis=0
    )

    @pl.when(pl.program_id(0) == 0)
    def _():
        sums_ref[...] = table

    @pl.when(pl.program_id(0) > 0)
    def _():
        sums_ref[...] += table


def layer(me, tokens, cotangent, mixed, mine, other, params):
    n_ctx = len(mixed)
    seqs, blk, width = tokens.shape
    group = width // n_ctx
    spans = (2 * mine.shape[1] // width - 1) // 2
    hidden = spans * width

    def by_seq(*shape):
        return pl.BlockSpec((1,) + shape, lambda s, m: (s,) + (0,) * len(shape))

    def whole(shape):
        return pl.BlockSpec(shape, lambda s, m: (0,) * len(shape), pipeline_mode=pl.Buffered(1))

    return pl.pallas_call(
        functools.partial(layer_kernel, n_ctx, spans),
        grid_spec=pltpu.PrefetchScalarGridSpec(
            num_scalar_prefetch=1,
            grid=(seqs,),
            in_specs=[by_seq(blk, width)] * 2
            + [by_seq(blk, group)] * n_ctx
            + [pl.BlockSpec(memory_space=pl.ANY)] * 2
            + [whole(params.shape)],
            out_specs=[
                by_seq(blk, width),
                by_seq(blk, width),
                by_seq(blk, width),
                pl.BlockSpec((width, blk), lambda s, m: (0, s)),
                pl.BlockSpec((hidden, blk), lambda s, m: (0, s)),
                by_seq(blk, hidden),
            ]
            + [by_seq(blk, group)] * n_ctx
            + [pl.BlockSpec((4 + spans, width), lambda s, m: (0, 0))],
            scratch_shapes=[pltpu.VMEM((2,) + mine.shape, BF16), pltpu.SemaphoreType.DMA((2,))],
        ),
        out_shape=[
            jax.ShapeDtypeStruct((seqs, blk, width), BF16),
            jax.ShapeDtypeStruct((seqs, blk, width), F32),
            jax.ShapeDtypeStruct((seqs, blk, width), BF16),
            jax.ShapeDtypeStruct((width, seqs * blk), BF16),
            jax.ShapeDtypeStruct((hidden, seqs * blk), BF16),
            jax.ShapeDtypeStruct((seqs, blk, hidden), BF16),
        ]
        + [jax.ShapeDtypeStruct((seqs, blk, group), BF16)] * n_ctx
        + [jax.ShapeDtypeStruct((4 + spans, width), F32)],
        compiler_params=pltpu.CompilerParams(vmem_limit_bytes=VMEM_BYTES),
        cost_estimate=COST,
        name="layer",
    )(me, tokens, cotangent, *mixed, mine, other, params)


def backward_kernel(
    n_blk, blk, heads, me_ref, joint_ref, *refs
):
    grad_refs = refs[:n_blk]
    start_ref, log_ref, out_ref, joint, grads, bias, totals = refs[n_blk:]
    me = me_ref[0]
    group = heads * HDIM
    for place in range(n_blk):
        rows = pl.ds(pl.multiple_of(lax.bitwise_xor(me, place) * blk, blk), blk)
        joint[rows, :] = joint_ref[place, 0]
        grads[rows, :] = grad_refs[place][0]
    offsets = fill_bias(bias, start_ref, n_blk, blk)
    tasks = [(block, head) for block in reversed(range(n_blk)) for head in range(heads)]

    def products(task):
        block, head = task
        low = head * HDIM
        keys = (block + 1) * blk
        rows = slice(block * blk, keys)
        query = joint[rows, low : low + HDIM] * 0.125
        grad = grads[rows, low : low + HDIM]
        scores = dot(joint[:keys, group + low : group + low + HDIM], query, ((1,), (1,)))
        grad_probs = dot(joint[:keys, 2 * group + low : 2 * group + low + HDIM], grad, ((1,), (1,)))
        zeros = jnp.zeros((blk, HDIM), BF16)
        pair = jnp.concatenate(
            [jnp.concatenate([query, zeros], axis=1), jnp.concatenate([zeros, grad], axis=1)], axis=0
        )
        return scores, grad_probs, pair

    ahead = products(tasks[0])
    grad_queries = []
    for number, (block, head) in enumerate(tasks):
        scores, grad_probs, pair = ahead
        if number + 1 < len(tasks):
            ahead = products(tasks[number + 1])
        keys = (block + 1) * blk
        low = head * HDIM
        scores = scores + bias[offsets[block] : offsets[block] + keys, :]
        probs = jnp.exp(scores - log_ref[0, head : head + 1, block * blk : keys])
        inner = jnp.sum(probs * grad_probs, axis=0, keepdims=True)
        grad_scores = (probs * (grad_probs - inner)).astype(BF16)
        terms = dot(jnp.concatenate([grad_scores, probs.astype(BF16)], axis=1), pair, ((1,), (0,)))
        if block == n_blk - 1:
            totals[head, :keys, :] = terms
        else:
            totals[head, :keys, :] += terms
        key = joint[:keys, group + low : group + low + HDIM]
        grad_queries.append(dot(key, grad_scores, ((0,), (0,))) * 0.125)
        if head == heads - 1:
            out_ref[lax.bitwise_xor(me, block), 0, :, :group] = jnp.concatenate(grad_queries, axis=0).T.astype(BF16)
            grad_queries = []
    for block in range(n_blk):
        rows = slice(block * blk, (block + 1) * blk)
        place = lax.bitwise_xor(me, block)
        sides = [totals[head, rows, :].astype(BF16) for head in range(heads)]
        out_ref[place, 0, :, group:] = jnp.concatenate(
            [side[:, :HDIM] for side in sides] + [side[:, HDIM:] for side in sides], axis=1
        )


def attend_backward(me, joint, grads, start, logs, first):
    n_blk, count, blk, cols = joint.shape
    group = cols // 3
    heads = group // HDIM
    length = n_blk * blk
    return pl.pallas_call(
        functools.partial(backward_kernel, n_blk, blk, heads),
        grid_spec=pltpu.PrefetchScalarGridSpec(
            num_scalar_prefetch=1,
            grid=(count,),
            in_specs=[pl.BlockSpec((n_blk, 1, blk, cols), lambda s, m: (0, s, 0, 0))]
            + [pl.BlockSpec((1, blk, group), lambda s, m: (s + first, 0, 0))] * n_blk
            + [
                pl.BlockSpec((1, 1, length), lambda s, m: (s, 0, 0)),
                pl.BlockSpec((1, heads, length), lambda s, m: (s, 0, 0)),
            ],
            out_specs=pl.BlockSpec((n_blk, 1, blk, cols), lambda s, m: (0, s, 0, 0)),
            scratch_shapes=[
                pltpu.VMEM((length, cols), BF16),
                pltpu.VMEM((length, group), BF16),
                pltpu.VMEM((bias_rows(n_blk, blk), blk), F32),
                pltpu.VMEM((heads, length, 2 * HDIM), F32),
            ],
        ),
        out_shape=jax.ShapeDtypeStruct((n_blk, count, blk, cols), BF16),
        compiler_params=pltpu.CompilerParams(vmem_limit_bytes=VMEM_BYTES),
        cost_estimate=COST,
        name="attend_backward",
    )(me, joint, *grads, start, logs)


def collect_kernel(n_blk, first, last, me_ref, grad_ref, normed_ref, params_ref, weight_ref, table_ref, *refs):
    terms_ref, bias_ref = refs[-2:]
    blk, cols = grad_ref.shape[2:]
    group = cols // 3
    vectors, width = params_ref.shape
    grad = grad_ref[...].reshape(n_blk * blk, cols)
    weight_grad = dot(normed_ref[...].reshape(n_blk * blk, width), grad, ((0,), (0,)))
    bias_grad = column_sum(grad.astype(F32))

    @pl.when(pl.program_id(0) == 0)
    def _():
        terms_ref[:, :cols] = weight_grad if first else weight_grad + refs[0][:, :cols]
        bias_ref[...] = bias_grad if first else bias_grad + refs[1][...]

    @pl.when(pl.program_id(0) > 0)
    def _():
        terms_ref[:, :cols] += weight_grad
        bias_ref[...] += bias_grad

    @pl.when(pl.program_id(0) == pl.num_programs(0) - 1)
    def _():
        if not last:
            terms_ref[:, cols:] = jnp.zeros((width, vectors), F32)
            return
        weight = weight_ref[...].astype(F32)
        bias = bias_ref[...]
        columns = params_ref[...].T
        shift_sum = jnp.sum(weight * bias, axis=1, keepdims=True)
        gain_sum = jnp.sum(weight * terms_ref[:, :cols], axis=1, keepdims=True)
        gain_sum = (gain_sum - columns[:, 1:2] * shift_sum) / columns[:, 0:1]

        def placed(values):
            return jnp.concatenate([jnp.where(me_ref[0] == j, values, 0.0) for j in range(n_blk)], axis=1)

        table = jnp.concatenate([placed(bias[:, :group]), placed(bias[:, 2 * group :]), table_ref[...]], axis=0).T
        terms_ref[:, cols:] = jnp.concatenate([gain_sum, shift_sum, table], axis=1)


def collect(me, grad, normed, params, weight, table, earlier, last):
    n_blk, count, blk, cols = grad.shape
    vectors, width = params.shape

    def whole(shape):
        return pl.BlockSpec(shape, lambda s, m: (0, 0))

    def by_seq(size):
        return pl.BlockSpec((n_blk, 1, blk, size), lambda s, m: (0, s, 0, 0))

    shapes = [(width, cols + vectors), (1, cols)]
    return pl.pallas_call(
        functools.partial(collect_kernel, n_blk, not earlier, last),
        grid_spec=pltpu.PrefetchScalarGridSpec(
            num_scalar_prefetch=1,
            grid=(count,),
            in_specs=[by_seq(cols), by_seq(width)]
            + [whole(item.shape) for item in (params, weight, table, *earlier)],
            out_specs=[whole(shape) for shape in shapes],
        ),
        out_shape=[jax.ShapeDtypeStruct(shape, F32) for shape in shapes],
        compiler_params=pltpu.CompilerParams(vmem_limit_bytes=VMEM_BYTES),
        cost_estimate=COST,
        name="collect",
    )(me, grad, normed, params, weight, table, *earlier)


def unproject_kernel(n_blk, grad_ref, weight_ref, kept_ref, sent_ref):
    for place in range(n_blk):
        share = dot(grad_ref[place, 0], weight_ref[...], ((1,), (1,))).astype(BF16)
        (sent_ref if place % 2 else kept_ref)[place // 2, 0] = share


def unproject(grad, weight):
    n_blk, count, blk, cols = grad.shape
    width = weight.shape[0]
    out = pl.BlockSpec((n_blk // 2, 1, blk, width), lambda s: (0, s, 0, 0))
    return pl.pallas_call(
        functools.partial(unproject_kernel, n_blk),
        grid=(count,),
        in_specs=[
            pl.BlockSpec((n_blk, 1, blk, cols), lambda s: (0, s, 0, 0)),
            pl.BlockSpec(weight.shape, lambda s: (0, 0)),
        ],
        out_specs=[out, out],
        out_shape=[jax.ShapeDtypeStruct((n_blk // 2, count, blk, width), BF16)] * 2,
        compiler_params=pltpu.CompilerParams(vmem_limit_bytes=VMEM_BYTES),
        cost_estimate=COST,
        name="unproject",
    )(grad, weight)


def weigh_kernel(n_ctx, last, me_ref, act_ref, pre_ref, normed_ref, up_ref, branch_ref, *refs):
    mixed_refs, outs, total = refs[:n_ctx], refs[n_ctx : n_ctx + 6], refs[-1]
    step = pl.program_id(0)
    me = me_ref[0]
    core = lax.bitwise_and(me, 1)
    per_group = total.shape[0] // n_ctx

    @pl.when((step < last) | (step == 2 * last))
    def _():
        total[...] = dot(act_ref[...], up_ref[...], ((1,), (0,))).reshape(total.shape)

    @pl.when(((step >= last) & (step < 2 * last)) | (step == 2 * last + 1))
    def _():
        total[...] = dot(normed_ref[...], pre_ref[...], ((1,), (0,))).reshape(total.shape)

    @pl.when(step == 2 * last + 2)
    def _():
        for place in range(n_ctx):
            value = dot(mixed_refs[place][...], branch_ref[...], ((0,), (0,)))
            total[pl.ds(lax.bitwise_xor(me, place) * per_group, per_group)] = value.reshape(
                (per_group,) + total.shape[1:]
            )

    bounds = (0, last, 2 * last, 2 * last + 3)
    for number in range(3):
        keep_ref, send_ref = outs[2 * number : 2 * number + 2]

        @pl.when((step >= bounds[number]) & (step < bounds[number + 1]))
        def _():
            keep_ref[0] = total[:, core].astype(BF16)
            send_ref[0] = total[:, 1 - core].astype(BF16)


def weigh(me, activated, grad_pre, normed, upstream, branch, mixed, part):
    hidden, rows = activated.shape
    width = normed.shape[0]
    n_ctx = len(mixed)
    last = hidden // width - 1
    pairs = width // (2 * part)

    def whole(shape):
        return pl.BlockSpec(shape, lambda s, m: (0, 0), pipeline_mode=pl.Buffered(1))

    def units(count, begin):
        return pl.BlockSpec(
            (1, pairs, part, width), lambda s, m: (jnp.clip(s - begin, 0, count - 1), 0, 0, 0)
        )

    counts = ((last, 0), (last, last), (3, 2 * last))
    return pl.pallas_call(
        functools.partial(weigh_kernel, n_ctx, last),
        grid_spec=pltpu.PrefetchScalarGridSpec(
            num_scalar_prefetch=1,
            grid=(2 * last + 3,),
            in_specs=[
                pl.BlockSpec((width, rows), lambda s, m: (jnp.where(s < 2 * last, jnp.minimum(s, last - 1), last), 0)),
                pl.BlockSpec((rows, width), lambda s, m: (0, jnp.clip(s - last, 0, last))),
                whole(normed.shape),
                whole(upstream.shape),
                whole(branch.shape),
            ]
            + [whole(item.shape) for item in mixed],
            out_specs=[units(*item) for item in counts for _ in range(2)],
            scratch_shapes=[pltpu.VMEM((pairs, 2, part, width), F32)],
        ),
        out_shape=[
            jax.ShapeDtypeStruct((count, pairs, part, width), dtype) for count, _ in counts for dtype in (BF16, BF16)
        ],
        compiler_params=pltpu.CompilerParams(vmem_limit_bytes=VMEM_BYTES),
        cost_estimate=COST,
        name="weigh",
    )(me, activated, grad_pre, normed, upstream, branch, *mixed)


def update_kernel(n_dev, *refs):
    sums = [refs[c][...] + refs[3 + c][...].astype(F32) for c in range(3)]
    states, outs = refs[6:15], refs[15:]
    spans = sums[0].shape[0] + 1
    part = sums[0].shape[1]
    shrink = jnp.concatenate([sums[0][i] for i in range(spans - 1)] + [sums[2][0]], axis=0)
    units = [sums[1][i] for i in range(spans - 1)] + [sums[2][1]]
    expand = jnp.concatenate(
        [units[span][:, place * part : (place + 1) * part] for place in range(n_dev) for span in range(spans)], axis=1
    )
    for number, gradient in enumerate((sums[2][2], expand, shrink)):
        weight, first, second = [ref[...] for ref in states[3 * number : 3 * number + 3]]
        results = adam_step(weight, gradient, first, second, RATE_MATRIX, WEIGHT_DECAY)
        for out, result in zip(outs[3 * number : 3 * number + 3], results):
            out[...] = result


def update(keeps, gots, states, n_dev):
    vmem = pl.BlockSpec(memory_space=pltpu.VMEM)
    return pl.pallas_call(
        functools.partial(update_kernel, n_dev),
        in_specs=[vmem] * 15,
        out_specs=[vmem] * 9,
        out_shape=[jax.ShapeDtypeStruct(item.shape, F32) for item in states],
        compiler_params=pltpu.CompilerParams(vmem_limit_bytes=VMEM_BYTES),
        name="update",
    )(*keeps, *gots, *states)


def finish_kernel(n_ctx, me_ref, *refs):
    pieces, refs = refs[:n_ctx], refs[n_ctx:]
    states, outs, held = refs[:6], refs[6:12], refs[12]
    for place in range(n_ctx):
        held[place] = pieces[place][...].astype(F32)
    vectors = states[3].shape[0]
    cols = held.shape[-1] - vectors
    group = cols // 3
    groups = [held[lax.bitwise_xor(me_ref[0], j)] for j in range(n_ctx)]
    gradient = jnp.concatenate(
        [item[:, third * group : (third + 1) * group] for third in range(3) for item in groups], axis=1
    )
    small = sum(item[:, cols:] for item in groups).T
    results = adam_step(states[0][...], gradient, states[1][...], states[2][...], RATE_MATRIX, WEIGHT_DECAY)
    results += adam_step(states[3][...], small, states[4][...], states[5][...], RATE_VECTOR, 0.0)
    for out, result in zip(outs, results):
        out[...] = result


def finish(me, pieces, states):
    n_ctx = len(pieces)
    return pl.pallas_call(
        functools.partial(finish_kernel, n_ctx),
        in_specs=[pl.BlockSpec(memory_space=pltpu.SMEM)] + [pl.BlockSpec(memory_space=pltpu.VMEM)] * (n_ctx + 6),
        out_specs=[pl.BlockSpec(memory_space=pltpu.VMEM)] * 6,
        out_shape=[jax.ShapeDtypeStruct(item.shape, F32) for item in states],
        scratch_shapes=[pltpu.VMEM((n_ctx,) + pieces[0].shape, F32)],
        compiler_params=pltpu.CompilerParams(vmem_limit_bytes=VMEM_BYTES),
        name="finish",
    )(me, *pieces, *states)


def build(sizes):
    n_dp, n_ctx = sizes["dp"], sizes["ctx"]
    dp_bits = [bit for bit in range(16) if (1 << bit) < n_dp]
    ctx_bits = [bit for bit in range(16) if (1 << bit) < n_ctx]

    def swap(value, axis, mask):
        return lax.ppermute(value, axis, [(place, place ^ mask) for place in range(sizes[axis])])

    def reorder(items, me):
        stacked = jnp.stack(items)
        return [
            lax.dynamic_index_in_dim(stacked, lax.bitwise_xor(me, j), 0, keepdims=False) for j in range(len(items))
        ]

    def per_device(
        tokens_in,
        segments,
        cotangent,
        joint_weight,
        output_weight,
        expand_weight,
        shrink_weight,
        momentum_joint,
        momentum_output,
        momentum_expand,
        momentum_shrink,
        variance_joint,
        variance_output,
        variance_expand,
        variance_shrink,
        small_params,
        momentum_small,
        variance_small,
    ):
        seqs, stretch, width = tokens_in.shape
        hidden = expand_weight.shape[1]
        spans = hidden // width
        part = joint_weight.shape[0]
        group = width // n_ctx
        cols = 3 * group
        rows = seqs * stretch
        n_dev = n_dp * n_ctx
        n_bits = len(dp_bits)
        vectors = small_params.shape[0]
        me_dp, me = lax.axis_index("dp"), lax.axis_index("ctx")
        spots = {"dp": me_dp, "ctx": me}
        me_arr = me.astype(jnp.int32).reshape(1)

        joint_cast, small_cast = lax.optimization_barrier((joint_weight.astype(BF16), small_params.astype(BF16)))
        output_cast, expand_cast, shrink_cast = lax.optimization_barrier(
            (output_weight.astype(BF16), expand_weight.astype(BF16), shrink_weight.astype(BF16))
        )

        seg_blocks = {0: segments}
        for bit in reversed(ctx_bits):
            seg_blocks.update({k ^ (1 << bit): swap(value, "ctx", 1 << bit) for k, value in list(seg_blocks.items())})
        segs = jnp.concatenate(reorder([seg_blocks[k] for k in range(n_ctx)], me), axis=1)
        start = jnp.zeros_like(segs)
        for number in range(1, DOCS):
            bound = jnp.sum((segs < number).astype(jnp.int32), axis=1, keepdims=True)
            start = jnp.where(segs >= number, bound, start)
        start = start[:, None, :]

        small_cols = small_cast.T
        joint_cols = joint_cast.reshape(part, 3, n_ctx, group)

        def columns_for(k):
            picked = lax.dynamic_index_in_dim(joint_cols, lax.bitwise_xor(me, k), 2, keepdims=False)
            return jnp.concatenate([picked.reshape(part, cols), small_cols], axis=1)

        pieces = [columns_for(0)] + [swap(columns_for(k), "ctx", k) for k in range(1, n_ctx)]

        expand_wide = expand_cast.reshape(part, n_dev, spans, part).transpose(0, 2, 1, 3).reshape(part, hidden)
        shrink_wide = shrink_cast.reshape(spans, part, width).transpose(1, 0, 2).reshape(part, hidden)
        sides = [
            jnp.concatenate([item[:, h * size // 2 : (h + 1) * size // 2] for item, size in wide], axis=1)
            for wide in [((output_cast, width), (expand_wide, hidden), (shrink_wide, hidden))]
            for h in range(2)
        ]
        pair = me & 1
        rest_own = jnp.where(pair == 1, sides[1], sides[0])
        rest_got = swap(jnp.where(pair == 1, sides[0], sides[1]), "ctx", 1)
        rest = jnp.where(
            pair == 1,
            jnp.concatenate([rest_got, rest_own], axis=0),
            jnp.concatenate([rest_own, rest_got], axis=0),
        )
        rest = lax.all_gather(rest, ("dp", "ctx"), axis=0, tiled=True, axis_index_groups=[
            [d * n_ctx + c * 2 + p for d in range(n_dp) for c in range(n_ctx // 2)] for p in range(2)
        ])

        half = max(seqs // 2, 1)
        firsts = list(range(0, seqs, half))
        near, far_bits = 1, [bit for bit in reversed(ctx_bits) if bit]

        def fetch_far(blocks):
            for bit in far_bits:
                blocks.update({k ^ (1 << bit): swap(value, "ctx", 1 << bit) for k, value in list(blocks.items())})

        names = range(0, n_ctx, 2)
        ahead = {0: tokens_in[:1]}
        fetch_far(ahead)
        pieces, start, later, held = lax.optimization_barrier(
            (pieces, start, [tokens_in[1:half], tokens_in[half:]], [ahead[k] for k in names])
        )
        others = [{0: later[0]}, {0: later[1]}]
        for blocks in others:
            if blocks[0].shape[0]:
                fetch_far(blocks)
        first_half = {k: item for k, item in zip(names, held)}
        if half > 1:
            first_half = {k: jnp.concatenate([first_half[k], others[0][k]], axis=0) for k in names}
        tokens = [first_half, others[1]]
        for blocks, first in zip(tokens, firsts):
            blocks[0] = tokens_in[first : first + half]
        gathered = jnp.stack(reorder(pieces, me))
        for step, bit in enumerate(reversed(dp_bits)):
            other = swap(gathered, "dp", 1 << bit)
            upper = ((me_dp >> bit) & 1) == 1
            gathered = jnp.where(upper, jnp.stack([other, gathered]), jnp.stack([gathered, other]))
            if step == max(n_bits - 2, 0):
                flat = [(number, k) for number, blocks in enumerate(tokens) for k in sorted(blocks) if k]
                gathered, *held = lax.optimization_barrier((gathered,) + tuple(tokens[n][k] for n, k in flat))
                for (number, k), value in zip(flat, held):
                    tokens[number][k] = value
        for blocks in tokens:
            blocks.update({k ^ near: swap(value, "ctx", near) for k, value in list(blocks.items())})
        tokens = [[blocks[k] for k in range(n_ctx)] for blocks in tokens]

        gathered = gathered.transpose(tuple(reversed(range(n_bits))) + tuple(range(n_bits, n_bits + 3)))
        gathered = gathered.reshape(width, cols + vectors)
        joint_lo = gathered[:, :cols]
        params = gathered[:, cols:].T.astype(F32)
        mine_bias = lax.dynamic_slice(params[2:4], (0, me * group), (2, group))
        joint_bias = jnp.concatenate([mine_bias[:1], jnp.zeros((1, group), F32), mine_bias[1:]], axis=1)
        bias_hidden = params[7 : 7 + spans].reshape(n_dev, spans, part).transpose(1, 0, 2).reshape(spans, width)
        params = jnp.concatenate([params[:7], bias_hidden, params[7 + spans :]], axis=0)

        joints, normeds, logs, mixed, waiting = [], [], [], [], None
        starts = [start[first : first + half] for first in firsts]
        for number in range(len(firsts)):
            joint, normed = project(tokens[number], params, joint_lo, joint_bias)
            normeds.append(normed)
            if waiting is not None:
                waiting, joint = lax.optimization_barrier((waiting, joint))
                waiting = [waiting[0]] + [swap(waiting[k], "ctx", k) for k in range(1, n_ctx)]
            *attended, log = attend_forward(me_arr, joint, starts[number])
            if waiting is not None:
                waiting, attended = lax.optimization_barrier((waiting, attended))
                mixed.append(waiting)
            waiting = attended
            joints.append(joint)
            logs.append(log)
        waiting, rest = lax.optimization_barrier((waiting, rest))
        rest_other = swap(rest, "ctx", 1)
        mixed.append([waiting[0]] + [swap(waiting[k], "ctx", k) for k in range(1, n_ctx)])
        mixed = [jnp.concatenate(items, axis=0) for items in zip(*mixed)]
        block_output, grad_resid, branch, normed_two, activated, grad_pre, *grad_mixed, sums = layer(
            me_arr, tokens_in, cotangent, mixed, rest, rest_other, params
        )
        grads = [grad_mixed[0]] + [swap(grad_mixed[k], "ctx", k) for k in range(1, n_ctx)]

        activated, grad_pre, normed_two, branch, grads[1] = lax.optimization_barrier(
            (activated, grad_pre, normed_two, branch, grads[1])
        )
        branch = branch.reshape(rows, width)
        upstream = cotangent.reshape(rows, width)
        grad_pre = grad_pre.reshape(rows, hidden)
        labels = [("dp", bit) for bit in reversed(dp_bits)] + [("ctx", bit) for bit in reversed(ctx_bits)]
        bit_dims = (2,) * len(labels)
        core, far = [("ctx", ctx_bits[0])], [("ctx", bit) for bit in ctx_bits[1:]]
        low, high = [("dp", dp_bits[0])], [("dp", bit) for bit in dp_bits[1:]]
        mixed = [item.reshape(rows, group) for item in mixed]
        orders = [core + low + high + far, core + far + low + high, core + high[:1] + far + low + high[1:]]
        if part % 8 == 0:
            halves = weigh(me_arr, activated, grad_pre, normed_two, upstream, branch, mixed, part)
            halves, grads = lax.optimization_barrier((halves, grads))
            names = ["unit"] + [label for label in labels if label not in core]
            halves = [item.reshape(item.shape[:1] + bit_dims[1:] + (part, width)) for item in halves]
            chains = [[halves[2 * c], halves[2 * c + 1], names, orders[c]] for c in range(3)]
        else:
            grad_shrink = dot(activated, upstream, ((1,), (0,))).reshape(spans, width, width)
            grad_expand = dot(normed_two, grad_pre, ((1,), (0,))).reshape(width, spans, width).transpose(1, 0, 2)
            grad_output = jnp.concatenate(reorder([dot(item, branch, ((0,), (0,))) for item in mixed], me), axis=0)
            units = [
                grad_shrink[:-1],
                grad_expand[:-1],
                jnp.stack([grad_shrink[-1], grad_expand[-1], grad_output]),
            ]
            chains = [
                [item.reshape(item.shape[:1] + bit_dims + (part, width)), None, ["unit"] + labels, order]
                for item, order in zip(units, orders)
            ]

        def split(chain):
            value, _, names, order = chain
            axis, bit = order[0]
            pos = names.index((axis, bit))
            mine = (spots[axis] >> bit) & 1
            chain[0] = lax.dynamic_index_in_dim(value, mine, pos, keepdims=False)
            chain[1] = lax.dynamic_index_in_dim(value, 1 - mine, pos, keepdims=False).astype(BF16)

        def fetch(chain):
            axis, bit = chain[3][0]
            return swap(chain[1], axis, 1 << bit)

        def merge(chain, got):
            _, _, names, order = chain
            chain[0] = chain[0].astype(F32) + got.astype(F32)
            chain[2] = [name for name in names if name != order[0]]
            chain[3] = order[1:]

        def advance(after, before):
            if len(chains[0][3]) < 2:
                return after, before
            after, keeps, gots = lax.optimization_barrier(
                (after, [chain[0] for chain in chains], [fetch(chain) for chain in chains])
            )
            for chain, keep, got in zip(chains, keeps, gots):
                chain[0] = keep
                merge(chain, got)
                split(chain)
            before, keeps, sends = lax.optimization_barrier(
                (before, [chain[0] for chain in chains], [chain[1] for chain in chains])
            )
            for chain, keep, send in zip(chains, keeps, sends):
                chain[0], chain[1] = keep, send
            return after, before

        if part % 8:
            for chain in chains:
                split(chain)

        sums_hidden = sums[3 : 3 + spans].reshape(spans, n_dev, part).transpose(1, 0, 2).reshape(spans, width)
        table = jnp.concatenate([sums[:3], sums_hidden, sums[3 + spans :]], axis=0)
        pending, shares = None, []
        earlier, after = (), branch
        for number, first in enumerate(firsts):
            _, (source, pending) = advance(after, (joints[number], pending))
            grad_joint = attend_backward(me_arr, source, grads, starts[number], logs[number], first)
            if pending:
                pending[1] = [swap(value, "ctx", 1 << bit) for value, bit in zip(pending[1], ctx_bits[1:])]
            (grad_joint, pending), _ = advance((grad_joint, pending), start)
            if pending:
                shares.append(sum((value.astype(F32) for value in pending[1]), pending[0]))
            earlier = collect(
                me_arr, grad_joint, normeds[number], params, joint_lo, table, earlier, number == len(firsts) - 1
            )
            if number == len(firsts) - 1:
                grad_joint, earlier = lax.optimization_barrier((grad_joint, earlier))
            kept, sent = unproject(grad_joint, joint_lo)
            after = (earlier, kept)
            if number < len(firsts) - 1:
                joined = kept.astype(F32) + swap(sent, "ctx", 1).astype(F32)
                pending = [joined[0], [joined[1 << (bit - 1)].astype(BF16) for bit in ctx_bits[1:]]]

        terms = earlier[0].reshape((2,) * n_bits + (n_ctx, part, cols + vectors))
        chain = [terms, None, [("dp", bit) for bit in reversed(dp_bits)], low + high]
        split(chain)
        got, sent, kept = lax.optimization_barrier((fetch(chain), swap(sent, "ctx", 1), kept))
        merge(chain, got)
        joined = kept.astype(F32) + sent.astype(F32)
        crossing = [swap(joined[1 << (bit - 1)].astype(BF16), "ctx", 1 << bit) for bit in ctx_bits[1:]]
        while len(chains[0][3]) > 1:
            for item in chains:
                merge(item, fetch(item))
                split(item)
        chain[0], keeps = lax.optimization_barrier((chain[0], [item[0] for item in chains]))
        for item, keep in zip(chains, keeps):
            item[0] = keep
        states = (
            (output_weight, momentum_output, variance_output)
            + (expand_weight, momentum_expand, variance_expand)
            + (shrink_weight, momentum_shrink, variance_shrink)
        )
        if part % 8 == 0:
            updated = update([item[0] for item in chains], [fetch(item) for item in chains], states, n_dev)
        else:
            for item in chains:
                merge(item, fetch(item))
            last_shrink, last_expand, sum_output = chains[2][0]
            sum_shrink = jnp.concatenate([*chains[0][0], last_shrink], axis=0)
            sum_expand = jnp.stack([*chains[1][0], last_expand], axis=1)
            sum_expand = sum_expand.reshape(part, spans, n_dev, part).transpose(0, 2, 1, 3).reshape(part, hidden)
            updated = []
            for number, gradient in enumerate((sum_output, sum_expand, sum_shrink)):
                weight, first, second = states[3 * number : 3 * number + 3]
                updated += adam_step(weight, gradient, first, second, RATE_MATRIX, WEIGHT_DECAY)
        if n_dp <= 8:
            items = chain[0].reshape(n_dp // 2, n_ctx, part, cols + vectors)
            spot = me_dp >> 1
            total = lax.dynamic_index_in_dim(items, spot, 0, keepdims=False)
            sent = [
                lax.dynamic_index_in_dim(items, lax.bitwise_xor(spot, j), 0, keepdims=False).astype(BF16)
                for j in range(1, n_dp // 2)
            ]
            gots = [swap(item, "dp", 2 * (j + 1)) for j, item in enumerate(sent)]
            total, gots, crossing, updated = lax.optimization_barrier((total, gots, crossing, updated))
            total = sum((item.astype(F32) for item in gots), total)
        else:
            while chain[3]:
                split(chain)
                merge(chain, fetch(chain))
            total = chain[0]
        shares.append(sum((value.astype(F32) for value in crossing), joined[0]))

        def terms_for(k):
            return lax.dynamic_index_in_dim(total, lax.bitwise_xor(me, k), 0, keepdims=False)

        sent = lax.optimization_barrier([terms_for(k).astype(BF16) for k in range(1, n_ctx)])
        arrived = [terms_for(0)] + [swap(item, "ctx", k + 1) for k, item in enumerate(sent)]
        new_joint, first_joint, second_joint, new_small, first_small, second_small = finish(
            me_arr,
            arrived,
            (joint_weight, momentum_joint, variance_joint, small_params, momentum_small, variance_small),
        )

        plain, scale = norm_parts(tokens_in.astype(F32))
        input_grad = grad_resid + norm_back(plain, scale, jnp.concatenate(shares, axis=0), params[0])

        new_output, first_output, second_output = updated[:3]
        new_expand, first_expand, second_expand = updated[3:6]
        new_shrink, first_shrink, second_shrink = updated[6:]
        return (
            block_output,
            input_grad,
            new_joint,
            new_output,
            new_expand,
            new_shrink,
            first_joint,
            first_output,
            first_expand,
            first_shrink,
            second_joint,
            second_output,
            second_expand,
            second_shrink,
            new_small,
            first_small,
            second_small,
        )

    return per_device


def solution(mesh):
    sizes = {axis: mesh.shape[axis] for axis in ("dp", "ctx")}
    tokens = P("dp", "ctx", None)
    matrix = P(("dp", "ctx"), None)
    table = P(None, ("dp", "ctx"))
    return jax.shard_map(
        build(sizes),
        mesh=mesh,
        in_specs=(tokens, P("dp", "ctx"), tokens) + (matrix,) * 12 + (table,) * 3,
        out_specs=(tokens, tokens) + (matrix,) * 12 + (table,) * 3,
        check_vma=False,
    )
```

```python
import functools

import jax
import jax.numpy as jnp
from jax import lax
from jax.experimental import pallas as pl
from jax.experimental.pallas import tpu as pltpu
from jax.sharding import PartitionSpec as P

HDIM = 64
STEP = 10

NORM_EPSILON = 1e-05
MASKED_SCORE = -1000000000.0
BETA_ONE = 0.9
BETA_TWO = 0.999
ADAM_EPSILON = 1e-08
RATE_MATRIX = 0.05
RATE_VECTOR = 0.3
WEIGHT_DECAY = 0.1
DOCS = 4
GELU_ROOT = 0.7978845608028654
GELU_CUBE = 0.044715
VMEM_BYTES = 56 * 1024 * 1024
COST = pl.CostEstimate(flops=20_000_000_000, bytes_accessed=1_000_000, transcendentals=0)

BF16 = jnp.bfloat16
F32 = jnp.float32


def norm_parts(values):
    centre = values - jnp.mean(values, axis=-1, keepdims=True)
    scale = lax.rsqrt(jnp.mean(centre * centre, axis=-1, keepdims=True) + NORM_EPSILON)
    return centre * scale, scale


def norm_back(plain, scale, grad, gain):
    grad_plain = grad * gain
    along = jnp.mean(grad_plain * plain, axis=-1, keepdims=True)
    return (grad_plain - jnp.mean(grad_plain, axis=-1, keepdims=True) - plain * along) * scale


def column_sum(values):
    return jnp.sum(values, axis=0, keepdims=True)


def adam_step(weight, gradient, first, second, rate, decay):
    first_new = BETA_ONE * first + (1.0 - BETA_ONE) * gradient
    second_new = BETA_TWO * second + (1.0 - BETA_TWO) * gradient * gradient
    first_hat = first_new / (1.0 - BETA_ONE**STEP)
    second_hat = second_new / (1.0 - BETA_TWO**STEP)
    updated = weight - rate * (first_hat / (jnp.sqrt(second_hat) + ADAM_EPSILON) + decay * weight)
    return (updated, first_new, second_new)


def dot(left, right, dims):
    return lax.dot_general(left, right, (dims, ((), ())), preferred_element_type=F32)


def project_kernel(n_blk, *refs):
    tokens, (params_ref, weight_ref, bias_ref, joint_ref, normed_ref) = refs[:n_blk], refs[n_blk:]
    for place in range(n_blk):
        plain, _ = norm_parts(tokens[place][0].astype(F32))
        normed = (plain * params_ref[0:1, :] + params_ref[1:2, :]).astype(BF16)
        normed_ref[place, 0] = normed
        joint = dot(normed, weight_ref[...], ((1,), (0,))) + bias_ref[...]
        joint_ref[place, 0] = joint.astype(BF16)


def project(tokens, params, weight, bias):
    n_blk = len(tokens)
    seqs, blk, width = tokens[0].shape
    cols = weight.shape[1]
    return pl.pallas_call(
        functools.partial(project_kernel, n_blk),
        grid=(seqs,),
        in_specs=[pl.BlockSpec((1, blk, width), lambda s: (s, 0, 0))] * n_blk
        + [
            pl.BlockSpec(params.shape, lambda s: (0, 0)),
            pl.BlockSpec(weight.shape, lambda s: (0, 0)),
            pl.BlockSpec(bias.shape, lambda s: (0, 0)),
        ],
        out_specs=[pl.BlockSpec((n_blk, 1, blk, size), lambda s: (0, s, 0, 0)) for size in (cols, width)],
        out_shape=[jax.ShapeDtypeStruct((n_blk, seqs, blk, size), BF16) for size in (cols, width)],
        compiler_params=pltpu.CompilerParams(vmem_limit_bytes=VMEM_BYTES),
        cost_estimate=COST,
        name="project",
    )(*tokens, params, weight, bias)


def fill_bias(bias, start_ref, n_blk, blk):
    offsets = []
    offset = 0
    for block in range(n_blk):
        keys = (block + 1) * blk
        key_pos = lax.broadcasted_iota(jnp.int32, (keys, blk), 0)
        query_pos = lax.broadcasted_iota(jnp.int32, (keys, blk), 1) + block * blk
        first = start_ref[0, :, block * blk : (block + 1) * blk]
        allowed = (key_pos >= first) & (key_pos <= query_pos)
        bias[offset : offset + keys, :] = jnp.where(allowed, 0.0, MASKED_SCORE)
        offsets.append(offset)
        offset += keys
    return offsets


def bias_rows(n_blk, blk):
    return n_blk * (n_blk + 1) // 2 * blk


def forward_kernel(n_blk, blk, heads, me_ref, joint_ref, start_ref, *refs):
    out_refs, (log_ref, joint, bias, out) = refs[:n_blk], refs[n_blk:]
    me = me_ref[0]
    group = heads * HDIM
    for block in range(n_blk):
        joint[block * blk : (block + 1) * blk, :] = joint_ref[lax.bitwise_xor(me, block), 0]
    offsets = fill_bias(bias, start_ref, n_blk, blk)
    tasks = [(block, head) for block in reversed(range(n_blk)) for head in range(heads)]

    def raw_scores(task):
        block, head = task
        low = head * HDIM
        query = joint[block * blk : (block + 1) * blk, low : low + HDIM] * 0.125
        return dot(joint[: (block + 1) * blk, group + low : group + low + HDIM], query, ((1,), (1,)))

    ahead = raw_scores(tasks[0])
    mixed = []
    for number, (block, head) in enumerate(tasks):
        scores = ahead
        if number + 1 < len(tasks):
            ahead = raw_scores(tasks[number + 1])
        keys = (block + 1) * blk
        low = head * HDIM
        scores = scores + bias[offsets[block] : offsets[block] + keys, :]
        top = jnp.max(scores, axis=0, keepdims=True)
        exponent = jnp.exp(scores - top)
        total = jnp.sum(exponent, axis=0, keepdims=True)
        value = joint[:keys, 2 * group + low : 2 * group + low + HDIM]
        mixed.append(dot(value, exponent.astype(BF16), ((0,), (0,))) * (1.0 / total))
        log_ref[0, head : head + 1, block * blk : (block + 1) * blk] = top + jnp.log(total)
        if head == heads - 1:
            out[lax.bitwise_xor(me, block)] = jnp.concatenate(mixed, axis=0).T.astype(BF16)
            mixed = []
    for place in range(n_blk):
        out_refs[place][0] = out[place]


def attend_forward(me, joint, start):
    n_blk, seqs, blk, cols = joint.shape
    group = cols // 3
    heads = group // HDIM
    length = n_blk * blk
    return pl.pallas_call(
        functools.partial(forward_kernel, n_blk, blk, heads),
        grid_spec=pltpu.PrefetchScalarGridSpec(
            num_scalar_prefetch=1,
            grid=(seqs,),
            in_specs=[
                pl.BlockSpec((n_blk, 1, blk, cols), lambda s, m: (0, s, 0, 0)),
                pl.BlockSpec((1, 1, length), lambda s, m: (s, 0, 0)),
            ],
            out_specs=[pl.BlockSpec((1, blk, group), lambda s, m: (s, 0, 0))] * n_blk
            + [pl.BlockSpec((1, heads, length), lambda s, m: (s, 0, 0))],
            scratch_shapes=[
                pltpu.VMEM((length, cols), BF16),
                pltpu.VMEM((bias_rows(n_blk, blk), blk), F32),
                pltpu.VMEM((n_blk, blk, group), BF16),
            ],
        ),
        out_shape=[jax.ShapeDtypeStruct((seqs, blk, group), BF16)] * n_blk
        + [jax.ShapeDtypeStruct((seqs, heads, length), F32)],
        compiler_params=pltpu.CompilerParams(vmem_limit_bytes=VMEM_BYTES),
        cost_estimate=COST,
        name="attend_forward",
    )(me, joint, start)


def layer_kernel(
    n_ctx,
    spans,
    me_ref,
    x_ref,
    y_ref,
    *refs,
):
    mixed_refs = refs[:n_ctx]
    mine_ref, other_ref, params_ref = refs[n_ctx : n_ctx + 3]
    result_ref, resid_ref, branch_ref, normed_ref, act_ref, pre_ref = refs[n_ctx + 3 : n_ctx + 9]
    mix_refs = refs[n_ctx + 9 : 2 * n_ctx + 9]
    sums_ref, rest_ref, sems = refs[2 * n_ctx + 9 :]
    me = me_ref[0]
    width = x_ref.shape[-1]
    group = width // n_ctx
    side = width // 2
    inner = spans // 2

    core = lax.bitwise_and(me, 1)
    cuts = (0, side, side + width * inner, side + 2 * width * inner)

    def arrivals(sections):
        return [
            pltpu.make_async_copy(
                source.at[:, cuts[section] : cuts[section + 1]],
                rest_ref.at[half, :, cuts[section] : cuts[section + 1]],
                sems.at[number, section],
            )
            for section in sections
            for number, (source, half) in enumerate(((mine_ref, core), (other_ref, 1 - core)))
        ]

    @pl.when(pl.program_id(0) == 0)
    def _():
        for copy in arrivals((0, 1, 2)):
            copy.start()
        for copy in arrivals((0,)):
            copy.wait()

    def output_rows(place, half):
        first = pl.multiple_of(lax.bitwise_xor(me, place) * group, group)
        return rest_ref[half, pl.ds(first, group), 0:side]

    def param(row):
        return params_ref[row : row + 1, :]

    upstream = y_ref[0]
    mixed = [ref[0] for ref in mixed_refs]
    sides = [
        sum(dot(mixed[place], output_rows(place, half), ((1,), (0,))) for place in range(n_ctx)) for half in range(2)
    ]
    residual = x_ref[0].astype(F32) + (jnp.concatenate(sides, axis=1) + param(4))
    plain, scale = norm_parts(residual)
    normed = (plain * param(5) + param(6)).astype(BF16)
    normed_ref[...] = normed.T
    result = residual + param(7 + spans)
    grad_normed = jnp.zeros(residual.shape, F32)

    @pl.when(pl.program_id(0) == 0)
    def _():
        for copy in arrivals((1, 2)):
            copy.wait()

    sums = []
    for span in range(spans):
        half, low = span // inner, side + width * (span % inner)
        expand = rest_ref[half, :, low : low + width]
        shrink = rest_ref[half, :, low + width * inner : low + width * (inner + 1)]
        pre = dot(normed, expand, ((1,), (0,))) + param(7 + span)
        square = pre * pre
        bent = jnp.tanh(GELU_ROOT * (pre + GELU_CUBE * (square * pre)))
        half = 0.5 * (1.0 + bent)
        activated = (pre * half).astype(BF16)
        slope = half + (0.5 * pre) * (1.0 - bent * bent) * (GELU_ROOT + (3.0 * GELU_ROOT * GELU_CUBE) * square)
        act_ref[width * span : width * (span + 1), :] = activated.T
        result = result + dot(activated, shrink, ((1,), (0,)))
        grad_pre = (dot(upstream, shrink, ((1,), (1,))) * slope).astype(BF16)
        pre_ref[0, :, width * span : width * (span + 1)] = grad_pre
        grad_normed = grad_normed + dot(grad_pre, expand, ((1,), (1,)))
        sums.append(column_sum(grad_pre.astype(F32)))
    result_ref[0] = result.astype(BF16)
    gain_sum = column_sum(grad_normed * plain)
    shift_sum = column_sum(grad_normed)
    upstream_wide = upstream.astype(F32)
    grad_resid = upstream_wide + norm_back(plain, scale, grad_normed, param(5))
    resid_ref[0] = grad_resid
    branch = grad_resid.astype(BF16)
    branch_ref[0] = branch
    for place in range(n_ctx):
        mix = dot(branch[:, :side], output_rows(place, 0), ((1,), (1,)))
        mix_refs[place][0] = (mix + dot(branch[:, side:], output_rows(place, 1), ((1,), (1,)))).astype(BF16)
    table = jnp.concatenate(
        [column_sum(branch.astype(F32)), gain_sum, shift_sum] + sums + [column_sum(upstream_wide)], axis=0
    )

    @pl.when(pl.program_id(0) == 0)
    def _():
        sums_ref[...] = table

    @pl.when(pl.program_id(0) > 0)
    def _():
        sums_ref[...] += table


def layer(me, tokens, cotangent, mixed, mine, other, params):
    n_ctx = len(mixed)
    seqs, blk, width = tokens.shape
    group = width // n_ctx
    spans = (2 * mine.shape[1] // width - 1) // 2
    hidden = spans * width

    def by_seq(*shape):
        return pl.BlockSpec((1,) + shape, lambda s, m: (s,) + (0,) * len(shape))

    def whole(shape):
        return pl.BlockSpec(shape, lambda s, m: (0,) * len(shape), pipeline_mode=pl.Buffered(1))

    return pl.pallas_call(
        functools.partial(layer_kernel, n_ctx, spans),
        grid_spec=pltpu.PrefetchScalarGridSpec(
            num_scalar_prefetch=1,
            grid=(seqs,),
            in_specs=[by_seq(blk, width)] * 2
            + [by_seq(blk, group)] * n_ctx
            + [pl.BlockSpec(memory_space=pl.ANY)] * 2
            + [whole(params.shape)],
            out_specs=[
                by_seq(blk, width),
                by_seq(blk, width),
                by_seq(blk, width),
                pl.BlockSpec((width, blk), lambda s, m: (0, s)),
                pl.BlockSpec((hidden, blk), lambda s, m: (0, s)),
                by_seq(blk, hidden),
            ]
            + [by_seq(blk, group)] * n_ctx
            + [pl.BlockSpec((4 + spans, width), lambda s, m: (0, 0))],
            scratch_shapes=[pltpu.VMEM((2,) + mine.shape, BF16), pltpu.SemaphoreType.DMA((2, 3))],
        ),
        out_shape=[
            jax.ShapeDtypeStruct((seqs, blk, width), BF16),
            jax.ShapeDtypeStruct((seqs, blk, width), F32),
            jax.ShapeDtypeStruct((seqs, blk, width), BF16),
            jax.ShapeDtypeStruct((width, seqs * blk), BF16),
            jax.ShapeDtypeStruct((hidden, seqs * blk), BF16),
            jax.ShapeDtypeStruct((seqs, blk, hidden), BF16),
        ]
        + [jax.ShapeDtypeStruct((seqs, blk, group), BF16)] * n_ctx
        + [jax.ShapeDtypeStruct((4 + spans, width), F32)],
        compiler_params=pltpu.CompilerParams(vmem_limit_bytes=VMEM_BYTES),
        cost_estimate=COST,
        name="layer",
    )(me, tokens, cotangent, *mixed, mine, other, params)


def backward_kernel(
    n_blk, blk, heads, me_ref, joint_ref, *refs
):
    grad_refs = refs[:n_blk]
    start_ref, log_ref, out_ref, joint, grads, bias, totals = refs[n_blk:]
    me = me_ref[0]
    group = heads * HDIM
    for place in range(n_blk):
        rows = pl.ds(pl.multiple_of(lax.bitwise_xor(me, place) * blk, blk), blk)
        joint[rows, :] = joint_ref[place, 0]
        grads[rows, :] = grad_refs[place][0]
    offsets = fill_bias(bias, start_ref, n_blk, blk)
    tasks = [(block, head) for block in reversed(range(n_blk)) for head in range(heads)]

    def products(task):
        block, head = task
        low = head * HDIM
        keys = (block + 1) * blk
        rows = slice(block * blk, keys)
        query = joint[rows, low : low + HDIM] * 0.125
        grad = grads[rows, low : low + HDIM]
        scores = dot(joint[:keys, group + low : group + low + HDIM], query, ((1,), (1,)))
        grad_probs = dot(joint[:keys, 2 * group + low : 2 * group + low + HDIM], grad, ((1,), (1,)))
        zeros = jnp.zeros((blk, HDIM), BF16)
        pair = jnp.concatenate(
            [jnp.concatenate([query, zeros], axis=1), jnp.concatenate([zeros, grad], axis=1)], axis=0
        )
        return scores, grad_probs, pair

    ahead = products(tasks[0])
    grad_queries = []
    for number, (block, head) in enumerate(tasks):
        scores, grad_probs, pair = ahead
        if number + 1 < len(tasks):
            ahead = products(tasks[number + 1])
        keys = (block + 1) * blk
        low = head * HDIM
        scores = scores + bias[offsets[block] : offsets[block] + keys, :]
        probs = jnp.exp(scores - log_ref[0, head : head + 1, block * blk : keys])
        inner = jnp.sum(probs * grad_probs, axis=0, keepdims=True)
        grad_scores = (probs * (grad_probs - inner)).astype(BF16)
        terms = dot(jnp.concatenate([grad_scores, probs.astype(BF16)], axis=1), pair, ((1,), (0,)))
        if block == n_blk - 1:
            totals[head, :keys, :] = terms
        else:
            totals[head, :keys, :] += terms
        key = joint[:keys, group + low : group + low + HDIM]
        grad_queries.append(dot(key, grad_scores, ((0,), (0,))) * 0.125)
        if head == heads - 1:
            out_ref[lax.bitwise_xor(me, block), 0, :, :group] = jnp.concatenate(grad_queries, axis=0).T.astype(BF16)
            grad_queries = []
    for block in range(n_blk):
        rows = slice(block * blk, (block + 1) * blk)
        place = lax.bitwise_xor(me, block)
        sides = [totals[head, rows, :].astype(BF16) for head in range(heads)]
        out_ref[place, 0, :, group:] = jnp.concatenate(
            [side[:, :HDIM] for side in sides] + [side[:, HDIM:] for side in sides], axis=1
        )


def attend_backward(me, joint, grads, start, logs, first):
    n_blk, count, blk, cols = joint.shape
    group = cols // 3
    heads = group // HDIM
    length = n_blk * blk
    return pl.pallas_call(
        functools.partial(backward_kernel, n_blk, blk, heads),
        grid_spec=pltpu.PrefetchScalarGridSpec(
            num_scalar_prefetch=1,
            grid=(count,),
            in_specs=[pl.BlockSpec((n_blk, 1, blk, cols), lambda s, m: (0, s, 0, 0))]
            + [pl.BlockSpec((1, blk, group), lambda s, m: (s + first, 0, 0))] * n_blk
            + [
                pl.BlockSpec((1, 1, length), lambda s, m: (s, 0, 0)),
                pl.BlockSpec((1, heads, length), lambda s, m: (s, 0, 0)),
            ],
            out_specs=pl.BlockSpec((n_blk, 1, blk, cols), lambda s, m: (0, s, 0, 0)),
            scratch_shapes=[
                pltpu.VMEM((length, cols), BF16),
                pltpu.VMEM((length, group), BF16),
                pltpu.VMEM((bias_rows(n_blk, blk), blk), F32),
                pltpu.VMEM((heads, length, 2 * HDIM), F32),
            ],
        ),
        out_shape=jax.ShapeDtypeStruct((n_blk, count, blk, cols), BF16),
        compiler_params=pltpu.CompilerParams(vmem_limit_bytes=VMEM_BYTES),
        cost_estimate=COST,
        name="attend_backward",
    )(me, joint, *grads, start, logs)


def collect_kernel(n_blk, first, last, me_ref, grad_ref, normed_ref, params_ref, weight_ref, table_ref, *refs):
    terms_ref, bias_ref = refs[-2:]
    blk, cols = grad_ref.shape[2:]
    group = cols // 3
    vectors, width = params_ref.shape
    grad = grad_ref[...].reshape(n_blk * blk, cols)
    weight_grad = dot(normed_ref[...].reshape(n_blk * blk, width), grad, ((0,), (0,)))
    bias_grad = column_sum(grad.astype(F32))

    @pl.when(pl.program_id(0) == 0)
    def _():
        terms_ref[:, :cols] = weight_grad if first else weight_grad + refs[0][:, :cols]
        bias_ref[...] = bias_grad if first else bias_grad + refs[1][...]

    @pl.when(pl.program_id(0) > 0)
    def _():
        terms_ref[:, :cols] += weight_grad
        bias_ref[...] += bias_grad

    @pl.when(pl.program_id(0) == pl.num_programs(0) - 1)
    def _():
        if not last:
            terms_ref[:, cols:] = jnp.zeros((width, vectors), F32)
            return
        weight = weight_ref[...].astype(F32)
        bias = bias_ref[...]
        columns = params_ref[...].T
        shift_sum = jnp.sum(weight * bias, axis=1, keepdims=True)
        gain_sum = jnp.sum(weight * terms_ref[:, :cols], axis=1, keepdims=True)
        gain_sum = (gain_sum - columns[:, 1:2] * shift_sum) / columns[:, 0:1]

        def placed(values):
            return jnp.concatenate([jnp.where(me_ref[0] == j, values, 0.0) for j in range(n_blk)], axis=1)

        table = jnp.concatenate([placed(bias[:, :group]), placed(bias[:, 2 * group :]), table_ref[...]], axis=0).T
        terms_ref[:, cols:] = jnp.concatenate([gain_sum, shift_sum, table], axis=1)


def collect(me, grad, normed, params, weight, table, earlier, last):
    n_blk, count, blk, cols = grad.shape
    vectors, width = params.shape

    def whole(shape):
        return pl.BlockSpec(shape, lambda s, m: (0, 0))

    def by_seq(size):
        return pl.BlockSpec((n_blk, 1, blk, size), lambda s, m: (0, s, 0, 0))

    shapes = [(width, cols + vectors), (1, cols)]
    return pl.pallas_call(
        functools.partial(collect_kernel, n_blk, not earlier, last),
        grid_spec=pltpu.PrefetchScalarGridSpec(
            num_scalar_prefetch=1,
            grid=(count,),
            in_specs=[by_seq(cols), by_seq(width)]
            + [whole(item.shape) for item in (params, weight, table, *earlier)],
            out_specs=[whole(shape) for shape in shapes],
        ),
        out_shape=[jax.ShapeDtypeStruct(shape, F32) for shape in shapes],
        compiler_params=pltpu.CompilerParams(vmem_limit_bytes=VMEM_BYTES),
        cost_estimate=COST,
        name="collect",
    )(me, grad, normed, params, weight, table, *earlier)


def unproject_kernel(grad_ref, weight_ref, kept_ref, sent_ref):
    share = dot(grad_ref[0, 0], weight_ref[...], ((1,), (1,))).astype(BF16)
    odd = pl.program_id(1) % 2

    @pl.when(odd == 0)
    def _():
        kept_ref[0, 0] = share

    @pl.when(odd == 1)
    def _():
        sent_ref[0, 0] = share


def unproject(grad, weight):
    n_blk, count, blk, cols = grad.shape
    width = weight.shape[0]
    out = pl.BlockSpec((1, 1, blk, width), lambda s, k: (k // 2, s, 0, 0))
    return pl.pallas_call(
        unproject_kernel,
        grid=(count, n_blk),
        in_specs=[
            pl.BlockSpec((1, 1, blk, cols), lambda s, k: (k, s, 0, 0)),
            pl.BlockSpec(weight.shape, lambda s, k: (0, 0)),
        ],
        out_specs=[out, out],
        out_shape=[jax.ShapeDtypeStruct((n_blk // 2, count, blk, width), BF16)] * 2,
        compiler_params=pltpu.CompilerParams(vmem_limit_bytes=VMEM_BYTES),
        cost_estimate=COST,
        name="unproject",
    )(grad, weight)


def weigh_kernel(n_ctx, last, me_ref, act_ref, pre_ref, normed_ref, up_ref, branch_ref, *refs):
    mixed_refs, outs, total = refs[:n_ctx], refs[n_ctx : n_ctx + 6], refs[-1]
    step = pl.program_id(0)
    me = me_ref[0]
    core = lax.bitwise_and(me, 1)
    per_group = total.shape[0] // n_ctx

    @pl.when((step < last) | (step == 2 * last))
    def _():
        total[...] = dot(act_ref[...], up_ref[...], ((1,), (0,))).reshape(total.shape)

    @pl.when(((step >= last) & (step < 2 * last)) | (step == 2 * last + 1))
    def _():
        total[...] = dot(normed_ref[...], pre_ref[...], ((1,), (0,))).reshape(total.shape)

    @pl.when(step == 2 * last + 2)
    def _():
        for place in range(n_ctx):
            value = dot(mixed_refs[place][...], branch_ref[...], ((0,), (0,)))
            total[pl.ds(lax.bitwise_xor(me, place) * per_group, per_group)] = value.reshape(
                (per_group,) + total.shape[1:]
            )

    bounds = (0, last, 2 * last, 2 * last + 3)
    for number in range(3):
        keep_ref, send_ref = outs[2 * number : 2 * number + 2]

        @pl.when((step >= bounds[number]) & (step < bounds[number + 1]))
        def _():
            keep_ref[0] = total[:, core].astype(BF16)
            send_ref[0] = total[:, 1 - core].astype(BF16)


def weigh(me, activated, grad_pre, normed, upstream, branch, mixed, part):
    hidden, rows = activated.shape
    width = normed.shape[0]
    n_ctx = len(mixed)
    last = hidden // width - 1
    pairs = width // (2 * part)

    def whole(shape):
        return pl.BlockSpec(shape, lambda s, m: (0, 0), pipeline_mode=pl.Buffered(1))

    def units(count, begin):
        return pl.BlockSpec(
            (1, pairs, part, width), lambda s, m: (jnp.clip(s - begin, 0, count - 1), 0, 0, 0)
        )

    counts = ((last, 0), (last, last), (3, 2 * last))
    return pl.pallas_call(
        functools.partial(weigh_kernel, n_ctx, last),
        grid_spec=pltpu.PrefetchScalarGridSpec(
            num_scalar_prefetch=1,
            grid=(2 * last + 3,),
            in_specs=[
                pl.BlockSpec((width, rows), lambda s, m: (jnp.where(s < 2 * last, jnp.minimum(s, last - 1), last), 0)),
                pl.BlockSpec((rows, width), lambda s, m: (0, jnp.clip(s - last, 0, last))),
                whole(normed.shape),
                whole(upstream.shape),
                whole(branch.shape),
            ]
            + [whole(item.shape) for item in mixed],
            out_specs=[units(*item) for item in counts for _ in range(2)],
            scratch_shapes=[pltpu.VMEM((pairs, 2, part, width), F32)],
        ),
        out_shape=[
            jax.ShapeDtypeStruct((count, pairs, part, width), dtype) for count, _ in counts for dtype in (BF16, BF16)
        ],
        compiler_params=pltpu.CompilerParams(vmem_limit_bytes=VMEM_BYTES),
        cost_estimate=COST,
        name="weigh",
    )(me, activated, grad_pre, normed, upstream, branch, *mixed)


def update_kernel(n_dev, *refs):
    sums = [refs[c][...] + refs[3 + c][...].astype(F32) for c in range(3)]
    states, outs = refs[6:15], refs[15:]
    spans = sums[0].shape[0] + 1
    part = sums[0].shape[1]
    shrink = jnp.concatenate([sums[0][i] for i in range(spans - 1)] + [sums[2][0]], axis=0)
    units = [sums[1][i] for i in range(spans - 1)] + [sums[2][1]]
    expand = jnp.concatenate(
        [units[span][:, place * part : (place + 1) * part] for place in range(n_dev) for span in range(spans)], axis=1
    )
    for number, gradient in enumerate((sums[2][2], expand, shrink)):
        weight, first, second = [ref[...] for ref in states[3 * number : 3 * number + 3]]
        results = adam_step(weight, gradient, first, second, RATE_MATRIX, WEIGHT_DECAY)
        for out, result in zip(outs[3 * number : 3 * number + 3], results):
            out[...] = result


def update(keeps, gots, states, n_dev):
    vmem = pl.BlockSpec(memory_space=pltpu.VMEM)
    return pl.pallas_call(
        functools.partial(update_kernel, n_dev),
        in_specs=[vmem] * 15,
        out_specs=[vmem] * 9,
        out_shape=[jax.ShapeDtypeStruct(item.shape, F32) for item in states],
        compiler_params=pltpu.CompilerParams(vmem_limit_bytes=VMEM_BYTES),
        name="update",
    )(*keeps, *gots, *states)


def finish_kernel(n_ctx, me_ref, *refs):
    pieces, refs = refs[:n_ctx], refs[n_ctx:]
    states, outs, held = refs[:6], refs[6:12], refs[12]
    for place in range(n_ctx):
        held[place] = pieces[place][...].astype(F32)
    vectors = states[3].shape[0]
    cols = held.shape[-1] - vectors
    group = cols // 3
    groups = [held[lax.bitwise_xor(me_ref[0], j)] for j in range(n_ctx)]
    gradient = jnp.concatenate(
        [item[:, third * group : (third + 1) * group] for third in range(3) for item in groups], axis=1
    )
    small = sum(item[:, cols:] for item in groups).T
    results = adam_step(states[0][...], gradient, states[1][...], states[2][...], RATE_MATRIX, WEIGHT_DECAY)
    results += adam_step(states[3][...], small, states[4][...], states[5][...], RATE_VECTOR, 0.0)
    for out, result in zip(outs, results):
        out[...] = result


def finish(me, pieces, states):
    n_ctx = len(pieces)
    return pl.pallas_call(
        functools.partial(finish_kernel, n_ctx),
        in_specs=[pl.BlockSpec(memory_space=pltpu.SMEM)] + [pl.BlockSpec(memory_space=pltpu.VMEM)] * (n_ctx + 6),
        out_specs=[pl.BlockSpec(memory_space=pltpu.VMEM)] * 6,
        out_shape=[jax.ShapeDtypeStruct(item.shape, F32) for item in states],
        scratch_shapes=[pltpu.VMEM((n_ctx,) + pieces[0].shape, F32)],
        compiler_params=pltpu.CompilerParams(vmem_limit_bytes=VMEM_BYTES),
        name="finish",
    )(me, *pieces, *states)


def build(sizes):
    n_dp, n_ctx = sizes["dp"], sizes["ctx"]
    dp_bits = [bit for bit in range(16) if (1 << bit) < n_dp]
    ctx_bits = [bit for bit in range(16) if (1 << bit) < n_ctx]

    def swap(value, axis, mask):
        return lax.ppermute(value, axis, [(place, place ^ mask) for place in range(sizes[axis])])

    def reorder(items, me):
        stacked = jnp.stack(items)
        return [
            lax.dynamic_index_in_dim(stacked, lax.bitwise_xor(me, j), 0, keepdims=False) for j in range(len(items))
        ]

    def per_device(
        tokens_in,
        segments,
        cotangent,
        joint_weight,
        output_weight,
        expand_weight,
        shrink_weight,
        momentum_joint,
        momentum_output,
        momentum_expand,
        momentum_shrink,
        variance_joint,
        variance_output,
        variance_expand,
        variance_shrink,
        small_params,
        momentum_small,
        variance_small,
    ):
        seqs, stretch, width = tokens_in.shape
        hidden = expand_weight.shape[1]
        spans = hidden // width
        part = joint_weight.shape[0]
        group = width // n_ctx
        cols = 3 * group
        rows = seqs * stretch
        n_dev = n_dp * n_ctx
        n_bits = len(dp_bits)
        vectors = small_params.shape[0]
        me_dp, me = lax.axis_index("dp"), lax.axis_index("ctx")
        spots = {"dp": me_dp, "ctx": me}
        me_arr = me.astype(jnp.int32).reshape(1)

        joint_cast, small_cast = lax.optimization_barrier((joint_weight.astype(BF16), small_params.astype(BF16)))
        output_cast, expand_cast, shrink_cast = lax.optimization_barrier(
            (output_weight.astype(BF16), expand_weight.astype(BF16), shrink_weight.astype(BF16))
        )

        seg_blocks = {0: segments}
        for bit in reversed(ctx_bits):
            seg_blocks.update({k ^ (1 << bit): swap(value, "ctx", 1 << bit) for k, value in list(seg_blocks.items())})
        segs = jnp.concatenate(reorder([seg_blocks[k] for k in range(n_ctx)], me), axis=1)
        start = jnp.zeros_like(segs)
        for number in range(1, DOCS):
            bound = jnp.sum((segs < number).astype(jnp.int32), axis=1, keepdims=True)
            start = jnp.where(segs >= number, bound, start)
        start = start[:, None, :]

        small_cols = small_cast.T
        joint_cols = joint_cast.reshape(part, 3, n_ctx, group)

        def columns_for(k):
            picked = lax.dynamic_index_in_dim(joint_cols, lax.bitwise_xor(me, k), 2, keepdims=False)
            return jnp.concatenate([picked.reshape(part, cols), small_cols], axis=1)

        pieces = [columns_for(0)] + [swap(columns_for(k), "ctx", k) for k in range(1, n_ctx)]

        expand_wide = expand_cast.reshape(part, n_dev, spans, part).transpose(0, 2, 1, 3).reshape(part, hidden)
        shrink_wide = shrink_cast.reshape(spans, part, width).transpose(1, 0, 2).reshape(part, hidden)
        sides = [
            jnp.concatenate([item[:, h * size // 2 : (h + 1) * size // 2] for item, size in wide], axis=1)
            for wide in [((output_cast, width), (expand_wide, hidden), (shrink_wide, hidden))]
            for h in range(2)
        ]
        pair = me & 1
        rest_own = jnp.where(pair == 1, sides[1], sides[0])
        rest_got = swap(jnp.where(pair == 1, sides[0], sides[1]), "ctx", 1)
        rest = jnp.where(
            pair == 1,
            jnp.concatenate([rest_got, rest_own], axis=0),
            jnp.concatenate([rest_own, rest_got], axis=0),
        )
        rest = lax.all_gather(rest, ("dp", "ctx"), axis=0, tiled=True, axis_index_groups=[
            [d * n_ctx + c * 2 + p for d in range(n_dp) for c in range(n_ctx // 2)] for p in range(2)
        ])

        half = max(seqs // 2, 1)
        firsts = list(range(0, seqs, half))
        near, far_bits = 1, [bit for bit in reversed(ctx_bits) if bit]

        def fetch_far(blocks):
            for bit in far_bits:
                blocks.update({k ^ (1 << bit): swap(value, "ctx", 1 << bit) for k, value in list(blocks.items())})

        names = range(0, n_ctx, 2)
        ahead = {0: tokens_in[:1]}
        fetch_far(ahead)
        pieces, start, later, held = lax.optimization_barrier(
            (pieces, start, [tokens_in[1:half], tokens_in[half:]], [ahead[k] for k in names])
        )
        others = [{0: later[0]}, {0: later[1]}]
        for blocks in others:
            if blocks[0].shape[0]:
                fetch_far(blocks)
        first_half = {k: item for k, item in zip(names, held)}
        if half > 1:
            first_half = {k: jnp.concatenate([first_half[k], others[0][k]], axis=0) for k in names}
        tokens = [first_half, others[1]]
        for blocks, first in zip(tokens, firsts):
            blocks[0] = tokens_in[first : first + half]
        gathered = jnp.stack(reorder(pieces, me))
        for step, bit in enumerate(reversed(dp_bits)):
            other = swap(gathered, "dp", 1 << bit)
            upper = ((me_dp >> bit) & 1) == 1
            gathered = jnp.where(upper, jnp.stack([other, gathered]), jnp.stack([gathered, other]))
            if step == max(n_bits - 2, 0):
                flat = [(number, k) for number, blocks in enumerate(tokens) for k in sorted(blocks) if k]
                gathered, *held = lax.optimization_barrier((gathered,) + tuple(tokens[n][k] for n, k in flat))
                for (number, k), value in zip(flat, held):
                    tokens[number][k] = value
        for blocks in tokens:
            blocks.update({k ^ near: swap(value, "ctx", near) for k, value in list(blocks.items())})
        tokens = [[blocks[k] for k in range(n_ctx)] for blocks in tokens]

        gathered = gathered.transpose(tuple(reversed(range(n_bits))) + tuple(range(n_bits, n_bits + 3)))
        gathered = gathered.reshape(width, cols + vectors)
        joint_lo = gathered[:, :cols]
        params = gathered[:, cols:].T.astype(F32)
        mine_bias = lax.dynamic_slice(params[2:4], (0, me * group), (2, group))
        joint_bias = jnp.concatenate([mine_bias[:1], jnp.zeros((1, group), F32), mine_bias[1:]], axis=1)
        bias_hidden = params[7 : 7 + spans].reshape(n_dev, spans, part).transpose(1, 0, 2).reshape(spans, width)
        params = jnp.concatenate([params[:7], bias_hidden, params[7 + spans :]], axis=0)

        joints, normeds, logs, mixed, waiting = [], [], [], [], None
        starts = [start[first : first + half] for first in firsts]
        for number in range(len(firsts)):
            joint, normed = project(tokens[number], params, joint_lo, joint_bias)
            normeds.append(normed)
            if waiting is not None:
                waiting, joint = lax.optimization_barrier((waiting, joint))
                waiting = [waiting[0]] + [swap(waiting[k], "ctx", k) for k in range(1, n_ctx)]
            *attended, log = attend_forward(me_arr, joint, starts[number])
            if waiting is not None:
                waiting, attended = lax.optimization_barrier((waiting, attended))
                mixed.append(waiting)
            waiting = attended
            joints.append(joint)
            logs.append(log)
        waiting, rest = lax.optimization_barrier((waiting, rest))
        rest_other = swap(rest, "ctx", 1)
        mixed.append([waiting[0]] + [swap(waiting[k], "ctx", k) for k in range(1, n_ctx)])
        mixed = [jnp.concatenate(items, axis=0) for items in zip(*mixed)]
        block_output, grad_resid, branch, normed_two, activated, grad_pre, *grad_mixed, sums = layer(
            me_arr, tokens_in, cotangent, mixed, rest, rest_other, params
        )
        grads = [grad_mixed[0]] + [swap(grad_mixed[k], "ctx", k) for k in range(1, n_ctx)]

        activated, grad_pre, normed_two, branch, grads[1] = lax.optimization_barrier(
            (activated, grad_pre, normed_two, branch, grads[1])
        )
        branch = branch.reshape(rows, width)
        upstream = cotangent.reshape(rows, width)
        grad_pre = grad_pre.reshape(rows, hidden)
        labels = [("dp", bit) for bit in reversed(dp_bits)] + [("ctx", bit) for bit in reversed(ctx_bits)]
        bit_dims = (2,) * len(labels)
        core, far = [("ctx", ctx_bits[0])], [("ctx", bit) for bit in ctx_bits[1:]]
        low, high = [("dp", dp_bits[0])], [("dp", bit) for bit in dp_bits[1:]]
        mixed = [item.reshape(rows, group) for item in mixed]
        orders = [core + low + high + far, core + far + low + high, core + high[:1] + far + low + high[1:]]
        if part % 8 == 0:
            halves = weigh(me_arr, activated, grad_pre, normed_two, upstream, branch, mixed, part)
            halves, grads = lax.optimization_barrier((halves, grads))
            names = ["unit"] + [label for label in labels if label not in core]
            halves = [item.reshape(item.shape[:1] + bit_dims[1:] + (part, width)) for item in halves]
            chains = [[halves[2 * c], halves[2 * c + 1], names, orders[c]] for c in range(3)]
        else:
            grad_shrink = dot(activated, upstream, ((1,), (0,))).reshape(spans, width, width)
            grad_expand = dot(normed_two, grad_pre, ((1,), (0,))).reshape(width, spans, width).transpose(1, 0, 2)
            grad_output = jnp.concatenate(reorder([dot(item, branch, ((0,), (0,))) for item in mixed], me), axis=0)
            units = [
                grad_shrink[:-1],
                grad_expand[:-1],
                jnp.stack([grad_shrink[-1], grad_expand[-1], grad_output]),
            ]
            chains = [
                [item.reshape(item.shape[:1] + bit_dims + (part, width)), None, ["unit"] + labels, order]
                for item, order in zip(units, orders)
            ]

        def split(chain):
            value, _, names, order = chain
            axis, bit = order[0]
            pos = names.index((axis, bit))
            mine = (spots[axis] >> bit) & 1
            chain[0] = lax.dynamic_index_in_dim(value, mine, pos, keepdims=False)
            chain[1] = lax.dynamic_index_in_dim(value, 1 - mine, pos, keepdims=False).astype(BF16)

        def fetch(chain):
            axis, bit = chain[3][0]
            return swap(chain[1], axis, 1 << bit)

        def merge(chain, got):
            _, _, names, order = chain
            chain[0] = chain[0].astype(F32) + got.astype(F32)
            chain[2] = [name for name in names if name != order[0]]
            chain[3] = order[1:]

        def advance(after, before):
            if len(chains[0][3]) < 2:
                return after, before
            after, keeps, gots = lax.optimization_barrier(
                (after, [chain[0] for chain in chains], [fetch(chain) for chain in chains])
            )
            for chain, keep, got in zip(chains, keeps, gots):
                chain[0] = keep
                merge(chain, got)
                split(chain)
            before, keeps, sends = lax.optimization_barrier(
                (before, [chain[0] for chain in chains], [chain[1] for chain in chains])
            )
            for chain, keep, send in zip(chains, keeps, sends):
                chain[0], chain[1] = keep, send
            return after, before

        if part % 8:
            for chain in chains:
                split(chain)

        sums_hidden = sums[3 : 3 + spans].reshape(spans, n_dev, part).transpose(1, 0, 2).reshape(spans, width)
        table = jnp.concatenate([sums[:3], sums_hidden, sums[3 + spans :]], axis=0)
        pending, shares = None, []
        earlier, after = (), branch
        for number, first in enumerate(firsts):
            _, (source, pending) = advance(after, (joints[number], pending))
            grad_joint = attend_backward(me_arr, source, grads, starts[number], logs[number], first)
            if pending:
                pending[1] = [swap(value, "ctx", 1 << bit) for value, bit in zip(pending[1], ctx_bits[1:])]
            (grad_joint, pending), _ = advance((grad_joint, pending), start)
            if pending:
                shares.append(sum((value.astype(F32) for value in pending[1]), pending[0]))
            earlier = collect(
                me_arr, grad_joint, normeds[number], params, joint_lo, table, earlier, number == len(firsts) - 1
            )
            if number == len(firsts) - 1:
                grad_joint, earlier = lax.optimization_barrier((grad_joint, earlier))
            kept, sent = unproject(grad_joint, joint_lo)
            after = (earlier, kept)
            if number < len(firsts) - 1:
                joined = kept.astype(F32) + swap(sent, "ctx", 1).astype(F32)
                pending = [joined[0], [joined[1 << (bit - 1)].astype(BF16) for bit in ctx_bits[1:]]]

        terms = earlier[0].reshape((2,) * n_bits + (n_ctx, part, cols + vectors))
        chain = [terms, None, [("dp", bit) for bit in reversed(dp_bits)], low + high]
        split(chain)
        got, sent, kept = lax.optimization_barrier((fetch(chain), swap(sent, "ctx", 1), kept))
        merge(chain, got)
        joined = kept.astype(F32) + sent.astype(F32)
        crossing = [swap(joined[1 << (bit - 1)].astype(BF16), "ctx", 1 << bit) for bit in ctx_bits[1:]]
        while len(chains[0][3]) > 1:
            for item in chains:
                merge(item, fetch(item))
                split(item)
        chain[0], keeps = lax.optimization_barrier((chain[0], [item[0] for item in chains]))
        for item, keep in zip(chains, keeps):
            item[0] = keep
        states = (
            (output_weight, momentum_output, variance_output)
            + (expand_weight, momentum_expand, variance_expand)
            + (shrink_weight, momentum_shrink, variance_shrink)
        )
        if part % 8 == 0:
            updated = update([item[0] for item in chains], [fetch(item) for item in chains], states, n_dev)
        else:
            for item in chains:
                merge(item, fetch(item))
            last_shrink, last_expand, sum_output = chains[2][0]
            sum_shrink = jnp.concatenate([*chains[0][0], last_shrink], axis=0)
            sum_expand = jnp.stack([*chains[1][0], last_expand], axis=1)
            sum_expand = sum_expand.reshape(part, spans, n_dev, part).transpose(0, 2, 1, 3).reshape(part, hidden)
            updated = []
            for number, gradient in enumerate((sum_output, sum_expand, sum_shrink)):
                weight, first, second = states[3 * number : 3 * number + 3]
                updated += adam_step(weight, gradient, first, second, RATE_MATRIX, WEIGHT_DECAY)
        if n_dp <= 8:
            items = chain[0].reshape(n_dp // 2, n_ctx, part, cols + vectors)
            spot = me_dp >> 1
            total = lax.dynamic_index_in_dim(items, spot, 0, keepdims=False)
            sent = [
                lax.dynamic_index_in_dim(items, lax.bitwise_xor(spot, j), 0, keepdims=False).astype(BF16)
                for j in range(1, n_dp // 2)
            ]
            gots = [swap(item, "dp", 2 * (j + 1)) for j, item in enumerate(sent)]
            total, gots, crossing, updated = lax.optimization_barrier((total, gots, crossing, updated))
            total = sum((item.astype(F32) for item in gots), total)
        else:
            while chain[3]:
                split(chain)
                merge(chain, fetch(chain))
            total = chain[0]
        shares.append(sum((value.astype(F32) for value in crossing), joined[0]))

        def terms_for(k):
            return lax.dynamic_index_in_dim(total, lax.bitwise_xor(me, k), 0, keepdims=False)

        sent = lax.optimization_barrier([terms_for(k).astype(BF16) for k in range(1, n_ctx)])
        arrived = [terms_for(0)] + [swap(item, "ctx", k + 1) for k, item in enumerate(sent)]
        new_joint, first_joint, second_joint, new_small, first_small, second_small = finish(
            me_arr,
            arrived,
            (joint_weight, momentum_joint, variance_joint, small_params, momentum_small, variance_small),
        )

        plain, scale = norm_parts(tokens_in.astype(F32))
        input_grad = grad_resid + norm_back(plain, scale, jnp.concatenate(shares, axis=0), params[0])

        new_output, first_output, second_output = updated[:3]
        new_expand, first_expand, second_expand = updated[3:6]
        new_shrink, first_shrink, second_shrink = updated[6:]
        return (
            block_output,
            input_grad,
            new_joint,
            new_output,
            new_expand,
            new_shrink,
            first_joint,
            first_output,
            first_expand,
            first_shrink,
            second_joint,
            second_output,
            second_expand,
            second_shrink,
            new_small,
            first_small,
            second_small,
        )

    return per_device


def solution(mesh):
    sizes = {axis: mesh.shape[axis] for axis in ("dp", "ctx")}
    tokens = P("dp", "ctx", None)
    matrix = P(("dp", "ctx"), None)
    table = P(None, ("dp", "ctx"))
    return jax.shard_map(
        build(sizes),
        mesh=mesh,
        in_specs=(tokens, P("dp", "ctx"), tokens) + (matrix,) * 12 + (table,) * 3,
        out_specs=(tokens, tokens) + (matrix,) * 12 + (table,) * 3,
        check_vma=False,
    )
```
